32 devices in a mesh: section: 2 (over x), dp: 16 (over z, y, core).
Axes of the slice: x: 2, y: 2, z: 4, core: 2. Of those that a mesh axis runs over, the one named last changes fastest.
Arguments:
- embedded: bfloat16 [2, 32, 512, 768], P('section', 'dp'), may hold values from -6 to 6
- lengths: int32 [32], P('dp'), may hold values from 256 to 512, as said below
- positions: int32 [2, 32, 64], P('section', 'dp'), may hold values from 1 to 511, as said below
- labels: int32 [2, 32, 64], P('section', 'dp'), may hold values from 0 to 30719
- joint_weight: bfloat16 [2, 768, 2304], P('section'), may hold values from -0.21875 to 0.21875
- mixer_weight: bfloat16 [2, 768, 768], P('section'), may hold values from -0.875 to 0.875
- expand_weight: bfloat16 [2, 768, 3072], P('section'), may hold values from -0.21875 to 0.21875
- contract_weight: bfloat16 [2, 3072, 768], P('section'), may hold values from -0.109375 to 0.109375
- head_weight: bfloat16 [2, 768, 768], P('section'), may hold values from -0.21875 to 0.21875
- gains: float32 [2, 3, 768], P('section'), may hold values from 0.5 to 1.5
- biases: float32 [2, 8, 768], P('section'), may hold values from -2 to 2
- expand_bias: float32 [2, 3072], P('section'), may hold values from -2 to 2
- word_table: bfloat16 [30720, 768], P('dp'), may hold values from -0.4375 to 0.4375
- word_bias: bfloat16 [30720], P('dp'), may hold values from -3 to 3
Outputs:
- loss: float32 [2], P('section')
- logits: bfloat16 [2, 32, 64, 30720], P('section', 'dp')
- input_grads: float32 [2, 32, 512, 768], P('section', 'dp')
- joint_grad: float32 [2, 768, 2304], P('section', 'dp')
- mixer_grad: float32 [2, 768, 768], P('section', 'dp')
- expand_grad: float32 [2, 768, 3072], P('section', 'dp')
- contract_grad: float32 [2, 3072, 768], P('section', 'dp')
- head_grads: float32 [2, 768, 768], P('section', 'dp')
- gain_grads: float32 [2, 3, 768], P('section')
- bias_grads: float32 [2, 8, 768], P('section')
- expand_bias_grad: float32 [2, 3072], P('section')
- table_grads: float32 [30720, 768], P('dp')
- word_bias_grad: float32 [30720], P('dp')
The draws below stay inside these ranges and needn't reach their ends.
Inputs may be any that keep to these rules, and one draw needn't show every extreme that they name: `lengths`: every passage is at least 256 long, and some passage is exactly 512. `positions`: distinct within each passage and section, each at least 1 and below that passage's length.
All inputs are finite; a program needn't handle non-finite values.
Results may differ from the reference program's by a relative error of at most 0.018.
Values may be sent and summed in bfloat16 or wider, within the bound.
No kernel may reach another device: no remote copies, remote signals or barrier semaphores. Data moves between devices by JAX's collectives and lax.ppermute only.
A program may use at most 512 MiB of HBM per device.

```python
import jax
import jax.numpy as jnp
from jax import lax

D = 768
HEADS = 12
HEAD_DIM = 64
FF = 3072
VOCAB = 30720
LEN = 512
MASK = 64
PASSAGES = 32


def passage_plan(key):
    sizes_key = jax.random.fold_in(key, 101)
    longest_key = jax.random.fold_in(key, 102)
    sizes = jax.random.randint(sizes_key, (PASSAGES,), LEN // 2, LEN + 1)
    longest = jax.random.randint(longest_key, (), 0, PASSAGES)
    return (sizes.at[longest].set(LEN).astype(jnp.int32), longest)


def draw_lengths(key, part):
    sizes, longest = passage_plan(key)
    return sizes


def draw_positions(key, part):
    sizes, longest = passage_plan(key)
    key = jax.random.fold_in(key, 7)
    place = jnp.arange(LEN, dtype=jnp.int32)
    scores = jax.random.randint(key, (2, PASSAGES, LEN), 0, 2 ** 20) * LEN + place[None, None, :]
    barred = (place[None, None, :] == 0) | (place[None, None, :] >= sizes[None, :, None])
    scores = jnp.where(barred, 2 ** 30, scores)
    chosen = (jnp.arange(PASSAGES)[None, :, None] == longest) & ((place == 1) | (place == LEN - 1))[None, None, :]
    scores = jnp.where(chosen, -1, scores)
    order = jnp.argsort(scores, axis=-1, stable=True)
    return order[:, :, :MASK].astype(jnp.int32)


def draw_embedded(key, part):
    key = jax.random.fold_in(key, 11)
    word_key = jax.random.fold_in(key, 1)
    table_key = jax.random.fold_in(key, 2)
    jitter_key = jax.random.fold_in(key, 3)
    word_ids = jax.random.randint(word_key, (2, PASSAGES, LEN), 0, 32)
    prototypes = jax.random.normal(table_key, (32, D), jnp.float32)
    jitter = jax.random.normal(jitter_key, (2, PASSAGES, LEN, D), jnp.float32)
    blended = 0.9 * prototypes[word_ids] + 0.44 * jitter
    return jnp.clip(blended, -6.0, 6.0).astype(jnp.bfloat16)


def place_ends(entries, key, least, top_value):
    longest = entries.shape.index(max(entries.shape))
    spots = []
    for shift in (0, 1):
        where = [jax.random.randint(jax.random.fold_in(key, axis), (), 0, length) for axis, length in enumerate(entries.shape)]
        where[longest] = (where[longest] + shift) % entries.shape[longest]
        spots.append(tuple(where))
    return entries.at[spots[0]].set(least).at[spots[1]].set(top_value)


def level_of(own_key, dims, split, low, largest):
    level = 1.0
    for dim, parts in split:
        draws = jax.random.uniform(jax.random.fold_in(jax.random.fold_in(own_key, 6), dim), (parts,), jnp.float32, low / len(split), largest / len(split))
        level = level * jnp.repeat(jnp.exp(draws), dims[dim] // parts).reshape((-1,) + (1,) * (len(dims) - 1 - dim))
    return level


def bell_draw(key, dims, scale, reach, pieces=(), kind=jnp.bfloat16):
    values = scale * jax.random.normal(key, dims, jnp.float32)
    if pieces:
        values = values * level_of(key, dims, pieces, -0.22, 0.18)
    return jnp.clip(values, -reach, reach).astype(kind)


def setup_inputs(seed: int = 0) -> dict:
    key_list = jax.random.split(jax.random.key(seed), 15)
    embedded = draw_embedded(jax.random.fold_in(key_list[14], 71), 0)
    lengths = draw_lengths(jax.random.fold_in(key_list[14], 71), 0)
    positions = draw_positions(jax.random.fold_in(key_list[14], 71), 0)
    labels = place_ends(jax.random.randint(key_list[3], (2, PASSAGES, MASK), 0, VOCAB), jax.random.fold_in(key_list[3], 1), 0, VOCAB - 1).astype(jnp.int32)
    joint_weight = bell_draw(key_list[4], (2, D, 3 * D), D ** -0.5, 0.21875, ((0, 2),))
    mixer_weight = bell_draw(key_list[5], (2, D, D), (D // 16) ** -0.5, 0.875, ((0, 2),))
    expand_weight = bell_draw(key_list[6], (2, D, FF), D ** -0.5, 0.21875, ((0, 2),))
    contract_weight = bell_draw(key_list[7], (2, FF, D), FF ** -0.5, 0.109375, ((0, 2),))
    head_weight = bell_draw(key_list[8], (2, D, D), D ** -0.5, 0.21875, ((0, 2),))
    gains = jnp.clip(1.0 + 0.1 * jax.random.normal(key_list[9], (2, 3, D), jnp.float32), 0.5, 1.5)
    biases = bell_draw(key_list[10], (2, 8, D), 0.3, 2.0, ((0, 2),), jnp.float32)
    expand_bias = bell_draw(key_list[11], (2, FF), 0.3, 2.0, ((0, 2),), jnp.float32)
    word_table = bell_draw(key_list[12], (VOCAB, D), (D // 4) ** -0.5, 0.4375, ((0, 16),))
    word_bias = bell_draw(key_list[13], (VOCAB,), 0.5, 3.0, ((0, 16),))
    return {"embedded": embedded, "lengths": lengths, "positions": positions, "labels": labels, "joint_weight": joint_weight, "mixer_weight": mixer_weight, "expand_weight": expand_weight, "contract_weight": contract_weight, "head_weight": head_weight, "gains": gains, "biases": biases, "expand_bias": expand_bias, "word_table": word_table, "word_bias": word_bias}


@jax.custom_vjp
def low(v):
    return lax.optimization_barrier(v.astype(jnp.bfloat16)).astype(jnp.float32)

@jax.custom_vjp
def low_back(v):
    return v

def low_keep(v):
    return (low(v), None)

def low_pass(kept, grad):
    return (grad,)

def back_keep(v):
    return (v, None)

def back_low(kept, grad):
    return (low(grad),)
low.defvjp(low_keep, low_pass)
low_back.defvjp(back_keep, back_low)
EPS = 1e-12

def mult(left, right):
    return jnp.dot(left, right, precision=lax.Precision.HIGHEST, preferred_element_type=jnp.float32)

def norm(resid, gain, shift):
    centre = resid - lax.optimization_barrier(jnp.mean(resid, axis=-1, keepdims=True))
    scale_inv = lax.rsqrt(lax.optimization_barrier(jnp.mean(centre * centre, axis=-1, keepdims=True)) + EPS)
    return centre * scale_inv * gain + shift

def layer(inputs, length, joint, mixer, expand, contract, gain, bias, expand_shift):
    project = mult(low(inputs), joint)
    queries = low(low_back(project[:, :D] + bias[0])).reshape(LEN, HEADS, HEAD_DIM)
    keys = low(low_back(project[:, D:2 * D])).reshape(LEN, HEADS, HEAD_DIM)
    values = low(low_back(project[:, 2 * D:] + bias[1])).reshape(LEN, HEADS, HEAD_DIM)
    scores = low_back(jnp.einsum('qhd,khd->hqk', queries, keys, precision=lax.Precision.HIGHEST) * HEAD_DIM ** (-0.5))
    visible = jnp.arange(LEN) < length
    scores = jnp.where(visible[None, None, :], scores, -1000000000.0)
    attention = low(jax.nn.softmax(scores, axis=-1))
    context = jnp.einsum('hqk,khd->qhd', attention, values, precision=lax.Precision.HIGHEST).reshape(LEN, D)
    context = low(low_back(context))
    mixed = low_back(mult(context, mixer) + bias[2])
    first = norm(inputs + mixed, gain[0], bias[3])
    hidden = low_back(mult(low(first), expand) + expand_shift)
    active = low(jax.nn.gelu(hidden, approximate=False))
    branch = low_back(mult(active, contract) + bias[4])
    return norm(first + branch, gain[1], bias[5])

def head(hidden_rows, places, answers, head_matrix, gain, bias, table, word_shift):
    picked = hidden_rows[places]
    dense = low_back(mult(low(picked), head_matrix) + bias[6])
    normed = low(norm(jax.nn.gelu(dense, approximate=False), gain[2], bias[7]))
    scores = low_back(jnp.dot(normed, table.T, precision=lax.Precision.HIGHEST, preferred_element_type=jnp.float32) + word_shift)
    cross = jax.nn.logsumexp(scores, axis=-1) - jnp.take_along_axis(scores, answers[:, None], axis=1)[:, 0]
    return (jnp.sum(cross), scores)

def reference(embedded, lengths, positions, labels, joint_weight, mixer_weight, expand_weight, contract_weight, head_weight, gains, biases, expand_bias, word_table, word_bias):
    floats = [value.astype(jnp.float32) for value in (embedded, joint_weight, mixer_weight, expand_weight, contract_weight, head_weight, gains, biases, expand_bias, word_table, word_bias)]

    def forward(emb, joint, mixer, expand, contract, head_matrix, gain_all, bias_all, expand_all, table, word_shift):

        def run(section, sources):

            def step(total, item):
                inputs, length, places, answers, cls_row = item
                if section == 1:
                    inputs = inputs.at[0].set(cls_row)
                hidden_rows = layer(inputs, length, joint[section], mixer[section], expand[section], contract[section], gain_all[section], bias_all[section], expand_all[section])
                cross, scores = head(hidden_rows, places, answers, head_matrix[section], gain_all[section], bias_all[section], table, word_shift)
                return (total + cross, (scores, low(low_back(hidden_rows[0]))))
            return lax.scan(jax.checkpoint(step), jnp.zeros((), jnp.float32), sources)
        first_total, (first_scores, cls_rows) = run(0, (emb[0], lengths, positions[0], labels[0], emb[0][:, 0]))
        second_total, (second_scores, unused) = run(1, (emb[1], lengths, positions[1], labels[1], cls_rows))
        count = PASSAGES * MASK
        losses = jnp.stack([first_total, second_total]) / count
        return ((first_total + second_total) / MASK, (losses, jnp.stack([first_scores, second_scores])))
    total, pull, (loss, scores) = jax.vjp(forward, *floats, has_aux=True)
    grads = pull(jnp.ones_like(total))
    return (loss, scores.astype(jnp.bfloat16), grads[0], grads[1], grads[2], grads[3], grads[4], grads[5], grads[6], grads[7], grads[8], grads[9], grads[10])
```

```python
import functools

import jax
import jax.numpy as jnp
from jax import lax
from jax.experimental import pallas as pl
from jax.experimental.pallas import tpu as pltpu
from jax.sharding import PartitionSpec as P

HEADS = 12
EPS = 1e-12
ROOT_HALF = 0.7071067811865476
INV_ROOT_TAU = 0.3989422804014327
HIDDEN = -1000000000.0
LANES = 128
VMEM = 56 * 1024 * 1024
F32 = jnp.float32
BF16 = jnp.bfloat16


def product(left, right, left_dim, right_dim):
    return lax.dot_general(
        left, right, (((left_dim,), (right_dim,)), ((), ())), preferred_element_type=F32
    )


def matmul(left, right):
    return product(left, right, 1, 0)


def outer_sum(left, right):
    return product(left, right, 0, 0)


def back_mul(left, right):
    return product(left, right, 1, 1)


def passed_along(block, axis, distance):
    devices = range(lax.axis_size(axis))
    route = [(i - distance, i) for i in devices if i - distance in devices]
    return lax.ppermute(block, axis, route)


def swapped(block, bit):
    devices = range(lax.axis_size("dp"))
    return lax.ppermute(block, "dp", [(i, i ^ bit) for i in devices])


def bits_of(order):
    return [1 << i for i in range(order.bit_length() - 1)]


def gather_all(block):
    place = lax.axis_index("dp")
    shape = block.shape
    block = block[None]
    for bit in reversed(bits_of(lax.axis_size("dp"))):
        other = swapped(block, bit)
        low = (place & bit) == 0
        pair = [jnp.where(low, block, other), jnp.where(low, other, block)]
        block = jnp.stack(pair, axis=1).reshape((-1,) + shape)
    return block.reshape((-1,) + shape[1:])


def gather_near(block):
    near = lax.axis_size("dp") // 2
    parts = [block] + [swapped(block, mask) for mask in range(2, near, 2)]
    block = jnp.stack(parts)
    return jnp.stack([block, swapped(block, 1)], axis=1).reshape((near,) + parts[0].shape)


def scatter_near(blocks):
    blocks = blocks.reshape((-1, 2) + blocks.shape[1:])
    got = swapped(blocks[:, 1], 1)
    blocks = (blocks[:, 0].astype(F32) + got.astype(F32)).astype(BF16)
    total = blocks[0].astype(F32)
    for i in range(1, blocks.shape[0]):
        total = total + swapped(blocks[i], 2 * i).astype(F32)
    return total


def normalise(resid):
    centre = resid - jnp.mean(resid, axis=-1, keepdims=True)
    scale_inv = lax.rsqrt(jnp.mean(centre * centre, axis=-1, keepdims=True) + EPS)
    return centre * scale_inv, scale_inv


def norm_back(scaled, normed, scale_inv):
    first_mean = jnp.mean(scaled, axis=-1, keepdims=True)
    second_mean = jnp.mean(scaled * normed, axis=-1, keepdims=True)
    return scale_inv * (scaled - first_mean - normed * second_mean)


def gelu_and_slope(value):
    gate = 0.5 * (1.0 + lax.erf(value * ROOT_HALF))
    return value * gate, gate + value * jnp.exp(-0.5 * value * value) * INV_ROOT_TAU


def attend_kernel(lengths, q_ref, k_ref, v_ref, out_ref, log_ref, *, head_dim):
    length = lengths[pl.program_id(0)]
    rows, lanes = q_ref.shape
    q = q_ref[...] * (head_dim**-0.5)
    k = k_ref[...]
    v_t = v_ref[...].T
    head_of = lax.broadcasted_iota(jnp.int32, (rows, lanes), 1) // head_dim
    visible = lax.broadcasted_iota(jnp.int32, (rows, rows), 0) < length
    parts = []
    for head in range(lanes // head_dim):
        scores = back_mul(k, jnp.where(head_of == head, q, jnp.zeros_like(q)))
        scores = jnp.where(visible, scores, HIDDEN)
        peak = jnp.max(scores, axis=0, keepdims=True)
        powers = jnp.exp(scores - peak)
        total = jnp.sum(powers, axis=0, keepdims=True)
        piece = matmul(v_t[head * head_dim : (head + 1) * head_dim], powers.astype(BF16))
        parts.append(piece / total)
        log_ref[0, head : head + 1, :] = peak + jnp.log(total)
    out_ref[...] = jnp.concatenate(parts, axis=0).T.astype(BF16)


def attend(qkv, lengths, count):
    rows = qkv.shape[0] // count
    width = qkv.shape[1] // 3
    pairs = width // LANES
    head_dim = width // HEADS
    block = lambda part: pl.BlockSpec((rows, LANES), lambda b, p, _: (b, part * pairs + p))
    return pl.pallas_call(
        functools.partial(attend_kernel, head_dim=head_dim),
        grid_spec=pltpu.PrefetchScalarGridSpec(
            num_scalar_prefetch=1,
            grid=(count, pairs),
            in_specs=[block(0), block(1), block(2)],
            out_specs=[
                pl.BlockSpec((rows, LANES), lambda b, p, _: (b, p)),
                pl.BlockSpec((1, LANES // head_dim, rows), lambda b, p, _: (b * pairs + p, 0, 0)),
            ],
        ),
        out_shape=[
            jax.ShapeDtypeStruct((count * rows, width), BF16),
            jax.ShapeDtypeStruct((count * pairs, LANES // head_dim, rows), F32),
        ],
        compiler_params=pltpu.CompilerParams(vmem_limit_bytes=VMEM),
        name="attend",
    )(lengths, qkv, qkv, qkv)


def attend_back_kernel(lengths, q_ref, k_ref, v_ref, grad_ref, log_ref, *refs, head_dim, passage):
    out_ref = refs[-1]
    length = lengths[passage]
    rows, lanes = q_ref.shape
    scale = head_dim**-0.5
    q = q_ref[...] * scale
    k = k_ref[...]
    v = v_ref[...]
    grad = grad_ref[...]
    head_of = lax.broadcasted_iota(jnp.int32, (rows, lanes), 1) // head_dim
    visible = lax.broadcasted_iota(jnp.int32, (rows, rows), 0) < length
    totals = [jnp.zeros((rows, lanes), F32)] * 3
    for head in range(lanes // head_dim):
        mine = head_of == head
        scores = back_mul(k, jnp.where(mine, q, jnp.zeros_like(q)))
        share = jnp.where(visible, jnp.exp(scores - log_ref[0, head : head + 1, :]), 0.0)
        share_grad = back_mul(jnp.where(mine, v, jnp.zeros_like(v)), grad)
        inner = jnp.sum(share * share_grad, axis=0, keepdims=True)
        score_grad = (share * (share_grad - inner)).astype(BF16)
        parts = (
            outer_sum(score_grad, k) * scale,
            matmul(score_grad, q),
            matmul(share.astype(BF16), grad),
        )
        totals = [jnp.where(mine, part, total) for part, total in zip(parts, totals)]
    for i, total in enumerate(totals):
        out_ref[i] = total.astype(BF16)


def attend_back(qkv, grad, logs, lengths, passage, done=()):
    count = lengths.shape[0]
    rows = qkv.shape[0] // count
    width = qkv.shape[1] // 3
    pairs = width // LANES
    head_dim = width // HEADS
    block = lambda part: pl.BlockSpec((rows, LANES), lambda p, _: (passage, part * pairs + p))
    return pl.pallas_call(
        functools.partial(attend_back_kernel, head_dim=head_dim, passage=passage),
        grid_spec=pltpu.PrefetchScalarGridSpec(
            num_scalar_prefetch=1,
            grid=(pairs,),
            in_specs=[
                block(0),
                block(1),
                block(2),
                block(0),
                pl.BlockSpec((1, LANES // head_dim, rows), lambda p, _: (passage * pairs + p, 0, 0)),
            ]
            + [pl.BlockSpec(memory_space=pl.ANY)] * len(done),
            out_specs=pl.BlockSpec((3, rows, LANES), lambda p, _: (0, passage, p)),
        ),
        out_shape=jax.ShapeDtypeStruct((3, count * rows, width), BF16),
        input_output_aliases={6: 0} if done else {},
        compiler_params=pltpu.CompilerParams(vmem_limit_bytes=VMEM),
        name="attend_back",
    )(lengths, qkv, qkv, qkv, grad, logs, *done)


def tail_kernel(
    ctx_ref, x_ref, mixer_ref, expand_ref, contract_ref, gain_ref, bias_ref, shift_ref,
    y_ref, normed_one_ref, scale_one_ref, first_ref, active_ref, slope_ref, normed_two_ref, scale_two_ref,
    *, chunk,
):
    mixed = matmul(ctx_ref[...], mixer_ref[...]) + bias_ref[2:3]
    normed, scale = normalise(x_ref[...].astype(F32) + mixed)
    first = normed * gain_ref[0:1] + bias_ref[3:4]
    first_low = first.astype(BF16)
    normed_one_ref[...] = normed.astype(BF16)
    scale_one_ref[...] = jnp.broadcast_to(scale, scale_one_ref.shape)
    first_ref[...] = first_low
    total = first + bias_ref[4:5]
    for start in range(0, expand_ref.shape[1], chunk):
        part = slice(start, start + chunk)
        hidden = matmul(first_low, expand_ref[:, part]) + shift_ref[0:1, part]
        active, slope = gelu_and_slope(hidden)
        active = active.astype(BF16)
        active_ref[:, part] = active
        slope_ref[:, part] = slope.astype(BF16)
        total = total + matmul(active, contract_ref[part, :])
    normed, scale = normalise(total)
    normed_two_ref[...] = normed.astype(BF16)
    scale_two_ref[...] = jnp.broadcast_to(scale, scale_two_ref.shape)
    y_ref[...] = (normed * gain_ref[1:2] + bias_ref[5:6]).astype(BF16)


def whole(array):
    return pl.BlockSpec(array.shape, lambda *_: (0,) * array.ndim, pipeline_mode=pl.Buffered(1))


def layer_tail(ctx, x, mats, gain, bias, shift, step=256, chunk=3072):
    rows, width = x.shape
    hidden = shift.shape[1]
    step = min(step, rows)
    by_row = lambda n: pl.BlockSpec((step, n), lambda i: (i, 0))
    shape = lambda n, kind: jax.ShapeDtypeStruct((rows, n), kind)
    widths = [(width, BF16), (width, BF16), (LANES, F32), (width, BF16), (hidden, BF16), (hidden, BF16), (width, BF16), (LANES, F32)]
    return pl.pallas_call(
        functools.partial(tail_kernel, chunk=min(chunk, hidden)),
        grid=(rows // step,),
        in_specs=[by_row(width), by_row(width)] + [whole(m) for m in mats + (gain, bias, shift)],
        out_specs=[by_row(n) for n, _ in widths],
        out_shape=[shape(n, kind) for n, kind in widths],
        compiler_params=pltpu.CompilerParams(vmem_limit_bytes=VMEM),
        name="layer_tail",
    )(ctx, x, *mats, gain, bias, shift)


def tail_back_kernel(
    grad_ref, normed_two_ref, scale_two_ref, slope_ref, normed_one_ref, scale_one_ref,
    mixer_ref, expand_ref, contract_ref, gain_ref,
    branch_ref, hidden_ref, one_ref, mixed_ref, ctx_ref, sums_ref, shift_sum_ref,
    *, chunk,
):
    @pl.when(pl.program_id(0) == 0)
    def _():
        sums_ref[...] = jnp.zeros_like(sums_ref)
        shift_sum_ref[...] = jnp.zeros_like(shift_sum_ref)

    def add_sum(row, value):
        sums_ref[row : row + 1] += jnp.sum(value, axis=0, keepdims=True)

    grad = grad_ref[...]
    normed = normed_two_ref[...].astype(F32)
    add_sum(0, grad * normed)
    add_sum(1, grad)
    total = norm_back(grad * gain_ref[1:2], normed, scale_two_ref[:, 0:1])
    branch = total.astype(BF16)
    branch_ref[...] = branch
    add_sum(2, branch.astype(F32))
    for start in range(0, expand_ref.shape[1], chunk):
        part = slice(start, start + chunk)
        hidden = back_mul(branch, contract_ref[part, :]) * slope_ref[:, part].astype(F32)
        hidden = hidden.astype(BF16)
        hidden_ref[:, part] = hidden
        shift_sum_ref[0:1, part] += jnp.sum(hidden.astype(F32), axis=0, keepdims=True)
        total = total + back_mul(hidden, expand_ref[:, part])
    normed = normed_one_ref[...].astype(F32)
    add_sum(3, total * normed)
    add_sum(4, total)
    total = norm_back(total * gain_ref[0:1], normed, scale_one_ref[:, 0:1])
    one_ref[...] = total
    mixed = total.astype(BF16)
    mixed_ref[...] = mixed
    add_sum(5, mixed.astype(F32))
    ctx_ref[...] = back_mul(mixed, mixer_ref[...]).astype(BF16)


def tail_back(grad, kept, mats, gain, step=256, chunk=3072):
    rows, width = grad.shape
    hidden = mats[1].shape[1]
    step = min(step, rows)
    by_row = lambda n: pl.BlockSpec((step, n), lambda i: (i, 0))
    shape = lambda n, kind: jax.ShapeDtypeStruct((rows, n), kind)
    widths = [(width, BF16), (hidden, BF16), (width, F32), (width, BF16), (width, BF16)]
    return pl.pallas_call(
        functools.partial(tail_back_kernel, chunk=min(chunk, hidden)),
        grid=(rows // step,),
        in_specs=[by_row(array.shape[1]) for array in (grad,) + kept] + [whole(m) for m in mats + (gain,)],
        out_specs=[by_row(n) for n, _ in widths]
        + [pl.BlockSpec((8, width), lambda i: (0, 0)), pl.BlockSpec((1, hidden), lambda i: (0, 0))],
        out_shape=[shape(n, kind) for n, kind in widths]
        + [jax.ShapeDtypeStruct((8, width), F32), jax.ShapeDtypeStruct((1, hidden), F32)],
        compiler_params=pltpu.CompilerParams(vmem_limit_bytes=VMEM),
        name="tail_back",
    )(grad, *kept, *mats, gain)


PACK = 16


def first_block(rows, width, passage):
    return pl.BlockSpec((PACK, width), lambda *_: (passage * rows // PACK, 0))


def packed(refs):
    rows = [ref[...].astype(F32)[0:1] for ref in refs]
    place = lax.broadcasted_iota(jnp.int32, (PACK, rows[0].shape[1]), 0)
    total = jnp.zeros((PACK, rows[0].shape[1]), F32)
    for i, row in enumerate(rows):
        total = jnp.where(place == i, row, total)
    return total


def per_head(row, head_dim):
    shape = (PACK, row.shape[1])
    mine = lax.broadcasted_iota(jnp.int32, shape, 1) // head_dim == lax.broadcasted_iota(jnp.int32, shape, 0)
    return jnp.where(mine, row, 0.0)


def heads_joined(block, head_dim):
    mine = lax.broadcasted_iota(jnp.int32, block.shape, 1) // head_dim == lax.broadcasted_iota(jnp.int32, block.shape, 0)
    return jnp.sum(jnp.where(mine, block, 0.0), axis=0, keepdims=True)


def first_share(query, keys, length):
    scores = back_mul(query, keys)
    visible = lax.broadcasted_iota(jnp.int32, scores.shape, 1) < length
    scores = jnp.where(visible, scores, HIDDEN)
    powers = jnp.exp(scores - jnp.max(scores, axis=1, keepdims=True))
    return powers / jnp.sum(powers, axis=1, keepdims=True)


def cls_kernel(lengths, *refs, count, rows, head_dim, chunk):
    x_refs, (qkv_ref, mixer_ref, expand_ref, contract_ref, gain_ref, bias_ref, shift_ref, out_ref) = (
        refs[:count],
        refs[count:],
    )
    width = out_ref.shape[1]
    x = packed(x_refs)
    place = lax.broadcasted_iota(jnp.int32, (PACK, width), 0)
    ctx = jnp.zeros((PACK, width), F32)
    for b in range(count):
        base = b * rows
        query = qkv_ref[base : base + PACK, 0:width].astype(F32)[0:1] * head_dim**-0.5
        query = per_head(query, head_dim).astype(BF16)
        share = first_share(query, qkv_ref[base : base + rows, width : 2 * width], lengths[b])
        mixed = matmul(share.astype(BF16), qkv_ref[base : base + rows, 2 * width : 3 * width])
        ctx = jnp.where(place == b, heads_joined(mixed, head_dim), ctx)
    mixed = matmul(ctx.astype(BF16), mixer_ref[...]) + bias_ref[2:3]
    first = normalise(x + mixed)[0] * gain_ref[0:1] + bias_ref[3:4]
    first_low = first.astype(BF16)
    total = first + bias_ref[4:5]
    for start in range(0, expand_ref.shape[1], chunk):
        part = slice(start, start + chunk)
        active, _ = gelu_and_slope(matmul(first_low, expand_ref[:, part]) + shift_ref[0:1, part])
        total = total + matmul(active.astype(BF16), contract_ref[part, :])
    out_ref[...] = (normalise(total)[0] * gain_ref[1:2] + bias_ref[5:6]).astype(BF16)


def cls_forward(x, qkv, lengths, mats, gain, bias, shift):
    count = lengths.shape[0]
    rows, width = x.shape[0] // count, x.shape[1]
    rest = (qkv,) + mats + (gain, bias, shift)
    return pl.pallas_call(
        functools.partial(cls_kernel, count=count, rows=rows, head_dim=width // HEADS, chunk=768),
        grid_spec=pltpu.PrefetchScalarGridSpec(
            num_scalar_prefetch=1,
            grid=(1,),
            in_specs=[first_block(rows, width, b) for b in range(count)] + [whole(r) for r in rest],
            out_specs=pl.BlockSpec((PACK, width), lambda *_: (0, 0)),
        ),
        out_shape=jax.ShapeDtypeStruct((PACK, width), BF16),
        compiler_params=pltpu.CompilerParams(vmem_limit_bytes=VMEM),
        name="cls_forward",
    )(lengths, *[x] * count, *rest)


def place_kernel(decoder, cls_ref, x_ref, qkv_ref, joint_ref, shift_ref, x_out, qkv_out, new_ref):
    step = pl.program_id(0)

    @pl.when(step == 0)
    def _():
        new_ref[...] = (matmul(cls_ref[...], joint_ref[...]) + shift_ref[...]).astype(BF16).astype(F32)

    def put(old, new, out):
        spot = lax.broadcasted_iota(jnp.int32, new.shape, 0)
        row = jnp.sum(jnp.where(spot == step, new, 0.0), axis=0, keepdims=True)
        here = (spot == 0) & (decoder[0] == 1)
        out[...] = jnp.where(here, row, old.astype(F32)).astype(BF16)

    put(x_ref[...], cls_ref[...].astype(F32), x_out)
    put(qkv_ref[...], new_ref[...], qkv_out)


def place_first(decoder, cls, x, qkv, joint, shift, count):
    rows, width = x.shape[0] // count, x.shape[1]
    block = lambda n: pl.BlockSpec((PACK, n), lambda b, _: (b * rows // PACK, 0))
    return pl.pallas_call(
        place_kernel,
        grid_spec=pltpu.PrefetchScalarGridSpec(
            num_scalar_prefetch=1,
            grid=(count,),
            in_specs=[whole(cls), block(width), block(3 * width), whole(joint), whole(shift)],
            out_specs=[block(width), block(3 * width)],
            scratch_shapes=[pltpu.VMEM((PACK, 3 * width), F32)],
        ),
        out_shape=[jax.ShapeDtypeStruct(x.shape, BF16), jax.ShapeDtypeStruct(qkv.shape, BF16)],
        input_output_aliases={2: 0, 3: 1},
        compiler_params=pltpu.CompilerParams(vmem_limit_bytes=VMEM),
        name="place_first",
    )(decoder, cls, x, qkv, joint, shift)


def cls_grad_kernel(*refs, count):
    part_refs, one_refs, (joint_ref, out_ref) = refs[:count], refs[count : 2 * count], refs[2 * count :]
    width = out_ref.shape[1]
    total = packed(one_refs)
    for i in range(3):
        grad = packed([ref.at[i] for ref in part_refs]).astype(BF16)
        total = total + back_mul(grad, joint_ref[:, i * width : (i + 1) * width])
    out_ref[...] = total.astype(BF16)


def cls_back(parts, one, joint, count):
    rows, width = one.shape[0] // count, one.shape[1]
    part = lambda b: pl.BlockSpec((3, PACK, width), lambda *_: (0, b * rows // PACK, 0))
    return pl.pallas_call(
        functools.partial(cls_grad_kernel, count=count),
        grid=(1,),
        in_specs=[part(b) for b in range(count)]
        + [first_block(rows, width, b) for b in range(count)]
        + [whole(joint)],
        out_specs=pl.BlockSpec((PACK, width), lambda *_: (0, 0)),
        out_shape=jax.ShapeDtypeStruct((PACK, width), BF16),
        compiler_params=pltpu.CompilerParams(vmem_limit_bytes=VMEM),
        name="cls_back",
    )(*[parts] * count, *[one] * count, joint)


def first_back_kernel(lengths, grad_ref, *refs, count, rows, head_dim, chunk):
    kept = [packed(refs[i * count : (i + 1) * count]) for i in range(5)]
    normed_two, scale_two, slope, normed_one, scale_one = kept
    scale_two, scale_one = scale_two[:, 0:1], scale_one[:, 0:1]
    mixer_ref, expand_ref, contract_ref, gain_ref, qkv_ref, parts_ref = refs[5 * count : 5 * count + 6]
    branch_ref, hidden_ref, mixed_ref, one_ref, sums_ref, shift_sum_ref, out_ref, part_sums_ref = refs[5 * count + 6 :]
    width = grad_ref.shape[1]
    grad = grad_ref[...].astype(F32)
    sums_ref[...] = jnp.zeros_like(sums_ref)

    def add_sum(row, value):
        sums_ref[row : row + 1] = jnp.sum(value, axis=0, keepdims=True)

    add_sum(0, grad * normed_two)
    add_sum(1, grad)
    total = norm_back(grad * gain_ref[1:2], normed_two, scale_two)
    branch = total.astype(BF16)
    branch_ref[...] = branch
    add_sum(2, branch.astype(F32))
    for start in range(0, expand_ref.shape[1], chunk):
        part = slice(start, start + chunk)
        hidden = (back_mul(branch, contract_ref[part, :]) * slope[:, part]).astype(BF16)
        hidden_ref[:, part] = hidden
        shift_sum_ref[0:1, part] = jnp.sum(hidden.astype(F32), axis=0, keepdims=True)
        total = total + back_mul(hidden, expand_ref[:, part])
    add_sum(3, total * normed_one)
    add_sum(4, total)
    total = norm_back(total * gain_ref[0:1], normed_one, scale_one)
    one_ref[...] = total
    mixed = total.astype(BF16)
    mixed_ref[...] = mixed
    add_sum(5, mixed.astype(F32))
    ctx = back_mul(mixed, mixer_ref[...]).astype(BF16).astype(F32)
    for b in range(count):
        span = slice(b * rows, (b + 1) * rows)
        keys, values = qkv_ref[span, width : 2 * width], qkv_ref[span, 2 * width : 3 * width]
        query = qkv_ref[b * rows : b * rows + PACK, 0:width].astype(F32)[0:1] * head_dim**-0.5
        query = per_head(query, head_dim).astype(BF16)
        share = first_share(query, keys, lengths[b])
        ctx_heads = per_head(ctx[b : b + 1], head_dim).astype(BF16)
        share_grad = back_mul(ctx_heads, values)
        inner = jnp.sum(share * share_grad, axis=1, keepdims=True)
        score = (share * (share_grad - inner)).astype(BF16)
        query_grad = heads_joined(matmul(score, keys), head_dim) * head_dim**-0.5
        head_rows = parts_ref[0, b * rows : b * rows + PACK].astype(F32)
        top = lax.broadcasted_iota(jnp.int32, head_rows.shape, 0) == 0
        out_ref[0, span] = parts_ref[0, span]
        out_ref[0, b * rows : b * rows + PACK] = jnp.where(top, head_rows + query_grad, head_rows).astype(BF16)
        out_ref[1, span] = (parts_ref[1, span].astype(F32) + outer_sum(score, query)).astype(BF16)
        out_ref[2, span] = (parts_ref[2, span].astype(F32) + outer_sum(share.astype(BF16), ctx_heads)).astype(BF16)
    part_sums_ref[...] = jnp.zeros_like(part_sums_ref)
    for i in (0, 2):
        part_sums_ref[i : i + 1] = jnp.sum(out_ref[i].astype(F32), axis=0, keepdims=True)


def first_back(grad, kept, mats, gain, qkv, parts, lengths):
    count = lengths.shape[0]
    rows, width = qkv.shape[0] // count, grad.shape[1]
    hidden = mats[1].shape[1]
    blocks = [first_block(rows, array.shape[1], b) for array in kept for b in range(count)]
    rest = mats + (gain, qkv, parts)
    small = lambda n, kind, r=PACK: (pl.BlockSpec((r, n), lambda *_: (0, 0)), jax.ShapeDtypeStruct((r, n), kind))
    outs = [small(width, BF16), small(hidden, BF16), small(width, BF16), small(width, F32), small(width, F32, 8), small(hidden, F32, 1)]
    outs.append((whole(parts), jax.ShapeDtypeStruct(parts.shape, BF16)))
    outs.append(small(width, F32, 8))
    return pl.pallas_call(
        functools.partial(first_back_kernel, count=count, rows=rows, head_dim=width // HEADS, chunk=768),
        grid_spec=pltpu.PrefetchScalarGridSpec(
            num_scalar_prefetch=1,
            grid=(1,),
            in_specs=[whole(grad)] + blocks + [whole(r) for r in rest],
            out_specs=[spec for spec, _ in outs],
        ),
        out_shape=[shape for _, shape in outs],
        compiler_params=pltpu.CompilerParams(vmem_limit_bytes=VMEM),
        name="first_back",
    )(lengths, grad, *[array for array in kept for _ in range(count)], *rest)


def project_kernel(x_ref, joint_ref, shift_ref, out_ref):
    out_ref[...] = (matmul(x_ref[...], joint_ref[...]) + shift_ref[...]).astype(BF16)


def project(x, joint, shift):
    rows, width = x.shape
    step = min(256, rows)
    return pl.pallas_call(
        project_kernel,
        grid=(rows // step,),
        in_specs=[pl.BlockSpec((step, width), lambda i: (i, 0)), whole(joint), whole(shift)],
        out_specs=pl.BlockSpec((step, joint.shape[1]), lambda i: (i, 0)),
        out_shape=jax.ShapeDtypeStruct((rows, joint.shape[1]), BF16),
        compiler_params=pltpu.CompilerParams(vmem_limit_bytes=VMEM),
        name="project",
    )(x, joint, shift)


def input_grad_kernel(decoder, parts_ref, one_ref, first_ref, joint_ref, out_ref, *, step, rows):
    i = pl.program_id(0)
    width = out_ref.shape[1]

    total = one_ref[...]
    for j in range(3):
        total = total + back_mul(parts_ref[j], joint_ref[:, j * width : (j + 1) * width])
    out_ref[...] = total

    @pl.when(lax.rem(i * step, rows) == 0)
    def _():
        spot = lax.broadcasted_iota(jnp.int32, first_ref.shape, 0)
        row = jnp.sum(jnp.where(spot == i * step // rows, first_ref[...], 0.0), axis=0, keepdims=True)
        head = total[0:8]
        keep = jnp.where(decoder[0] == 1, 0.0, 1.0)
        top = lax.broadcasted_iota(jnp.int32, head.shape, 0) == 0
        out_ref[0:8] = jnp.where(top, (head + row) * keep, head)


def input_gradient(decoder, parts, one, one_first, joint, count):
    total_rows, width = one.shape
    rows = total_rows // count
    step = min(256, rows)
    return pl.pallas_call(
        functools.partial(input_grad_kernel, step=step, rows=rows),
        grid_spec=pltpu.PrefetchScalarGridSpec(
            num_scalar_prefetch=1,
            grid=(total_rows // step,),
            in_specs=[
                pl.BlockSpec((3, step, width), lambda i, _: (0, i, 0)),
                pl.BlockSpec((step, width), lambda i, _: (i, 0)),
                whole(one_first),
                whole(joint),
            ],
            out_specs=pl.BlockSpec((step, width), lambda i, _: (i, 0)),
        ),
        out_shape=jax.ShapeDtypeStruct(one.shape, F32),
        compiler_params=pltpu.CompilerParams(vmem_limit_bytes=VMEM),
        name="input_gradient",
    )(decoder, parts, one, one_first, joint)


def weight_grad_kernel(place, left_ref, right_ref, *refs):
    keep_ref, send_ref = refs[-2:]
    own, rows, _ = keep_ref.shape
    total = outer_sum(left_ref[...], right_ref[0]).astype(BF16)
    odd = lax.rem(place[0], 2) == 1
    for i in range(own):
        pair = [total[(2 * i + j) * rows : (2 * i + j + 1) * rows] for j in range(2)]
        keep_ref[i] = jnp.where(odd, pair[1], pair[0])
        send_ref[i] = jnp.where(odd, pair[0], pair[1])


def weight_grads(place, *pairs, tile=768):
    groups = lax.axis_size("dp")
    pairs = [(left, right if right.ndim == 3 else right[None]) for left, right in pairs]
    width = min(right.shape[2] for _, right in pairs)
    sizes = [left.shape[1] // groups for left, _ in pairs]
    heights = [size * right.shape[0] * right.shape[2] // width for size, (_, right) in zip(sizes, pairs)]
    if any(size % 16 for size in sizes):
        blocks = []
        for size, (left, right) in zip(sizes, pairs):
            total = jnp.concatenate([outer_sum(left, r) for r in right], axis=1).astype(BF16)
            total = total.reshape(groups, size, -1, width).transpose(0, 2, 1, 3)
            blocks.append(total.reshape(groups // 2, 2, -1, width))
        blocks = jnp.concatenate(blocks, axis=2)
        odd = lax.rem(place, 2)
        return tuple(lax.dynamic_index_in_dim(blocks, i, 1, False) for i in (odd, 1 - odd))
    shape = jax.ShapeDtypeStruct((groups // 2, sum(heights), width), BF16)
    done = []
    for i, (size, (left, right)) in enumerate(zip(sizes, pairs)):
        rows, height = left.shape
        cuts = right.shape[2] // width
        first = sum(heights[:i]) // size
        spec = pl.BlockSpec((tile // size // 2, size, width), lambda j, i, _, first=first: (i, first + j, 0))
        done = pl.pallas_call(
            weight_grad_kernel,
            grid_spec=pltpu.PrefetchScalarGridSpec(
                num_scalar_prefetch=1,
                grid=(right.shape[0] * cuts, height // tile),
                in_specs=[
                    pl.BlockSpec((rows, tile), lambda j, i, _: (0, i)),
                    pl.BlockSpec((1, rows, width), lambda j, i, _, cuts=cuts: (j // cuts, 0, j % cuts)),
                ]
                + [pl.BlockSpec(memory_space=pl.ANY)] * len(done),
                out_specs=[spec, spec],
            ),
            out_shape=[shape, shape],
            input_output_aliases={3: 0, 4: 1} if done else {},
            compiler_params=pltpu.CompilerParams(vmem_limit_bytes=VMEM),
            name="weight_grad",
        )(place.reshape(1), left, right, *done)
    return tuple(done)


def unstacked(total, shapes):
    parts = []
    start = 0
    for rows, columns in shapes:
        height = rows * columns // total.shape[1]
        part = total[start : start + height].reshape(-1, rows, total.shape[1])
        parts.append(part.transpose(1, 0, 2).reshape(rows, columns))
        start += height
    return parts


def add_split_kernel(mine, keep_a, got_a, keep_b, got_b, keep_ref, send_ref):
    keep_ref[...] = (keep_a[...].astype(F32) + got_a[...].astype(F32)).astype(BF16)
    send_ref[...] = (keep_b[...].astype(F32) + got_b[...].astype(F32)).astype(BF16)


def add_split(keep, got, axis, mine):
    rows, width = keep.shape[-2:]
    if rows % 16:
        total = (keep.astype(F32) + got.astype(F32)).astype(BF16)
        return tuple(lax.dynamic_index_in_dim(total, i, axis, False) for i in (mine, 1 - mine))
    rest = keep.shape[:axis] + keep.shape[axis + 1 : -2]
    before = 2**axis
    after = 2 ** (len(rest) - axis)
    shaped = [array.reshape(before, 2, after, rows, width) for array in (keep, got)]
    block = lambda other: pl.BlockSpec(
        (before, None, after, rows, min(width, 768)), lambda j, m: (0, (1 - m[0]) if other else m[0], 0, 0, j)
    )
    out = pl.BlockSpec((before, after, rows, min(width, 768)), lambda j, m: (0, 0, 0, j))
    shape = jax.ShapeDtypeStruct((before, after, rows, width), BF16)
    keep, send = pl.pallas_call(
        add_split_kernel,
        grid_spec=pltpu.PrefetchScalarGridSpec(
            num_scalar_prefetch=1,
            grid=(width // min(width, 768),),
            in_specs=[block(False), block(False), block(True), block(True)],
            out_specs=[out, out],
        ),
        out_shape=[shape, shape],
        compiler_params=pltpu.CompilerParams(vmem_limit_bytes=VMEM),
        name="add_split",
    )(mine.reshape(1), *shaped, *shaped)
    return keep.reshape(rest + (rows, width)), send.reshape(rest + (rows, width))


def first_hop(pair):
    keep, send = pair
    axes = tuple(reversed(bits_of(lax.axis_size("dp"))))[:-1]
    shape = (2,) * len(axes) + keep.shape[1:]
    return keep.reshape(shape), swapped(send, 1).reshape(shape), axes


def added(state, bit):
    keep, got, axes = state
    axis = axes.index(bit)
    mine = jnp.where((lax.axis_index("dp") & bit) == 0, 0, 1)
    return (*add_split(keep, got, axis, mine), axes[:axis] + axes[axis + 1 :])


def sent(halves, bit):
    keep, send, axes = halves
    return keep, swapped(send, bit), axes


def rest_of(state, order):
    for bit in order:
        state = sent(added(state, bit), bit)
    return state[0].astype(F32) + state[1].astype(F32)


def tied(*values):
    return lax.optimization_barrier(values)


def as_row(column):
    return jnp.broadcast_to(column, (column.shape[0], LANES)).T[0:1]


def as_column(row):
    return jnp.broadcast_to(row, (LANES, row.shape[1])).T[:, 0:1]


def word_cuts(slice_rows):
    size = 768
    return [
        (i, slice(start, min(start + size, slice_rows)), slice(i * slice_rows + start, i * slice_rows + min(start + size, slice_rows)))
        for i in range(2)
        for start in range(0, slice_rows, size)
    ]


def join(section, mine_ref, other_ref, out_ref):
    @pl.when(pl.program_id(0) == 0)
    def _():
        half = mine_ref.shape[0]
        swap = section == 1
        mine, other = mine_ref[...], other_ref[...]
        out_ref[:half] = jnp.where(swap, other, mine)
        out_ref[half:] = jnp.where(swap, mine, other)


def word_kernel(place, head_ref, own_ref, mine_ref, other_ref, shift_ref, peak_ref, total_ref, own_logit_ref, far_logit_ref, scores_ref, far_ref, *, steps):
    join(place[1], mine_ref, other_ref, far_ref)
    group, picks, _ = head_ref.shape
    width = own_ref.shape[1]
    rows = group * picks
    head = head_ref[:, :, 0:width].reshape(rows, width)
    peak = jnp.full((rows, 1), -jnp.inf, F32)
    cuts = word_cuts(own_ref.shape[0])
    for table, part, columns in cuts:
        scores = back_mul(head, (own_ref, far_ref)[table][part]) + shift_ref[0:1, columns]
        scores_ref[:, columns] = scores
        peak = jnp.maximum(peak, jnp.max(scores, axis=1, keepdims=True))
    total = jnp.zeros_like(peak)
    for _, _, columns in cuts:
        total = total + jnp.sum(jnp.exp(scores_ref[:, columns] - peak), axis=1, keepdims=True)
    for g in range(group):
        part = slice(g * picks, (g + 1) * picks)
        peak_ref[g] = as_row(peak[part])
        total_ref[g] = as_row(total[part])

    @pl.when(pl.program_id(0) < steps)
    def _():
        for g in range(group):
            part = slice(g * picks, (g + 1) * picks)
            spot = jnp.bitwise_xor(lax.rem(place[0], group), g)
            own_logit_ref[spot] = scores_ref[part, : own_ref.shape[0]].astype(BF16)
            far_logit_ref[spot] = scores_ref[part, own_ref.shape[0] :].astype(BF16)


def word_scores(place, head, own, mine, other, shift, group=4):
    near, picks, padded = head.shape
    vocab = shift.shape[1]
    quarter = near // 2
    steps = quarter // group
    row = pl.BlockSpec((group, 1, picks), lambda k, _: (k, 0, 0))
    row_shape = jax.ShapeDtypeStruct((near, 1, picks), F32)
    spot = lambda k, p: (jnp.bitwise_xor(lax.rem(p[0], quarter) // group, jnp.minimum(k, steps - 1)), 0, 0)
    return pl.pallas_call(
        functools.partial(word_kernel, steps=steps),
        grid_spec=pltpu.PrefetchScalarGridSpec(
            num_scalar_prefetch=1,
            grid=(near // group,),
            in_specs=[pl.BlockSpec((group, picks, padded), lambda k, _: (k, 0, 0))]
            + [whole(array) for array in (own, mine, other, shift)],
            out_specs=[row, row] + [pl.BlockSpec((group, picks, vocab // 2), spot)] * 2,
            scratch_shapes=[pltpu.VMEM((group * picks, vocab), F32), pltpu.VMEM(own.shape, BF16)],
        ),
        out_shape=[row_shape] * 2 + [jax.ShapeDtypeStruct((quarter, picks, vocab // 2), BF16)] * 2,
        compiler_params=pltpu.CompilerParams(vmem_limit_bytes=VMEM),
        name="word_scores",
    )(place, head, own, mine, other, shift)


def side_kernel(place, head_ref, own_mine, own_other, far_mine, far_other, shift_ref, logit_ref, own_ref, far_ref):
    join(place[1], own_mine, own_other, own_ref)
    join(place[1], far_mine, far_other, far_ref)
    group, picks, _ = head_ref.shape
    width = own_ref.shape[1]
    head = head_ref[:, :, 0:width].reshape(group * picks, width)
    for table, part, columns in word_cuts(own_ref.shape[0]):
        scores = back_mul(head, (own_ref, far_ref)[table][part]) + shift_ref[0:1, columns]
        scores = scores.astype(BF16)
        for g in range(group):
            spot = jnp.bitwise_xor(lax.rem(place[0], group), g)
            logit_ref[spot, :, columns] = scores[g * picks : (g + 1) * picks]


def side_scores(place, head, own, far, shift, group=4):
    tables = own + far
    near, picks, padded = head.shape
    vocab = shift.shape[1]
    quarter = near // 2
    spot = lambda k, p: (jnp.bitwise_xor(lax.rem(p[0], quarter) // group, k), 0, 0)
    return pl.pallas_call(
        side_kernel,
        grid_spec=pltpu.PrefetchScalarGridSpec(
            num_scalar_prefetch=1,
            grid=(quarter // group,),
            in_specs=[pl.BlockSpec((group, picks, padded), lambda k, _: (k, 0, 0))]
            + [whole(array) for array in tables + (shift,)],
            out_specs=pl.BlockSpec((group, picks, vocab), spot),
            scratch_shapes=[pltpu.VMEM((vocab // 2, own[0].shape[1]), BF16)] * 2,
        ),
        out_shape=jax.ShapeDtypeStruct((quarter, picks, vocab), BF16),
        compiler_params=pltpu.CompilerParams(vmem_limit_bytes=VMEM),
        name="side_scores",
    )(place, head, *tables, shift)


def word_back_kernel(first, head_ref, log_ref, own_ref, mine_ref, other_ref, shift_ref, grad_ref, out_ref, sums_ref, hit_ref, far_ref, *, masked):
    join(first[2], mine_ref, other_ref, far_ref)

    @pl.when(pl.program_id(0) == 0)
    def _():
        sums_ref[...] = jnp.zeros_like(sums_ref)

    group, picks, width = out_ref.shape
    rows = group * picks
    label = head_ref[:, :, width:].reshape(rows, -1).astype(F32)
    label = (label[:, 0:1] * 256.0 + label[:, 1:2]).astype(jnp.int32)
    logs = jnp.concatenate([as_column(log_ref[g]) for g in range(group)])
    head = head_ref[:, :, 0:width].reshape(rows, width)
    total = jnp.zeros((rows, width), F32)
    hit = jnp.zeros((rows, 1), F32)
    for table, part, columns in word_cuts(own_ref.shape[0]):
        words = (own_ref, far_ref)[table][part]
        scores = back_mul(head, words) + shift_ref[0:1, columns]
        share = jnp.exp(scores - logs)
        mine = lax.broadcasted_iota(jnp.int32, share.shape, 1) == label - (first[table] + part.start)
        hit = hit + jnp.sum(jnp.where(mine, scores, 0.0), axis=1, keepdims=True)
        grad = (jnp.where(mine, share - 1.0, share) * (1.0 / masked)).astype(BF16)
        grad_ref[:, :, columns] = grad.reshape(group, picks, -1)
        sums_ref[0:1, columns] += jnp.sum(grad.astype(F32), axis=0, keepdims=True)
        total = total + matmul(grad, words)
    out_ref[...] = total.astype(BF16).reshape(group, picks, width)
    for g in range(group):
        hit_ref[g] = as_row(hit[g * picks : (g + 1) * picks])


def word_back(first, head, logs, own, mine, other, shift, masked, group=4):
    near, picks, padded = head.shape
    width = own.shape[1]
    vocab = shift.shape[1]
    block = lambda n: pl.BlockSpec((group, picks, n), lambda k, _: (k, 0, 0))
    row = pl.BlockSpec((group, 1, picks), lambda k, _: (k, 0, 0))
    return pl.pallas_call(
        functools.partial(word_back_kernel, masked=masked),
        grid_spec=pltpu.PrefetchScalarGridSpec(
            num_scalar_prefetch=1,
            grid=(near // group,),
            in_specs=[block(padded), row] + [whole(array) for array in (own, mine, other, shift)],
            out_specs=[block(vocab), block(width), pl.BlockSpec((1, vocab), lambda k, _: (0, 0)), row],
            scratch_shapes=[pltpu.VMEM(own.shape, BF16)],
        ),
        out_shape=[
            jax.ShapeDtypeStruct((near, picks, vocab), BF16),
            jax.ShapeDtypeStruct((near, picks, width), BF16),
            jax.ShapeDtypeStruct((1, vocab), F32),
            jax.ShapeDtypeStruct((near, 1, picks), F32),
        ],
        compiler_params=pltpu.CompilerParams(vmem_limit_bytes=VMEM),
        name="word_back",
    )(first, head, logs, own, mine, other, shift)


def assemble_kernel(place, own_ref, far_ref, side_ref, side_far_ref, out_ref, *, quarter):
    for i, ref in enumerate((own_ref, side_ref, far_ref, side_far_ref)):

        @pl.when(jnp.bitwise_xor(place[0] // quarter, pl.program_id(0)) == i)
        def _():
            out_ref[...] = ref[0]


def assembled(place, own, far, side):
    quarter, picks, slice_rows = own.shape
    if slice_rows % LANES:
        parts = jnp.stack([own, side[:, :, :slice_rows], far, side[:, :, slice_rows:]])
        parts = jnp.take(parts, jnp.bitwise_xor(jnp.arange(4), place // quarter), axis=0)
        return parts.transpose(2, 0, 1, 3).reshape(picks, 4 * quarter * slice_rows)

    def spec(flip, column):
        def index(b, j, p):
            turn = jnp.bitwise_xor(p[0] // quarter, flip)
            return jnp.where(b == turn, j, jnp.where(b < turn, 0, quarter - 1)), 0, column

        return pl.BlockSpec((1, picks, slice_rows), index)

    return pl.pallas_call(
        functools.partial(assemble_kernel, quarter=quarter),
        grid_spec=pltpu.PrefetchScalarGridSpec(
            num_scalar_prefetch=1,
            grid=(4, quarter),
            in_specs=[spec(0, 0), spec(2, 0), spec(1, 0), spec(3, 1)],
            out_specs=pl.BlockSpec((picks, slice_rows), lambda b, j, _: (0, b * quarter + j)),
        ),
        out_shape=jax.ShapeDtypeStruct((picks, 4 * quarter * slice_rows), BF16),
        compiler_params=pltpu.CompilerParams(vmem_limit_bytes=VMEM),
        name="assemble",
    )(place.reshape(1), own, far, side, side)


def on_device(
    embedded,
    lengths,
    positions,
    labels,
    joint_weight,
    mixer_weight,
    expand_weight,
    contract_weight,
    head_weight,
    gains,
    biases,
    expand_bias,
    word_table,
    word_bias,
):
    section = lax.axis_index("section")
    place = lax.axis_index("dp")
    groups = lax.axis_size("dp")
    decoder = section == 1
    count, rows, width = embedded.shape[1:]
    total_rows = count * rows
    head_dim = width // HEADS
    masked = positions.shape[-1]
    picks = count * masked
    joint = joint_weight[0]
    mats = (mixer_weight[0], expand_weight[0], contract_weight[0])
    head_matrix = head_weight[0]
    gain = gains[0]
    bias = biases[0]
    shift = expand_bias
    slice_rows = word_table.shape[0]

    flag = section.astype(jnp.int32).reshape(1)
    place32 = place.astype(jnp.int32)
    units = shift.shape[1]
    own = width // groups
    near, quarter = groups // 2, groups // 4
    half = slice_rows // 2
    bits = bits_of(groups)
    order = bits[1:]
    joint_order = bits[-2:-1] + bits[1:-2] + bits[-1:]
    across = lambda array: lax.ppermute(array, "section", [(0, 1), (1, 0)])
    pick_half = lambda array, which: lax.dynamic_slice_in_dim(array, which * half, half)

    def joined(mine, other):
        return jnp.where(decoder, jnp.concatenate([other, mine]), jnp.concatenate([mine, other]))

    my_half = pick_half(word_table, section)
    far_mine = swapped(my_half, near)
    side_half = swapped(my_half, quarter)

    x = embedded[0].reshape(total_rows, width)
    joint_shift = jnp.concatenate([bias[0], jnp.zeros((width,), F32), bias[1]])[None]
    qkv = project(x, joint, joint_shift)
    cls_out = cls_forward(x, qkv, lengths, mats, gain, bias, shift)
    cls_in = passed_along(cls_out, "section", 1)
    x, qkv = place_first(flag, cls_in, x, qkv, joint, joint_shift, count)
    ctx, logs = attend(qkv, lengths, count)
    ctx, side_half = tied(ctx, side_half)
    far_shift = swapped(word_bias, near)
    side_shift = swapped(word_bias, quarter)
    y, normed_one, scale_one, first_low, active, slope, normed_two, scale_two = layer_tail(
        ctx, x, mats, gain, bias, shift
    )
    y, far_mine, far_shift, side_shift = tied(y, far_mine, far_shift, side_shift)
    far_other = across(far_mine)
    side_far_shift = swapped(far_shift, quarter)

    chosen = positions[0][:, :, None] == jnp.arange(rows)[None, None, :]
    picked = jnp.einsum(
        "bml,blw->bmw", chosen.astype(BF16), y.reshape(count, rows, width), preferred_element_type=F32
    )
    picked_low = picked.astype(BF16).reshape(picks, width)
    dense = matmul(picked_low, head_matrix) + bias[6]
    dense_active, dense_slope = gelu_and_slope(dense)
    normed_head, scale_head = normalise(dense_active)
    head_low = (normed_head * gain[2] + bias[7]).astype(BF16)
    answers = labels[0].reshape(-1, 1)
    answers = jnp.concatenate([answers // 256, answers % 256, jnp.zeros((picks, LANES - 2), jnp.int32)], axis=1)
    head_all = gather_near(jnp.concatenate([head_low, answers.astype(BF16)], axis=1))
    head_all, far_other, side_far_shift, side_half = tied(head_all, far_other, side_far_shift, side_half)
    side_half_other = across(side_half)
    word_shift = jnp.concatenate([word_bias, far_shift]).astype(F32)[None]
    side_word_shift = jnp.concatenate([side_shift, side_far_shift]).astype(F32)[None]
    where_to = jnp.stack([place32, section.astype(jnp.int32)])
    peak, total, *logits = word_scores(where_to, head_all, word_table, far_mine, far_other, word_shift)
    grid = (2,) * (len(bits) - 1)
    peak, total = (array.reshape(grid + (picks,)) for array in (peak, total))
    for axis, bit in enumerate(reversed(bits[:-1])):
        other_peak, other_total = jnp.flip(swapped(jnp.stack([peak, total]), bit), axis + 1)
        top = jnp.maximum(peak, other_peak)
        total = total * jnp.exp(peak - top) + other_total * jnp.exp(other_peak - top)
        peak = top
    log_total = (peak + jnp.log(total)).reshape(near, 1, picks)
    log_total, far_mine, *logits = tied(log_total, far_mine, *logits)
    side_far_half = swapped(far_mine, quarter)
    exchanged = lambda part: lax.all_to_all(
        part, "dp", 0, 0, axis_index_groups=[list(range(i, i + quarter)) for i in range(0, groups, quarter)]
    )
    logits_own = exchanged(logits[0])
    first = (jnp.stack([place, jnp.bitwise_xor(place, near)]) * slice_rows).astype(jnp.int32)
    first = jnp.concatenate([first, flag])
    score_grad, head_back, word_sums, hits = word_back(
        first, head_all, log_total, word_table, far_mine, far_other, word_shift, masked
    )
    head_back, logits_own, side_half_other, side_far_half = tied(
        head_back, logits_own, side_half_other, side_far_half
    )
    side_far_other = across(side_far_half)
    loss_part = jnp.sum(log_total[0]) - jnp.sum(hits)
    head_grad = scatter_near(head_back)

    score_grad = score_grad.reshape(near * picks, 2 * slice_rows)
    head_rows = head_all[:, :, :width].reshape(near * picks, width)
    own_grad, far_grad = (
        outer_sum(score_grad[:, i * slice_rows : (i + 1) * slice_rows], head_rows).astype(BF16) for i in range(2)
    )
    head_grad, own_grad, far_grad, logits_far = tied(head_grad, own_grad, far_grad, logits[1])
    logits_far = exchanged(logits_far)
    far_got = across(pick_half(far_grad, 1 - section))

    gain_head = jnp.sum(head_grad * normed_head, 0)
    shift_head = jnp.sum(head_grad, 0)
    dense_grad = (norm_back(head_grad * gain[2], normed_head, scale_head) * dense_slope).astype(BF16)
    dense_shift = jnp.sum(dense_grad, axis=0, dtype=F32)
    picked_grad = back_mul(dense_grad, head_matrix).reshape(count, masked, width)
    grad = jnp.einsum(
        "bml,bmw->blw", chosen.astype(F32), picked_grad, precision=lax.Precision.HIGHEST
    ).reshape(total_rows, width)

    kept = (normed_two, scale_two, slope, normed_one, scale_one)
    branch, hidden, one, mixed, ctx_grad, sums, shift_sum = tail_back(grad, kept, mats, gain)
    hidden, branch, side_far_other, side_half_other, logits_far = tied(
        hidden, branch, side_far_other, side_half_other, logits_far
    )
    logits_side = side_scores(
        where_to, head_all, (side_half, side_half_other), (side_far_half, side_far_other), side_word_shift
    )
    branch, logits_side = tied(branch, logits_side)
    logits_side = exchanged(logits_side)
    one_pair = weight_grads(place32, (active, branch), (ctx, mixed))
    hidden, one_pair, far_got = tied(hidden, one_pair, far_got)
    one_state = first_hop(one_pair)
    far_half = (pick_half(far_grad, section).astype(F32) + far_got.astype(F32)).astype(BF16)
    far_quarters = [far_half[i * half // 4 : (i + 1) * half // 4] for i in range(4)]
    far_quarters[0] = swapped(far_quarters[0], near)
    two_pair = weight_grads(place32, (first_low, hidden), (picked_low, dense_grad))
    ctx_grad, two_pair = tied(ctx_grad, two_pair)
    two_state = first_hop(two_pair)
    halves = added(one_state, order[0])
    ctx_grad, halves_now, far_quarters[0], far_quarters[1] = tied(
        ctx_grad, halves[:2], far_quarters[0], far_quarters[1]
    )
    one_state = sent((*halves_now, halves[2]), order[0])
    far_quarters[1] = swapped(far_quarters[1], near)
    parts = attend_back(qkv, ctx_grad, logs, lengths, 0)
    halves = added(two_state, order[0])
    parts, halves_now, far_quarters[1], far_quarters[2] = tied(
        parts, halves[:2], far_quarters[1], far_quarters[2]
    )
    two_state = sent((*halves_now, halves[2]), order[0])
    far_quarters[2] = swapped(far_quarters[2], near)
    own_got = across(pick_half(own_grad, 1 - section))
    for passage in range(1, count):
        parts = attend_back(qkv, ctx_grad, logs, lengths, passage, (parts,))
    halves = added(one_state, order[1])
    parts, halves_now, logits_side, far_quarters[2], far_quarters[3] = tied(
        parts, halves[:2], logits_side, far_quarters[2], far_quarters[3]
    )
    one_state = sent((*halves_now, halves[2]), order[1])
    cls_grad = passed_along(cls_back(parts, one, joint, count), "section", -1)
    far_quarters[3] = swapped(far_quarters[3], near)

    branch_f, hidden_f, mixed_f, one_f, sums_f, shift_f, parts, part_sums = first_back(
        cls_grad, kept, mats, gain, qkv, parts, lengths
    )
    halves = added(two_state, order[1])
    parts, halves_now, far_quarters[3], own_got = tied(parts, halves[:2], far_quarters[3], own_got)
    two_state = sent((*halves_now, halves[2]), order[1])
    joint_pair = weight_grads(place32, (x, parts))
    parts, joint_pair = tied(parts, joint_pair)
    joint_state = first_hop(joint_pair)
    own_half = pick_half(own_grad, section).astype(F32) + own_got.astype(F32)
    own_half = (own_half + jnp.concatenate(far_quarters).astype(F32)).astype(BF16)
    table_total = joined(own_half, across(own_half)).astype(F32)
    word_total = word_sums[0, :slice_rows] + swapped(word_sums[0, slice_rows:], near)
    word_total = word_total + across(word_total)
    halves = added(one_state, order[2])
    parts, halves_now = tied(parts, halves[:2])
    one_state = sent((*halves_now, halves[2]), order[2])
    halves = added(joint_state, joint_order[0])
    parts, halves_now, *logits = tied(parts, halves[:2], logits_own, logits_far, logits_side)
    joint_state = sent((*halves_now, halves[2]), joint_order[0])
    input_grad = input_gradient(flag, parts, one, one_f, joint, count)
    joint_sum = unstacked(rest_of(joint_state, joint_order[1:]), [(own, 3 * width)])[0]
    contract_sum, mixer_sum = unstacked(rest_of(one_state, order[3:]), [(units // groups, width), (own, width)])
    expand_sum, head_sum = unstacked(rest_of(two_state, order[2:]), [(own, units), (own, width)])

    def firsts(array):
        return jnp.concatenate([array[b * rows : b * rows + 1] for b in range(count)])

    mine = jnp.concatenate(
        [firsts(active), firsts(first_low), firsts(ctx), branch_f[:count], hidden_f[:count], mixed_f[:count]],
        axis=1,
    )
    sums = sums + sums_f
    small = jnp.concatenate(
        [
            jnp.stack([sums[3], sums[0], gain_head]),
            jnp.stack(
                [part_sums[0], part_sums[2], sums[5], sums[4], sums[2], sums[1], dense_shift, shift_head]
            ),
            (shift_sum + shift_f).reshape(-1, width),
            jnp.broadcast_to(loss_part, (1, width)),
        ]
    )
    small_high = lax.reduce_precision(small, 8, 7)
    small_low = (small - small_high).astype(BF16)
    small_high = small_high.astype(BF16)
    mine = mine.reshape(-1, width)
    counts = [mine.shape[0], small.shape[0], small.shape[0]]
    rows_all = gather_all(jnp.concatenate([mine, small_high, small_low]))
    rows_all = rows_all.reshape(groups, -1, width)
    small = jnp.sum(rows_all[:, counts[0] :].astype(F32), axis=0)
    small = small[: counts[1]] + small[counts[1] :]
    rows_all = rows_all[:, : counts[0]].reshape(groups * count, -1)
    cuts = [units, width, width, width, units, width]
    starts = [sum(cuts[:i]) for i in range(len(cuts))]
    active_a, first_a, ctx_a, branch_a, hidden_a, mixed_a = (
        rows_all[:, s : s + n] for s, n in zip(starts, cuts)
    )

    def own_columns(array):
        size = array.shape[1] // groups
        return lax.dynamic_slice_in_dim(array, place * size, size, 1)

    contract_sum = contract_sum + outer_sum(own_columns(active_a), branch_a)
    expand_sum = expand_sum + outer_sum(own_columns(first_a), hidden_a)
    mixer_sum = mixer_sum + outer_sum(own_columns(ctx_a), mixed_a)

    logits_out = assembled(place32, *logits)
    loss = (small[-1, 0] / (picks * groups)).reshape(1)
    return (
        loss,
        logits_out.reshape(1, count, masked, -1),
        input_grad.reshape(1, count, rows, width),
        joint_sum[None],
        mixer_sum[None],
        expand_sum[None],
        contract_sum[None],
        head_sum[None],
        small[None, :3],
        small[None, 3:11],
        small[11:-1].reshape(1, -1),
        table_total,
        word_total,
    )


def solution(mesh):
    in_specs = (
        P("section", "dp", None, None),
        P("dp"),
        P("section", "dp", None),
        P("section", "dp", None),
        P("section", None, None),
        P("section", None, None),
        P("section", None, None),
        P("section", None, None),
        P("section", None, None),
        P("section", None, None),
        P("section", None, None),
        P("section", None),
        P("dp", None),
        P("dp"),
    )
    out_specs = (
        P("section"),
        P("section", "dp", None, None),
        P("section", "dp", None, None),
        P("section", "dp", None),
        P("section", "dp", None),
        P("section", "dp", None),
        P("section", "dp", None),
        P("section", "dp", None),
        P("section", None, None),
        P("section", None, None),
        P("section", None),
        P("dp", None),
        P("dp"),
    )
    return jax.shard_map(
        on_device, mesh=mesh, in_specs=in_specs, out_specs=out_specs, check_vma=False
    )
```

```python
import functools

import jax
import jax.numpy as jnp
from jax import lax
from jax.experimental import pallas as pl
from jax.experimental.pallas import tpu as pltpu
from jax.sharding import PartitionSpec as P

HEADS = 12
EPS = 1e-12
ROOT_HALF = 0.7071067811865476
INV_ROOT_TAU = 0.3989422804014327
HIDDEN = -1000000000.0
LANES = 128
MIB = 1024 * 1024
F32 = jnp.float32
BF16 = jnp.bfloat16


def product(left, right, left_dim, right_dim):
    return lax.dot_general(
        left, right, (((left_dim,), (right_dim,)), ((), ())), preferred_element_type=F32
    )


def matmul(left, right):
    return product(left, right, 1, 0)


def outer_sum(left, right):
    return product(left, right, 0, 0)


def back_mul(left, right):
    return product(left, right, 1, 1)


def passed_along(block, axis, distance):
    devices = range(lax.axis_size(axis))
    route = [(i - distance, i) for i in devices if i - distance in devices]
    return lax.ppermute(block, axis, route)


def swapped(block, bit):
    devices = range(lax.axis_size("dp"))
    return lax.ppermute(block, "dp", [(i, i ^ bit) for i in devices])


def bits_of(order):
    return [1 << i for i in range(order.bit_length() - 1)]


def tied(*values):
    return lax.optimization_barrier(values)


def side_by_side(blocks, other, bit):
    low = (lax.axis_index("dp") & bit) == 0
    pair = [jnp.where(low, blocks, other), jnp.where(low, other, blocks)]
    return jnp.stack(pair, axis=1).reshape((-1,) + blocks.shape[1:])


def gather_chips(block):
    return [block] + [swapped(block, mask) for mask in range(2, lax.axis_size("dp") // 2, 2)]


def gather_cores(blocks):
    blocks = jnp.stack(blocks)
    return jnp.stack([blocks, swapped(blocks, 1)], axis=1).reshape((-1,) + blocks.shape[1:])


def scatter_near(blocks):
    blocks = blocks.reshape((-1, 2) + blocks.shape[1:])
    got = swapped(blocks[:, 1], 1)
    blocks = (blocks[:, 0].astype(F32) + got.astype(F32)).astype(BF16)
    total = blocks[0].astype(F32)
    for i in range(1, blocks.shape[0]):
        total = total + swapped(blocks[i], 2 * i).astype(F32)
    return total


def normalise(resid):
    centre = resid - jnp.mean(resid, axis=-1, keepdims=True)
    scale_inv = lax.rsqrt(jnp.mean(centre * centre, axis=-1, keepdims=True) + EPS)
    return centre * scale_inv, scale_inv


def norm_back(scaled, normed, scale_inv):
    first_mean = jnp.mean(scaled, axis=-1, keepdims=True)
    second_mean = jnp.mean(scaled * normed, axis=-1, keepdims=True)
    return scale_inv * (scaled - first_mean - normed * second_mean)


def gelu_and_slope(value):
    gate = 0.5 * (1.0 + lax.erf(value * ROOT_HALF))
    return value * gate, gate + value * jnp.exp(-0.5 * value * value) * INV_ROOT_TAU


def attend_kernel(lengths, q_ref, k_ref, v_ref, out_ref, log_ref, *, head_dim):
    length = lengths[pl.program_id(0)]
    rows, lanes = q_ref.shape
    q = q_ref[...] * (head_dim**-0.5)
    k = k_ref[...]
    v_t = v_ref[...].T
    head_of = lax.broadcasted_iota(jnp.int32, (rows, lanes), 1) // head_dim
    visible = lax.broadcasted_iota(jnp.int32, (rows, rows), 0) < length
    parts = []
    for head in range(lanes // head_dim):
        scores = back_mul(k, jnp.where(head_of == head, q, jnp.zeros_like(q)))
        scores = jnp.where(visible, scores, HIDDEN)
        peak = jnp.max(scores, axis=0, keepdims=True)
        powers = jnp.exp(scores - peak)
        total = jnp.sum(powers, axis=0, keepdims=True)
        piece = matmul(v_t[head * head_dim : (head + 1) * head_dim], powers.astype(BF16))
        parts.append(piece / total)
        log_ref[0, head : head + 1, :] = peak + jnp.log(total)
    out_ref[...] = jnp.concatenate(parts, axis=0).T.astype(BF16)


def attend(qkv, lengths, count):
    rows = qkv.shape[0] // count
    width = qkv.shape[1] // 3
    pairs = width // LANES
    head_dim = width // HEADS
    block = lambda part: pl.BlockSpec((rows, LANES), lambda b, p, _: (b, part * pairs + p))
    return pl.pallas_call(
        functools.partial(attend_kernel, head_dim=head_dim),
        grid_spec=pltpu.PrefetchScalarGridSpec(
            num_scalar_prefetch=1,
            grid=(count, pairs),
            in_specs=[block(0), block(1), block(2)],
            out_specs=[
                pl.BlockSpec((rows, LANES), lambda b, p, _: (b, p)),
                pl.BlockSpec((1, LANES // head_dim, rows), lambda b, p, _: (b * pairs + p, 0, 0)),
            ],
        ),
        out_shape=[
            jax.ShapeDtypeStruct((count * rows, width), BF16),
            jax.ShapeDtypeStruct((count * pairs, LANES // head_dim, rows), F32),
        ],
        compiler_params=pltpu.CompilerParams(vmem_limit_bytes=48 * MIB),
        name="attend",
    )(lengths, qkv, qkv, qkv)


def attend_back_kernel(lengths, q_ref, k_ref, v_ref, grad_ref, log_ref, out_ref, *, head_dim):
    length = lengths[pl.program_id(0)]
    rows, lanes = q_ref.shape
    scale = head_dim**-0.5
    q = q_ref[...] * scale
    k = k_ref[...]
    v = v_ref[...]
    grad = grad_ref[...]
    head_of = lax.broadcasted_iota(jnp.int32, (rows, lanes), 1) // head_dim
    visible = lax.broadcasted_iota(jnp.int32, (rows, rows), 0) < length
    totals = [jnp.zeros((rows, lanes), F32)] * 3
    for head in range(lanes // head_dim):
        mine = head_of == head
        scores = back_mul(k, jnp.where(mine, q, jnp.zeros_like(q)))
        share = jnp.where(visible, jnp.exp(scores - log_ref[0, head : head + 1, :]), 0.0)
        share_grad = back_mul(jnp.where(mine, v, jnp.zeros_like(v)), grad)
        inner = jnp.sum(share * share_grad, axis=0, keepdims=True)
        score_grad = (share * (share_grad - inner)).astype(BF16)
        parts = (
            outer_sum(score_grad, k) * scale,
            matmul(score_grad, q),
            matmul(share.astype(BF16), grad),
        )
        totals = [jnp.where(mine, part, total) for part, total in zip(parts, totals)]
    for i, total in enumerate(totals):
        out_ref[i] = total.astype(BF16)


def attend_back(qkv, grad, logs, lengths):
    count = lengths.shape[0]
    rows = qkv.shape[0] // count
    width = qkv.shape[1] // 3
    pairs = width // LANES
    head_dim = width // HEADS
    block = lambda part: pl.BlockSpec((rows, LANES), lambda b, p, _: (b, part * pairs + p))
    return pl.pallas_call(
        functools.partial(attend_back_kernel, head_dim=head_dim),
        grid_spec=pltpu.PrefetchScalarGridSpec(
            num_scalar_prefetch=1,
            grid=(count, pairs),
            in_specs=[
                block(0),
                block(1),
                block(2),
                block(0),
                pl.BlockSpec((1, LANES // head_dim, rows), lambda b, p, _: (b * pairs + p, 0, 0)),
            ],
            out_specs=pl.BlockSpec((3, rows, LANES), lambda b, p, _: (0, b, p)),
        ),
        out_shape=jax.ShapeDtypeStruct((3, count * rows, width), BF16),
        compiler_params=pltpu.CompilerParams(vmem_limit_bytes=48 * MIB),
        name="attend_back",
    )(lengths, qkv, qkv, qkv, grad, logs)


def tail_kernel(
    ctx_ref, x_ref, mixer_ref, expand_ref, contract_ref, gain_ref, bias_ref, shift_ref,
    y_ref, normed_one_ref, scale_one_ref, first_ref, active_ref, slope_ref, normed_two_ref, scale_two_ref,
    *, chunk,
):
    mixed = matmul(ctx_ref[...], mixer_ref[...]) + bias_ref[2:3]
    normed, scale = normalise(x_ref[...].astype(F32) + mixed)
    first = normed * gain_ref[0:1] + bias_ref[3:4]
    first_low = first.astype(BF16)
    normed_one_ref[...] = normed.astype(BF16)
    scale_one_ref[...] = jnp.broadcast_to(scale, scale_one_ref.shape)
    first_ref[...] = first_low
    total = first + bias_ref[4:5]
    for start in range(0, expand_ref.shape[1], chunk):
        part = slice(start, start + chunk)
        hidden = matmul(first_low, expand_ref[:, part]) + shift_ref[0:1, part]
        active, slope = gelu_and_slope(hidden)
        active = active.astype(BF16)
        active_ref[:, part] = active
        slope_ref[:, part] = slope.astype(BF16)
        total = total + matmul(active, contract_ref[part, :])
    normed, scale = normalise(total)
    normed_two_ref[...] = normed.astype(BF16)
    scale_two_ref[...] = jnp.broadcast_to(scale, scale_two_ref.shape)
    y_ref[...] = (normed * gain_ref[1:2] + bias_ref[5:6]).astype(BF16)


def whole(array):
    return pl.BlockSpec(array.shape, lambda *_: (0,) * array.ndim, pipeline_mode=pl.Buffered(1))


def layer_tail(ctx, x, mats, gain, bias, shift, step=256, chunk=3072):
    rows, width = x.shape
    hidden = shift.shape[1]
    step = min(step, rows)
    by_row = lambda n: pl.BlockSpec((step, n), lambda i: (i, 0))
    shape = lambda n, kind: jax.ShapeDtypeStruct((rows, n), kind)
    widths = [(width, BF16), (width, BF16), (LANES, F32), (width, BF16), (hidden, BF16), (hidden, BF16), (width, BF16), (LANES, F32)]
    return pl.pallas_call(
        functools.partial(tail_kernel, chunk=min(chunk, hidden)),
        grid=(rows // step,),
        in_specs=[by_row(width), by_row(width)] + [whole(m) for m in mats + (gain, bias, shift)],
        out_specs=[by_row(n) for n, _ in widths],
        out_shape=[shape(n, kind) for n, kind in widths],
        compiler_params=pltpu.CompilerParams(vmem_limit_bytes=48 * MIB),
        name="layer_tail",
    )(ctx, x, *mats, gain, bias, shift)


def tail_back_kernel(
    grad_ref, normed_two_ref, scale_two_ref, slope_ref, normed_one_ref, scale_one_ref,
    mixer_ref, expand_ref, contract_ref, gain_ref,
    branch_ref, hidden_ref, one_ref, mixed_ref, ctx_ref, sums_ref, shift_sum_ref,
    *, chunk,
):
    @pl.when(pl.program_id(0) == 0)
    def _():
        sums_ref[...] = jnp.zeros_like(sums_ref)
        shift_sum_ref[...] = jnp.zeros_like(shift_sum_ref)

    def add_sum(row, value):
        sums_ref[row : row + 1] += jnp.sum(value, axis=0, keepdims=True)

    grad = grad_ref[...]
    normed = normed_two_ref[...].astype(F32)
    add_sum(0, grad * normed)
    add_sum(1, grad)
    total = norm_back(grad * gain_ref[1:2], normed, scale_two_ref[:, 0:1])
    branch = total.astype(BF16)
    branch_ref[...] = branch
    add_sum(2, branch.astype(F32))
    for start in range(0, expand_ref.shape[1], chunk):
        part = slice(start, start + chunk)
        hidden = back_mul(branch, contract_ref[part, :]) * slope_ref[:, part].astype(F32)
        hidden = hidden.astype(BF16)
        hidden_ref[:, part] = hidden
        shift_sum_ref[0:1, part] += jnp.sum(hidden.astype(F32), axis=0, keepdims=True)
        total = total + back_mul(hidden, expand_ref[:, part])
    normed = normed_one_ref[...].astype(F32)
    add_sum(3, total * normed)
    add_sum(4, total)
    total = norm_back(total * gain_ref[0:1], normed, scale_one_ref[:, 0:1])
    one_ref[...] = total
    mixed = total.astype(BF16)
    mixed_ref[...] = mixed
    add_sum(5, mixed.astype(F32))
    ctx_ref[...] = back_mul(mixed, mixer_ref[...]).astype(BF16)


def tail_back(grad, kept, mats, gain, step=256, chunk=3072):
    rows, width = grad.shape
    hidden = mats[1].shape[1]
    step = min(step, rows)
    by_row = lambda n: pl.BlockSpec((step, n), lambda i: (i, 0))
    shape = lambda n, kind: jax.ShapeDtypeStruct((rows, n), kind)
    widths = [(width, BF16), (hidden, BF16), (width, F32), (width, BF16), (width, BF16)]
    return pl.pallas_call(
        functools.partial(tail_back_kernel, chunk=min(chunk, hidden)),
        grid=(rows // step,),
        in_specs=[by_row(array.shape[1]) for array in (grad,) + kept] + [whole(m) for m in mats + (gain,)],
        out_specs=[by_row(n) for n, _ in widths]
        + [pl.BlockSpec((8, width), lambda i: (0, 0)), pl.BlockSpec((1, hidden), lambda i: (0, 0))],
        out_shape=[shape(n, kind) for n, kind in widths]
        + [jax.ShapeDtypeStruct((8, width), F32), jax.ShapeDtypeStruct((1, hidden), F32)],
        compiler_params=pltpu.CompilerParams(vmem_limit_bytes=48 * MIB),
        name="tail_back",
    )(grad, *kept, *mats, gain)


PACK = 16


def first_block(rows, width, passage):
    return pl.BlockSpec((PACK, width), lambda *_: (passage * rows // PACK, 0))


def packed(refs):
    rows = [ref[...].astype(F32)[0:1] for ref in refs]
    place = lax.broadcasted_iota(jnp.int32, (PACK, rows[0].shape[1]), 0)
    total = jnp.zeros((PACK, rows[0].shape[1]), F32)
    for i, row in enumerate(rows):
        total = jnp.where(place == i, row, total)
    return total


def per_head(row, head_dim):
    shape = (PACK, row.shape[1])
    mine = lax.broadcasted_iota(jnp.int32, shape, 1) // head_dim == lax.broadcasted_iota(jnp.int32, shape, 0)
    return jnp.where(mine, row, 0.0)


def heads_joined(block, head_dim):
    mine = lax.broadcasted_iota(jnp.int32, block.shape, 1) // head_dim == lax.broadcasted_iota(jnp.int32, block.shape, 0)
    return jnp.sum(jnp.where(mine, block, 0.0), axis=0, keepdims=True)


def first_share(query, keys, length):
    scores = back_mul(query, keys)
    visible = lax.broadcasted_iota(jnp.int32, scores.shape, 1) < length
    scores = jnp.where(visible, scores, HIDDEN)
    powers = jnp.exp(scores - jnp.max(scores, axis=1, keepdims=True))
    return powers / jnp.sum(powers, axis=1, keepdims=True)


def cls_kernel(lengths, *refs, count, rows, head_dim, chunk):
    x_refs, (qkv_ref, mixer_ref, expand_ref, contract_ref, gain_ref, bias_ref, shift_ref, out_ref) = (
        refs[:count],
        refs[count:],
    )
    width = out_ref.shape[1]
    x = packed(x_refs)
    place = lax.broadcasted_iota(jnp.int32, (PACK, width), 0)
    ctx = jnp.zeros((PACK, width), F32)
    for b in range(count):
        base = b * rows
        query = qkv_ref[base : base + PACK, 0:width].astype(F32)[0:1] * head_dim**-0.5
        query = per_head(query, head_dim).astype(BF16)
        share = first_share(query, qkv_ref[base : base + rows, width : 2 * width], lengths[b])
        mixed = matmul(share.astype(BF16), qkv_ref[base : base + rows, 2 * width : 3 * width])
        ctx = jnp.where(place == b, heads_joined(mixed, head_dim), ctx)
    mixed = matmul(ctx.astype(BF16), mixer_ref[...]) + bias_ref[2:3]
    first = normalise(x + mixed)[0] * gain_ref[0:1] + bias_ref[3:4]
    first_low = first.astype(BF16)
    total = first + bias_ref[4:5]
    for start in range(0, expand_ref.shape[1], chunk):
        part = slice(start, start + chunk)
        active, _ = gelu_and_slope(matmul(first_low, expand_ref[:, part]) + shift_ref[0:1, part])
        total = total + matmul(active.astype(BF16), contract_ref[part, :])
    out_ref[...] = (normalise(total)[0] * gain_ref[1:2] + bias_ref[5:6]).astype(BF16)


def cls_forward(x, qkv, lengths, mats, gain, bias, shift):
    count = lengths.shape[0]
    rows, width = x.shape[0] // count, x.shape[1]
    rest = (qkv,) + mats + (gain, bias, shift)
    return pl.pallas_call(
        functools.partial(cls_kernel, count=count, rows=rows, head_dim=width // HEADS, chunk=768),
        grid_spec=pltpu.PrefetchScalarGridSpec(
            num_scalar_prefetch=1,
            grid=(1,),
            in_specs=[first_block(rows, width, b) for b in range(count)] + [whole(r) for r in rest],
            out_specs=pl.BlockSpec((PACK, width), lambda *_: (0, 0)),
        ),
        out_shape=jax.ShapeDtypeStruct((PACK, width), BF16),
        compiler_params=pltpu.CompilerParams(vmem_limit_bytes=26 * MIB),
        name="cls_forward",
    )(lengths, *[x] * count, *rest)


def place_kernel(decoder, cls_ref, x_ref, qkv_ref, joint_ref, shift_ref, x_out, qkv_out, new_ref):
    step = pl.program_id(0)

    @pl.when(step == 0)
    def _():
        new_ref[...] = (matmul(cls_ref[...], joint_ref[...]) + shift_ref[...]).astype(BF16).astype(F32)

    def put(old, new, out):
        spot = lax.broadcasted_iota(jnp.int32, new.shape, 0)
        row = jnp.sum(jnp.where(spot == step, new, 0.0), axis=0, keepdims=True)
        here = (spot == 0) & (decoder[0] == 1)
        out[...] = jnp.where(here, row, old.astype(F32)).astype(BF16)

    put(x_ref[...], cls_ref[...].astype(F32), x_out)
    put(qkv_ref[...], new_ref[...], qkv_out)


def place_first(decoder, cls, x, qkv, joint, shift, count):
    rows, width = x.shape[0] // count, x.shape[1]
    block = lambda n: pl.BlockSpec((PACK, n), lambda b, _: (b * rows // PACK, 0))
    return pl.pallas_call(
        place_kernel,
        grid_spec=pltpu.PrefetchScalarGridSpec(
            num_scalar_prefetch=1,
            grid=(count,),
            in_specs=[whole(cls), block(width), block(3 * width), whole(joint), whole(shift)],
            out_specs=[block(width), block(3 * width)],
            scratch_shapes=[pltpu.VMEM((PACK, 3 * width), F32)],
        ),
        out_shape=[jax.ShapeDtypeStruct(x.shape, BF16), jax.ShapeDtypeStruct(qkv.shape, BF16)],
        input_output_aliases={2: 0, 3: 1},
        compiler_params=pltpu.CompilerParams(vmem_limit_bytes=8 * MIB),
        name="place_first",
    )(decoder, cls, x, qkv, joint, shift)


def cls_grad_kernel(*refs, count):
    part_refs, one_refs, (joint_ref, out_ref) = refs[:count], refs[count : 2 * count], refs[2 * count :]
    width = out_ref.shape[1]
    total = packed(one_refs)
    for i in range(3):
        grad = packed([ref.at[i] for ref in part_refs]).astype(BF16)
        total = total + back_mul(grad, joint_ref[:, i * width : (i + 1) * width])
    out_ref[...] = total.astype(BF16)


def cls_back(parts, one, joint, count):
    rows, width = one.shape[0] // count, one.shape[1]
    part = lambda b: pl.BlockSpec((3, PACK, width), lambda *_: (0, b * rows // PACK, 0))
    return pl.pallas_call(
        functools.partial(cls_grad_kernel, count=count),
        grid=(1,),
        in_specs=[part(b) for b in range(count)]
        + [first_block(rows, width, b) for b in range(count)]
        + [whole(joint)],
        out_specs=pl.BlockSpec((PACK, width), lambda *_: (0, 0)),
        out_shape=jax.ShapeDtypeStruct((PACK, width), BF16),
        compiler_params=pltpu.CompilerParams(vmem_limit_bytes=48 * MIB),
        name="cls_back",
    )(*[parts] * count, *[one] * count, joint)


def first_back_kernel(lengths, grad_ref, *refs, count, rows, head_dim, chunk):
    kept = [packed(refs[i * count : (i + 1) * count]) for i in range(5)]
    normed_two, scale_two, slope, normed_one, scale_one = kept
    scale_two, scale_one = scale_two[:, 0:1], scale_one[:, 0:1]
    mixer_ref, expand_ref, contract_ref, gain_ref, qkv_ref, parts_ref = refs[5 * count : 5 * count + 6]
    branch_ref, hidden_ref, mixed_ref, one_ref, sums_ref, shift_sum_ref, out_ref, part_sums_ref = refs[5 * count + 6 :]
    width = grad_ref.shape[1]
    grad = grad_ref[...].astype(F32)
    sums_ref[...] = jnp.zeros_like(sums_ref)

    def add_sum(row, value):
        sums_ref[row : row + 1] = jnp.sum(value, axis=0, keepdims=True)

    add_sum(0, grad * normed_two)
    add_sum(1, grad)
    total = norm_back(grad * gain_ref[1:2], normed_two, scale_two)
    branch = total.astype(BF16)
    branch_ref[...] = branch
    add_sum(2, branch.astype(F32))
    for start in range(0, expand_ref.shape[1], chunk):
        part = slice(start, start + chunk)
        hidden = (back_mul(branch, contract_ref[part, :]) * slope[:, part]).astype(BF16)
        hidden_ref[:, part] = hidden
        shift_sum_ref[0:1, part] = jnp.sum(hidden.astype(F32), axis=0, keepdims=True)
        total = total + back_mul(hidden, expand_ref[:, part])
    add_sum(3, total * normed_one)
    add_sum(4, total)
    total = norm_back(total * gain_ref[0:1], normed_one, scale_one)
    one_ref[...] = total
    mixed = total.astype(BF16)
    mixed_ref[...] = mixed
    add_sum(5, mixed.astype(F32))
    ctx = back_mul(mixed, mixer_ref[...]).astype(BF16).astype(F32)
    for b in range(count):
        span = slice(b * rows, (b + 1) * rows)
        keys, values = qkv_ref[span, width : 2 * width], qkv_ref[span, 2 * width : 3 * width]
        query = qkv_ref[b * rows : b * rows + PACK, 0:width].astype(F32)[0:1] * head_dim**-0.5
        query = per_head(query, head_dim).astype(BF16)
        share = first_share(query, keys, lengths[b])
        ctx_heads = per_head(ctx[b : b + 1], head_dim).astype(BF16)
        share_grad = back_mul(ctx_heads, values)
        inner = jnp.sum(share * share_grad, axis=1, keepdims=True)
        score = (share * (share_grad - inner)).astype(BF16)
        query_grad = heads_joined(matmul(score, keys), head_dim) * head_dim**-0.5
        head_rows = parts_ref[0, b * rows : b * rows + PACK].astype(F32)
        top = lax.broadcasted_iota(jnp.int32, head_rows.shape, 0) == 0
        out_ref[0, span] = parts_ref[0, span]
        out_ref[0, b * rows : b * rows + PACK] = jnp.where(top, head_rows + query_grad, head_rows).astype(BF16)
        out_ref[1, span] = (parts_ref[1, span].astype(F32) + outer_sum(score, query)).astype(BF16)
        out_ref[2, span] = (parts_ref[2, span].astype(F32) + outer_sum(share.astype(BF16), ctx_heads)).astype(BF16)
    part_sums_ref[...] = jnp.zeros_like(part_sums_ref)
    for i in (0, 2):
        part_sums_ref[i : i + 1] = jnp.sum(out_ref[i].astype(F32), axis=0, keepdims=True)


def first_back(grad, kept, mats, gain, qkv, parts, lengths):
    count = lengths.shape[0]
    rows, width = qkv.shape[0] // count, grad.shape[1]
    hidden = mats[1].shape[1]
    blocks = [first_block(rows, array.shape[1], b) for array in kept for b in range(count)]
    rest = mats + (gain, qkv, parts)
    small = lambda n, kind, r=PACK: (pl.BlockSpec((r, n), lambda *_: (0, 0)), jax.ShapeDtypeStruct((r, n), kind))
    outs = [small(width, BF16), small(hidden, BF16), small(width, BF16), small(width, F32), small(width, F32, 8), small(hidden, F32, 1)]
    outs.append((whole(parts), jax.ShapeDtypeStruct(parts.shape, BF16)))
    outs.append(small(width, F32, 8))
    return pl.pallas_call(
        functools.partial(first_back_kernel, count=count, rows=rows, head_dim=width // HEADS, chunk=768),
        grid_spec=pltpu.PrefetchScalarGridSpec(
            num_scalar_prefetch=1,
            grid=(1,),
            in_specs=[whole(grad)] + blocks + [whole(r) for r in rest],
            out_specs=[spec for spec, _ in outs],
        ),
        out_shape=[shape for _, shape in outs],
        compiler_params=pltpu.CompilerParams(vmem_limit_bytes=32 * MIB),
        name="first_back",
    )(lengths, grad, *[array for array in kept for _ in range(count)], *rest)


def project_kernel(x_ref, joint_ref, shift_ref, out_ref):
    out_ref[...] = (matmul(x_ref[...], joint_ref[...]) + shift_ref[...]).astype(BF16)


def project(x, joint, shift):
    rows, width = x.shape
    step = min(256, rows)
    return pl.pallas_call(
        project_kernel,
        grid=(rows // step,),
        in_specs=[pl.BlockSpec((step, width), lambda i: (i, 0)), whole(joint), whole(shift)],
        out_specs=pl.BlockSpec((step, joint.shape[1]), lambda i: (i, 0)),
        out_shape=jax.ShapeDtypeStruct((rows, joint.shape[1]), BF16),
        compiler_params=pltpu.CompilerParams(vmem_limit_bytes=16 * MIB),
        name="project",
    )(x, joint, shift)


def input_grad_kernel(decoder, parts_ref, one_ref, first_ref, joint_ref, out_ref, *, step, rows):
    i = pl.program_id(0)
    width = out_ref.shape[1]

    total = one_ref[...]
    for j in range(3):
        total = total + back_mul(parts_ref[j], joint_ref[:, j * width : (j + 1) * width])
    out_ref[...] = total

    @pl.when(lax.rem(i * step, rows) == 0)
    def _():
        spot = lax.broadcasted_iota(jnp.int32, first_ref.shape, 0)
        row = jnp.sum(jnp.where(spot == i * step // rows, first_ref[...], 0.0), axis=0, keepdims=True)
        head = total[0:8]
        keep = jnp.where(decoder[0] == 1, 0.0, 1.0)
        top = lax.broadcasted_iota(jnp.int32, head.shape, 0) == 0
        out_ref[0:8] = jnp.where(top, (head + row) * keep, head)


def input_gradient(decoder, parts, one, one_first, joint, count):
    total_rows, width = one.shape
    rows = total_rows // count
    step = min(256, rows)
    return pl.pallas_call(
        functools.partial(input_grad_kernel, step=step, rows=rows),
        grid_spec=pltpu.PrefetchScalarGridSpec(
            num_scalar_prefetch=1,
            grid=(total_rows // step,),
            in_specs=[
                pl.BlockSpec((3, step, width), lambda i, _: (0, i, 0)),
                pl.BlockSpec((step, width), lambda i, _: (i, 0)),
                whole(one_first),
                whole(joint),
            ],
            out_specs=pl.BlockSpec((step, width), lambda i, _: (i, 0)),
        ),
        out_shape=jax.ShapeDtypeStruct(one.shape, F32),
        compiler_params=pltpu.CompilerParams(vmem_limit_bytes=48 * MIB),
        name="input_gradient",
    )(decoder, parts, one, one_first, joint)


def weight_grad_kernel(place, left_ref, right_ref, *refs):
    keep_ref, send_ref = refs[-2:]
    own, rows, _ = keep_ref.shape
    total = outer_sum(left_ref[...], right_ref[0]).astype(BF16)
    odd = lax.rem(place[0], 2) == 1
    for i in range(own):
        pair = [total[(2 * i + j) * rows : (2 * i + j + 1) * rows] for j in range(2)]
        keep_ref[i] = jnp.where(odd, pair[1], pair[0])
        send_ref[i] = jnp.where(odd, pair[0], pair[1])


def weight_grads(place, *pairs, tile=768):
    groups = lax.axis_size("dp")
    pairs = [(left, right if right.ndim == 3 else right[None]) for left, right in pairs]
    width = min(right.shape[2] for _, right in pairs)
    sizes = [left.shape[1] // groups for left, _ in pairs]
    heights = [size * right.shape[0] * right.shape[2] // width for size, (_, right) in zip(sizes, pairs)]
    if any(size % 16 for size in sizes):
        blocks = []
        for size, (left, right) in zip(sizes, pairs):
            total = jnp.concatenate([outer_sum(left, r) for r in right], axis=1).astype(BF16)
            total = total.reshape(groups, size, -1, width).transpose(0, 2, 1, 3)
            blocks.append(total.reshape(groups // 2, 2, -1, width))
        blocks = jnp.concatenate(blocks, axis=2)
        odd = lax.rem(place, 2)
        return tuple(lax.dynamic_index_in_dim(blocks, i, 1, False) for i in (odd, 1 - odd))
    shape = jax.ShapeDtypeStruct((groups // 2, sum(heights), width), BF16)
    done = []
    for i, (size, (left, right)) in enumerate(zip(sizes, pairs)):
        rows, height = left.shape
        cuts = right.shape[2] // width
        first = sum(heights[:i]) // size
        spec = pl.BlockSpec((tile // size // 2, size, width), lambda j, i, _, first=first: (i, first + j, 0))
        done = pl.pallas_call(
            weight_grad_kernel,
            grid_spec=pltpu.PrefetchScalarGridSpec(
                num_scalar_prefetch=1,
                grid=(right.shape[0] * cuts, height // tile),
                in_specs=[
                    pl.BlockSpec((rows, tile), lambda j, i, _: (0, i)),
                    pl.BlockSpec((1, rows, width), lambda j, i, _, cuts=cuts: (j // cuts, 0, j % cuts)),
                ]
                + [pl.BlockSpec(memory_space=pl.ANY)] * len(done),
                out_specs=[spec, spec],
            ),
            out_shape=[shape, shape],
            input_output_aliases={3: 0, 4: 1} if done else {},
            compiler_params=pltpu.CompilerParams(vmem_limit_bytes=48 * MIB),
            name="weight_grad",
        )(place.reshape(1), left, right, *done)
    return tuple(done)


def unstacked(total, shapes):
    parts = []
    start = 0
    for rows, columns in shapes:
        height = rows * columns // total.shape[1]
        part = total[start : start + height].reshape(-1, rows, total.shape[1])
        parts.append(part.transpose(1, 0, 2).reshape(rows, columns))
        start += height
    return parts


def add_split_kernel(mine, keep_a, got_a, keep_b, got_b, keep_ref, send_ref):
    keep_ref[...] = (keep_a[...].astype(F32) + got_a[...].astype(F32)).astype(BF16)
    send_ref[...] = (keep_b[...].astype(F32) + got_b[...].astype(F32)).astype(BF16)


def add_split(keep, got, axis, mine):
    rows, width = keep.shape[-2:]
    if rows % 16:
        total = (keep.astype(F32) + got.astype(F32)).astype(BF16)
        return tuple(lax.dynamic_index_in_dim(total, i, axis, False) for i in (mine, 1 - mine))
    rest = keep.shape[:axis] + keep.shape[axis + 1 : -2]
    before = 2**axis
    after = 2 ** (len(rest) - axis)
    shaped = [array.reshape(before, 2, after, rows, width) for array in (keep, got)]
    block = lambda other: pl.BlockSpec(
        (before, None, after, rows, min(width, 768)), lambda j, m: (0, (1 - m[0]) if other else m[0], 0, 0, j)
    )
    out = pl.BlockSpec((before, after, rows, min(width, 768)), lambda j, m: (0, 0, 0, j))
    shape = jax.ShapeDtypeStruct((before, after, rows, width), BF16)
    keep, send = pl.pallas_call(
        add_split_kernel,
        grid_spec=pltpu.PrefetchScalarGridSpec(
            num_scalar_prefetch=1,
            grid=(width // min(width, 768),),
            in_specs=[block(False), block(False), block(True), block(True)],
            out_specs=[out, out],
        ),
        out_shape=[shape, shape],
        compiler_params=pltpu.CompilerParams(vmem_limit_bytes=48 * MIB),
        name="add_split",
    )(mine.reshape(1), *shaped, *shaped)
    return keep.reshape(rest + (rows, width)), send.reshape(rest + (rows, width))


def first_hop(pair):
    keep, send = pair
    axes = tuple(reversed(bits_of(lax.axis_size("dp"))))[:-1]
    shape = (2,) * len(axes) + keep.shape[1:]
    return keep.reshape(shape), swapped(send, 1).reshape(shape), axes


def added(state, bit):
    keep, got, axes = state
    axis = axes.index(bit)
    mine = jnp.where((lax.axis_index("dp") & bit) == 0, 0, 1)
    return (*add_split(keep, got, axis, mine), axes[:axis] + axes[axis + 1 :])


def sent(halves, bit):
    keep, send, axes = halves
    return keep, swapped(send, bit), axes


def rest_of(state, order):
    for bit in order:
        state = sent(added(state, bit), bit)
    return state[0].astype(F32) + state[1].astype(F32)


def as_row(column):
    return jnp.broadcast_to(column, (column.shape[0], LANES)).T[0:1]


def as_column(row):
    return jnp.broadcast_to(row, (LANES, row.shape[1])).T[:, 0:1]


def word_cuts(slice_rows):
    size = 768
    return [
        (i, slice(start, min(start + size, slice_rows)), slice(i * slice_rows + start, i * slice_rows + min(start + size, slice_rows)))
        for i in range(2)
        for start in range(0, slice_rows, size)
    ]


def join(section, mine_ref, other_ref, out_ref):
    @pl.when(pl.program_id(0) == 0)
    def _():
        half = mine_ref.shape[0]
        out_ref[pl.ds(pl.multiple_of(section * half, 16), half)] = mine_ref[...]
        out_ref[pl.ds(pl.multiple_of((1 - section) * half, 16), half)] = other_ref[...]


def word_kernel(section, head_ref, own_ref, mine_ref, other_ref, shift_ref, peak_ref, total_ref, scores_ref, far_ref):
    join(section[0], mine_ref, other_ref, far_ref)
    group, picks, _ = head_ref.shape
    width = own_ref.shape[1]
    rows = group * picks
    head = head_ref[:, :, 0:width].reshape(rows, width)
    peak = jnp.full((rows, 1), -jnp.inf, F32)
    cuts = word_cuts(own_ref.shape[0])
    for table, part, columns in cuts:
        scores = back_mul(head, (own_ref, far_ref)[table][part]) + shift_ref[0:1, columns]
        scores_ref[:, columns] = scores
        peak = jnp.maximum(peak, jnp.max(scores, axis=1, keepdims=True))
    total = jnp.zeros_like(peak)
    for _, _, columns in cuts:
        total = total + jnp.sum(jnp.exp(scores_ref[:, columns] - peak), axis=1, keepdims=True)
    for g in range(group):
        part = slice(g * picks, (g + 1) * picks)
        peak_ref[g] = as_row(peak[part])
        total_ref[g] = as_row(total[part])


def word_scores(section, head, own, mine, other, shift, group=4):
    near, picks, padded = head.shape
    vocab = shift.shape[1]
    row = pl.BlockSpec((group, 1, picks), lambda k, _: (k, 0, 0))
    row_shape = jax.ShapeDtypeStruct((near, 1, picks), F32)
    return pl.pallas_call(
        word_kernel,
        grid_spec=pltpu.PrefetchScalarGridSpec(
            num_scalar_prefetch=1,
            grid=(near // group,),
            in_specs=[pl.BlockSpec((group, picks, padded), lambda k, _: (k, 0, 0))]
            + [whole(array) for array in (own, mine, other, shift)],
            out_specs=[row, row],
            scratch_shapes=[pltpu.VMEM((group * picks, vocab), F32), pltpu.VMEM(own.shape, BF16)],
        ),
        out_shape=[row_shape] * 2,
        compiler_params=pltpu.CompilerParams(vmem_limit_bytes=48 * MIB),
        name="word_scores",
    )(section, head, own, mine, other, shift)


def logit_kernel(place, head_ref, *refs, wholes):
    pairs = len(wholes)
    tables = refs[: sum(1 if w else 2 for w in wholes)]
    shift_ref, logit_ref, *joined = refs[len(tables) :]
    group, picks, _ = head_ref.shape
    width = tables[0].shape[1]
    head = head_ref[:, :, 0:width].reshape(group * picks, width)
    slice_rows = shift_ref.shape[1] // pairs
    for i, is_whole in enumerate(wholes):
        table_ref, *tables = tables
        if not is_whole:
            mine_ref, (other_ref, *tables) = table_ref, tables
            table_ref, *joined = joined
            join(place[1], mine_ref, other_ref, table_ref)
        columns = slice(i * slice_rows, (i + 1) * slice_rows)
        scores = (back_mul(head, table_ref[...]) + shift_ref[0:1, columns]).astype(BF16)
        for g in range(group):
            spot = jnp.bitwise_xor(lax.rem(place[0], group), g)
            logit_ref[spot, :, columns] = scores[g * picks : (g + 1) * picks]


def word_logits(place, head, tables, shift, group=4):
    near, picks, padded = head.shape
    vocab = shift.shape[1]
    slice_rows = vocab // len(tables)
    quarter = near // 2
    wholes = tuple(len(table) == 1 for table in tables)
    arrays = [array for table in tables for array in table]
    spot = lambda k, p: (jnp.bitwise_xor(lax.rem(p[0], quarter) // group, k), 0, 0)
    return pl.pallas_call(
        functools.partial(logit_kernel, wholes=wholes),
        grid_spec=pltpu.PrefetchScalarGridSpec(
            num_scalar_prefetch=1,
            grid=(quarter // group,),
            in_specs=[pl.BlockSpec((group, picks, padded), lambda k, _: (k, 0, 0))]
            + [whole(array) for array in arrays + [shift]],
            out_specs=pl.BlockSpec((group, picks, vocab), spot),
            scratch_shapes=[pltpu.VMEM((slice_rows, arrays[0].shape[1]), BF16)] * (len(tables) - sum(wholes)),
        ),
        out_shape=jax.ShapeDtypeStruct((quarter, picks, vocab), BF16),
        compiler_params=pltpu.CompilerParams(vmem_limit_bytes=48 * MIB),
        name="word_logits",
    )(place, head, *arrays, shift)


def labels_of(head_ref, width):
    label = head_ref[:, :, width:].astype(F32)
    label = label.reshape(-1, label.shape[2])
    return (label[:, 0:1] * 256.0 + label[:, 1:2]).astype(jnp.int32)


def word_back_kernel(first, head_ref, log_ref, own_ref, mine_ref, other_ref, shift_ref, grad_ref, out_ref, hit_ref, far_ref, *, masked):
    join(first[2], mine_ref, other_ref, far_ref)
    group, picks, width = out_ref.shape
    rows = group * picks
    label = labels_of(head_ref, width)
    logs = jnp.concatenate([as_column(log_ref[g]) for g in range(group)])
    head = head_ref[:, :, 0:width].reshape(rows, width)
    total = jnp.zeros((rows, width), F32)
    hit = jnp.zeros((rows, 1), F32)
    for table, part, columns in word_cuts(own_ref.shape[0]):
        words = (own_ref, far_ref)[table][part]
        scores = back_mul(head, words) + shift_ref[0:1, columns]
        share = jnp.exp(scores - logs)
        mine = lax.broadcasted_iota(jnp.int32, share.shape, 1) == label - (first[table] + part.start)
        hit = hit + jnp.sum(jnp.where(mine, scores, 0.0), axis=1, keepdims=True)
        grad = (jnp.where(mine, share - 1.0, share) * (1.0 / masked)).astype(BF16)
        if table == 0:
            grad_ref[:, :, columns] = grad.reshape(group, picks, -1)
        total = total + matmul(grad, words)
    out_ref[...] = total.astype(BF16).reshape(group, picks, width)
    for g in range(group):
        hit_ref[g] = as_row(hit[g * picks : (g + 1) * picks])


def word_back(first, head, logs, own, mine, other, shift, masked, group=4):
    near, picks, padded = head.shape
    width = own.shape[1]
    vocab = shift.shape[1]
    block = lambda n: pl.BlockSpec((group, picks, n), lambda k, _: (k, 0, 0))
    row = pl.BlockSpec((group, 1, picks), lambda k, _: (k, 0, 0))
    return pl.pallas_call(
        functools.partial(word_back_kernel, masked=masked),
        grid_spec=pltpu.PrefetchScalarGridSpec(
            num_scalar_prefetch=1,
            grid=(near // group,),
            in_specs=[block(padded), row] + [whole(array) for array in (own, mine, other, shift)],
            out_specs=[block(vocab // 2), block(width), row],
            scratch_shapes=[pltpu.VMEM(own.shape, BF16)],
        ),
        out_shape=[
            jax.ShapeDtypeStruct((near, picks, vocab // 2), BF16),
            jax.ShapeDtypeStruct((near, picks, width), BF16),
            jax.ShapeDtypeStruct((near, 1, picks), F32),
        ],
        compiler_params=pltpu.CompilerParams(vmem_limit_bytes=48 * MIB),
        name="word_back",
    )(first, head, logs, own, mine, other, shift)


def table_kernel(first, grad_ref, head_ref, other_ref, log_ref, own_ref, shift_ref, out_ref, sums_ref, total_ref, *, masked):
    @pl.when(pl.program_id(0) == 0)
    def _():
        total_ref[...] = jnp.zeros_like(total_ref)
        sums_ref[...] = jnp.zeros_like(sums_ref)

    group, picks, slice_rows = grad_ref.shape
    rows = group * picks
    width = own_ref.shape[1]
    label = labels_of(other_ref, width)
    logs = jnp.concatenate([as_column(log_ref[g]) for g in range(group)])
    head = head_ref[:, :, 0:width].reshape(rows, width)
    other = other_ref[:, :, 0:width].reshape(rows, width)
    for table, part, columns in word_cuts(slice_rows):
        if table == 0:
            share = jnp.exp(back_mul(other, own_ref[part]) + shift_ref[0:1, columns] - logs)
            mine = lax.broadcasted_iota(jnp.int32, share.shape, 1) == label - (first[0] + part.start)
            other_grad = (jnp.where(mine, share - 1.0, share) * (1.0 / masked)).astype(BF16)
            grad = grad_ref[:, :, part].reshape(rows, -1)
            sums_ref[0:1, part] += jnp.sum(grad.astype(F32) + other_grad.astype(F32), axis=0, keepdims=True)
            total_ref[part] += outer_sum(grad, head) + outer_sum(other_grad, other)

    @pl.when(pl.program_id(0) == pl.num_programs(0) - 1)
    def _():
        out_ref[...] = total_ref[...].astype(BF16)


def table_gradient(first, grad, head, other, logs, own, shift, masked, group=4):
    near, picks, slice_rows = grad.shape
    padded, width = head.shape[2], own.shape[1]
    block = lambda n: pl.BlockSpec((group, picks, n), lambda k, _: (k, 0, 0))
    row = pl.BlockSpec((group, 1, picks), lambda k, _: (k, 0, 0))
    return pl.pallas_call(
        functools.partial(table_kernel, masked=masked),
        grid_spec=pltpu.PrefetchScalarGridSpec(
            num_scalar_prefetch=1,
            grid=(near // group,),
            in_specs=[block(slice_rows), block(padded), block(padded), row, whole(own), whole(shift)],
            out_specs=[pl.BlockSpec(own.shape, lambda k, _: (0, 0)), pl.BlockSpec((1, slice_rows), lambda k, _: (0, 0))],
            scratch_shapes=[pltpu.VMEM(own.shape, F32)],
        ),
        out_shape=[jax.ShapeDtypeStruct(own.shape, BF16), jax.ShapeDtypeStruct((1, slice_rows), F32)],
        compiler_params=pltpu.CompilerParams(vmem_limit_bytes=48 * MIB),
        name="table_gradient",
    )(first, grad, head, other, logs, own, shift)


def assemble_kernel(place, near_ref, side_ref, out_ref, *, quarter):
    turn = jnp.bitwise_xor(place[0] // quarter, pl.program_id(0))
    for i, ref in enumerate((near_ref, side_ref)):

        @pl.when(turn % 2 == i)
        def _():
            out_ref[...] = ref[0]


def assembled(place, nears, sides):
    quarter, picks, vocab = nears.shape
    slice_rows = vocab // 2
    if slice_rows % LANES:
        parts = jnp.stack([array.reshape(quarter, picks, 2, slice_rows) for array in (nears, sides)], axis=3)
        parts = parts.reshape(quarter, picks, 4, slice_rows)
        parts = jnp.take(parts, jnp.bitwise_xor(jnp.arange(4), place // quarter), axis=2)
        return parts.transpose(1, 2, 0, 3).reshape(picks, 2 * quarter * vocab)

    def spec(side):
        def index(b, j, p):
            turn = jnp.bitwise_xor(p[0] // quarter, b)
            last = jnp.bitwise_xor(p[0] // quarter, jnp.bitwise_xor(b, 1)) // 2
            first_of_pair = lax.rem(b, 2) == 0
            return (
                jnp.where(lax.rem(turn, 2) == side, j, jnp.where(first_of_pair, 0, quarter - 1)),
                0,
                jnp.where(lax.rem(turn, 2) == side, turn // 2, last),
            )

        return pl.BlockSpec((1, picks, slice_rows), index)

    return pl.pallas_call(
        functools.partial(assemble_kernel, quarter=quarter),
        grid_spec=pltpu.PrefetchScalarGridSpec(
            num_scalar_prefetch=1,
            grid=(4, quarter),
            in_specs=[spec(0), spec(1)],
            out_specs=pl.BlockSpec((picks, slice_rows), lambda b, j, _: (0, b * quarter + j)),
        ),
        out_shape=jax.ShapeDtypeStruct((picks, 2 * quarter * vocab), BF16),
        compiler_params=pltpu.CompilerParams(vmem_limit_bytes=48 * MIB),
        name="assemble",
    )(place.reshape(1), nears, sides)


def on_device(
    embedded,
    lengths,
    positions,
    labels,
    joint_weight,
    mixer_weight,
    expand_weight,
    contract_weight,
    head_weight,
    gains,
    biases,
    expand_bias,
    word_table,
    word_bias,
):
    section = lax.axis_index("section")
    place = lax.axis_index("dp")
    groups = lax.axis_size("dp")
    decoder = section == 1
    count, rows, width = embedded.shape[1:]
    total_rows = count * rows
    head_dim = width // HEADS
    masked = positions.shape[-1]
    picks = count * masked
    joint = joint_weight[0]
    mats = (mixer_weight[0], expand_weight[0], contract_weight[0])
    head_matrix = head_weight[0]
    gain = gains[0]
    bias = biases[0]
    shift = expand_bias
    slice_rows = word_table.shape[0]

    flag = section.astype(jnp.int32).reshape(1)
    place32 = place.astype(jnp.int32)
    units = shift.shape[1]
    own = width // groups
    near, quarter = groups // 2, groups // 4
    half = slice_rows // 2
    bits = bits_of(groups)
    order = bits[-2:-1] + bits[1:-2] + bits[-1:]
    turned = bits[1:]
    across = lambda array: lax.ppermute(array, "section", [(0, 1), (1, 0)])

    my_half = lax.dynamic_slice_in_dim(word_table, section * half, half)
    far_one, far_two = (swapped(piece, near) for piece in (my_half[: half // 2], my_half[half // 2 :]))
    side_half = swapped(my_half, quarter)

    x = embedded[0].reshape(total_rows, width)
    joint_shift = jnp.concatenate([bias[0], jnp.zeros((width,), F32), bias[1]])[None]
    qkv = project(x, joint, joint_shift)
    cls_out = cls_forward(x, qkv, lengths, mats, gain, bias, shift)
    cls_in = passed_along(cls_out, "section", 1)
    x, qkv = place_first(flag, cls_in, x, qkv, joint, joint_shift, count)
    ctx, logs = attend(qkv, lengths, count)
    ctx, far_one = tied(ctx, far_one)
    far_one_other = across(far_one)
    far_shift = swapped(word_bias, near)
    side_shift = swapped(word_bias, quarter)
    y, normed_one, scale_one, first_low, active, slope, normed_two, scale_two = layer_tail(
        ctx, x, mats, gain, bias, shift
    )
    y, far_one_other, far_two, far_shift, side_shift, side_half = tied(
        y, far_one_other, far_two, far_shift, side_shift, side_half
    )
    far_two_other = across(far_two)
    far_mine = jnp.concatenate([far_one, far_two])
    side_far_shift = swapped(far_shift, quarter)

    chosen = positions[0][:, :, None] == jnp.arange(rows)[None, None, :]
    picked = jnp.einsum(
        "bml,blw->bmw", chosen.astype(BF16), y.reshape(count, rows, width), preferred_element_type=F32
    )
    picked_low = picked.astype(BF16).reshape(picks, width)
    dense = matmul(picked_low, head_matrix) + bias[6]
    dense_active, dense_slope = gelu_and_slope(dense)
    normed_head, scale_head = normalise(dense_active)
    head_low = (normed_head * gain[2] + bias[7]).astype(BF16)
    answers = labels[0].reshape(-1, 1)
    answers = jnp.concatenate([answers // 256, answers % 256, jnp.zeros((picks, LANES - 2), jnp.int32)], axis=1)
    head_low = jnp.concatenate([head_low, answers.astype(BF16)], axis=1)
    head_all, head_low, far_two_other, side_far_shift = tied(
        gather_chips(head_low), head_low, far_two_other, side_far_shift
    )
    head_all = gather_cores(head_all)
    head_other = swapped(head_low, near)
    far_other = jnp.concatenate([far_one_other, far_two_other])
    word_shift = jnp.concatenate([word_bias, far_shift]).astype(F32)[None]
    side_word_shift = jnp.concatenate([side_shift, side_far_shift]).astype(F32)[None]
    where_to = jnp.stack([place32, section.astype(jnp.int32)])
    head_all, side_half = tied(head_all, side_half)
    side_half_other = across(side_half)
    peak, total = word_scores(flag, head_all, word_table, far_mine, far_other, word_shift)
    peak, head_other = tied(peak, head_other)
    grid = (2,) * (len(bits) - 1)
    peak, total = (array.reshape(grid + (picks,)) for array in (peak, total))
    for axis, bit in enumerate(reversed(bits[:-1])):
        other_peak, other_total = jnp.flip(swapped(jnp.stack([peak, total]), bit), axis + 1)
        top = jnp.maximum(peak, other_peak)
        total = total * jnp.exp(peak - top) + other_total * jnp.exp(other_peak - top)
        peak = top
    log_total = (peak + jnp.log(total)).reshape(near, 1, picks)
    log_other = swapped(log_total, near)
    head_other = gather_chips(head_other)
    first = (jnp.stack([place, jnp.bitwise_xor(place, near)]) * slice_rows).astype(jnp.int32)
    first = jnp.concatenate([first, flag])
    score_grad, head_back, hits = word_back(
        first, head_all, log_total, word_table, far_mine, far_other, word_shift, masked
    )
    head_back, side_half_other, head_other, log_other = tied(head_back, side_half_other, head_other, log_other)
    head_other = gather_cores(head_other)
    loss_part = jnp.sum(log_total[0]) - jnp.sum(hits)
    head_grad = scatter_near(head_back)
    table_grad, word_sums = table_gradient(
        first, score_grad, head_all, head_other, log_other, word_table, word_shift, masked
    )
    head_grad, table_grad, word_sums, far_mine = tied(head_grad, table_grad, word_sums, far_mine)
    word_other = across(word_sums)
    side_far_half = swapped(far_mine, quarter)
    exchanged = lambda part: lax.all_to_all(
        part, "dp", 0, 0, axis_index_groups=[list(range(i, i + quarter)) for i in range(0, groups, quarter)]
    )
    logits_near = word_logits(where_to, head_all, ((word_table,), (far_mine, far_other)), word_shift)
    head_grad, logits_near = tied(head_grad, logits_near)
    logits_near = exchanged(logits_near)

    gain_head = jnp.sum(head_grad * normed_head, 0)
    shift_head = jnp.sum(head_grad, 0)
    dense_grad = (norm_back(head_grad * gain[2], normed_head, scale_head) * dense_slope).astype(BF16)
    dense_shift = jnp.sum(dense_grad, axis=0, dtype=F32)
    picked_grad = back_mul(dense_grad, head_matrix).reshape(count, masked, width)
    grad = jnp.einsum(
        "bml,bmw->blw", chosen.astype(F32), picked_grad, precision=lax.Precision.HIGHEST
    ).reshape(total_rows, width)

    kept = (normed_two, scale_two, slope, normed_one, scale_one)
    branch, hidden, one, mixed, ctx_grad, sums, shift_sum = tail_back(grad, kept, mats, gain)
    hidden, branch, side_far_half, word_other = tied(hidden, branch, side_far_half, word_other)
    side_far_other = across(side_far_half)
    one_pair = weight_grads(place32, (active, branch), (ctx, mixed))
    hidden, one_pair = tied(hidden, one_pair)
    one_state = first_hop(one_pair)
    two_pair = weight_grads(place32, (first_low, hidden), (picked_low, dense_grad))
    ctx_grad, two_pair, logits_near = tied(ctx_grad, two_pair, logits_near)
    two_state = first_hop(two_pair)
    one_halves, two_halves = added(one_state, order[0]), added(two_state, turned[0])
    ctx_grad, one_now, two_now = tied(ctx_grad, one_halves[:2], two_halves[:2])
    one_state, two_state = sent((*one_now, one_halves[2]), order[0]), sent((*two_now, two_halves[2]), turned[0])
    parts = attend_back(qkv, ctx_grad, logs, lengths)
    one_halves, two_halves = added(one_state, order[1]), added(two_state, turned[1])
    parts, one_now, two_now, side_far_other = tied(parts, one_halves[:2], two_halves[:2], side_far_other)
    logits_side = word_logits(
        where_to, head_all, ((side_half, side_half_other), (side_far_half, side_far_other)), side_word_shift
    )
    one_state, two_state = sent((*one_now, one_halves[2]), order[1]), sent((*two_now, two_halves[2]), turned[1])
    logits_side = exchanged(logits_side)
    cls_grad = passed_along(cls_back(parts, one, joint, count), "section", -1)
    cls_grad, table_grad = tied(cls_grad, table_grad)
    table_top = across(table_grad[:half])

    branch_f, hidden_f, mixed_f, one_f, sums_f, shift_f, parts, part_sums = first_back(
        cls_grad, kept, mats, gain, qkv, parts, lengths
    )
    two_halves = added(two_state, turned[2])
    parts, two_now = tied(parts, two_halves[:2])
    two_state = sent((*two_now, two_halves[2]), turned[2])

    def firsts(array):
        return jnp.concatenate([array[b * rows : b * rows + 1] for b in range(count)])

    mine = jnp.concatenate(
        [firsts(active), firsts(first_low), firsts(ctx), branch_f[:count], hidden_f[:count], mixed_f[:count]],
        axis=1,
    )
    sums = sums + sums_f
    small = jnp.concatenate(
        [
            jnp.stack([sums[3], sums[0], gain_head]),
            jnp.stack(
                [part_sums[0], part_sums[2], sums[5], sums[4], sums[2], sums[1], dense_shift, shift_head]
            ),
            (shift_sum + shift_f).reshape(-1, width),
            jnp.broadcast_to(loss_part, (1, width)),
        ]
    )
    small_high = lax.reduce_precision(small, 8, 7)
    small_low = (small - small_high).astype(BF16)
    small_high = small_high.astype(BF16)
    mine = mine.reshape(-1, width)
    counts = [mine.shape[0], small.shape[0], small.shape[0]]
    gathered = jnp.concatenate([mine, small_high, small_low])[None]
    arriving = swapped(gathered, near)
    joint_pair = weight_grads(place32, (x, parts))
    parts, joint_pair, arriving, logits_side = tied(parts, joint_pair, arriving, logits_side)
    joint_state = first_hop(joint_pair)
    gathered = side_by_side(gathered, arriving, near)
    arriving = swapped(gathered, quarter)
    joint_halves = added(joint_state, order[0])
    parts, joint_now, arriving = tied(parts, joint_halves[:2], arriving)
    joint_state = sent((*joint_now, joint_halves[2]), order[0])
    bit = quarter
    for below in reversed(bits[:-2]):
        gathered = side_by_side(gathered, arriving, bit)
        arriving = swapped(gathered, below)
        bit = below
        if bit == 2:
            input_grad = input_gradient(flag, parts, one, one_f, joint, count)
            input_grad, logits_near, logits_side = tied(input_grad, logits_near, logits_side)
            logits_out = assembled(place32, logits_near, logits_side)
            logits_out, arriving = tied(logits_out, arriving)
    logits_out, one_got, table_top = tied(logits_out, one_state[1], table_top)
    table_rest = across(table_grad[half:])
    one_halves = added((one_state[0], one_got, one_state[2]), order[2])
    logits_out, one_now = tied(logits_out, one_halves[:2])
    one_state = sent((*one_now, one_halves[2]), order[2])
    joint_keep, joint_got, logits_out, input_grad, two_got = tied(
        *joint_state[:2], logits_out, input_grad, two_state[1]
    )
    two_state = two_state[0], two_got, two_state[2]
    joint_state = sent(added((joint_keep, joint_got, joint_state[2]), order[1]), order[1])
    expand_sum, head_sum = unstacked(rest_of(two_state, turned[3:]), [(own, units), (own, width)])
    joint_keep, joint_got, expand_sum, head_sum = tied(*joint_state[:2], expand_sum, head_sum)
    joint_keep, joint_send, axes = added((joint_keep, joint_got, joint_state[2]), order[2])
    joint_got = swapped(joint_send, order[2])
    joint_keep, arriving, one_got, table_rest = tied(joint_keep, arriving, one_state[1], table_rest)
    table_total = table_grad.astype(F32) + jnp.concatenate([table_top, table_rest]).astype(F32)
    one_state = one_state[0], one_got, one_state[2]
    contract_sum, mixer_sum = unstacked(rest_of(one_state, order[3:]), [(units // groups, width), (own, width)])
    joint_sum = unstacked(rest_of((joint_keep, joint_got, axes), order[3:]), [(own, 3 * width)])[0]
    rows_all = side_by_side(gathered, arriving, 1)
    small = jnp.sum(rows_all[:, counts[0] :].astype(F32), axis=0)
    small = small[: counts[1]] + small[counts[1] :]
    rows_all = rows_all[:, : counts[0]].reshape(groups * count, -1)
    word_total = word_sums[0] + word_other[0]
    cuts = [units, width, width, width, units, width]
    starts = [sum(cuts[:i]) for i in range(len(cuts))]
    active_a, first_a, ctx_a, branch_a, hidden_a, mixed_a = (
        rows_all[:, s : s + n] for s, n in zip(starts, cuts)
    )

    def own_columns(array):
        size = array.shape[1] // groups
        return lax.dynamic_slice_in_dim(array, place * size, size, 1)

    contract_sum = contract_sum + outer_sum(own_columns(active_a), branch_a)
    expand_sum = expand_sum + outer_sum(own_columns(first_a), hidden_a)
    mixer_sum = mixer_sum + outer_sum(own_columns(ctx_a), mixed_a)

    loss = (small[-1, 0] / (picks * groups)).reshape(1)
    return (
        loss,
        logits_out.reshape(1, count, masked, -1),
        input_grad.reshape(1, count, rows, width),
        joint_sum[None],
        mixer_sum[None],
        expand_sum[None],
        contract_sum[None],
        head_sum[None],
        small[None, :3],
        small[None, 3:11],
        small[11:-1].reshape(1, -1),
        table_total,
        word_total,
    )


def solution(mesh):
    in_specs = (
        P("section", "dp", None, None),
        P("dp"),
        P("section", "dp", None),
        P("section", "dp", None),
        P("section", None, None),
        P("section", None, None),
        P("section", None, None),
        P("section", None, None),
        P("section", None, None),
        P("section", None, None),
        P("section", None, None),
        P("section", None),
        P("dp", None),
        P("dp"),
    )
    out_specs = (
        P("section"),
        P("section", "dp", None, None),
        P("section", "dp", None, None),
        P("section", "dp", None),
        P("section", "dp", None),
        P("section", "dp", None),
        P("section", "dp", None),
        P("section", "dp", None),
        P("section", None, None),
        P("section", None, None),
        P("section", None),
        P("dp", None),
        P("dp"),
    )
    return jax.shard_map(
        on_device, mesh=mesh, in_specs=in_specs, out_specs=out_specs, check_vma=False
    )
```

```python
import functools

import jax
import jax.numpy as jnp
from jax import lax
from jax.experimental import pallas as pl
from jax.experimental.pallas import tpu as pltpu
from jax.sharding import PartitionSpec as P

HEADS = 12
EPS = 1e-12
ROOT_HALF = 0.7071067811865476
INV_ROOT_TAU = 0.3989422804014327
HIDDEN = -1000000000.0
LANES = 128
MIB = 1024 * 1024
F32 = jnp.float32
BF16 = jnp.bfloat16


def product(left, right, left_dim, right_dim):
    return lax.dot_general(
        left, right, (((left_dim,), (right_dim,)), ((), ())), preferred_element_type=F32
    )


def matmul(left, right):
    return product(left, right, 1, 0)


def outer_sum(left, right):
    return product(left, right, 0, 0)


def back_mul(left, right):
    return product(left, right, 1, 1)


def passed_along(block, axis, distance):
    devices = range(lax.axis_size(axis))
    route = [(i - distance, i) for i in devices if i - distance in devices]
    return lax.ppermute(block, axis, route)


def swapped(block, bit):
    devices = range(lax.axis_size("dp"))
    return lax.ppermute(block, "dp", [(i, i ^ bit) for i in devices])


def bits_of(order):
    return [1 << i for i in range(order.bit_length() - 1)]


def tied(*values):
    return lax.optimization_barrier(values)


def side_by_side(blocks, other, bit):
    low = (lax.axis_index("dp") & bit) == 0
    pair = [jnp.where(low, blocks, other), jnp.where(low, other, blocks)]
    return jnp.stack(pair, axis=1).reshape((-1,) + blocks.shape[1:])


def gather_chips(block):
    return [block] + [swapped(block, mask) for mask in range(2, lax.axis_size("dp") // 2, 2)]


def gather_cores(blocks):
    blocks = jnp.stack(blocks)
    return jnp.stack([blocks, swapped(blocks, 1)], axis=1).reshape((-1,) + blocks.shape[1:])


def scatter_near(blocks):
    blocks = blocks.reshape((-1, 2) + blocks.shape[1:])
    got = swapped(blocks[:, 1], 1)
    blocks = (blocks[:, 0].astype(F32) + got.astype(F32)).astype(BF16)
    total = blocks[0].astype(F32)
    for i in range(1, blocks.shape[0]):
        total = total + swapped(blocks[i], 2 * i).astype(F32)
    return total


def normalise(resid):
    centre = resid - jnp.mean(resid, axis=-1, keepdims=True)
    scale_inv = lax.rsqrt(jnp.mean(centre * centre, axis=-1, keepdims=True) + EPS)
    return centre * scale_inv, scale_inv


def norm_back(scaled, normed, scale_inv):
    first_mean = jnp.mean(scaled, axis=-1, keepdims=True)
    second_mean = jnp.mean(scaled * normed, axis=-1, keepdims=True)
    return scale_inv * (scaled - first_mean - normed * second_mean)


def gelu_and_slope(value):
    gate = 0.5 * (1.0 + lax.erf(value * ROOT_HALF))
    return value * gate, gate + value * jnp.exp(-0.5 * value * value) * INV_ROOT_TAU


def attend_kernel(lengths, q_ref, k_ref, v_ref, out_ref, log_ref, *, head_dim):
    length = lengths[pl.program_id(0)]
    rows, lanes = q_ref.shape
    q = q_ref[...] * (head_dim**-0.5)
    k = k_ref[...]
    v_t = v_ref[...].T
    head_of = lax.broadcasted_iota(jnp.int32, (rows, lanes), 1) // head_dim
    visible = lax.broadcasted_iota(jnp.int32, (rows, rows), 0) < length
    parts = []
    for head in range(lanes // head_dim):
        scores = back_mul(k, jnp.where(head_of == head, q, jnp.zeros_like(q)))
        scores = jnp.where(visible, scores, HIDDEN)
        peak = jnp.max(scores, axis=0, keepdims=True)
        powers = jnp.exp(scores - peak)
        total = jnp.sum(powers, axis=0, keepdims=True)
        piece = matmul(v_t[head * head_dim : (head + 1) * head_dim], powers.astype(BF16))
        parts.append(piece / total)
        log_ref[0, head : head + 1, :] = peak + jnp.log(total)
    out_ref[...] = jnp.concatenate(parts, axis=0).T.astype(BF16)


def attend(qkv, lengths, count):
    rows = qkv.shape[0] // count
    width = qkv.shape[1] // 3
    pairs = width // LANES
    head_dim = width // HEADS
    block = lambda part: pl.BlockSpec((rows, LANES), lambda b, p, _: (b, part * pairs + p))
    return pl.pallas_call(
        functools.partial(attend_kernel, head_dim=head_dim),
        grid_spec=pltpu.PrefetchScalarGridSpec(
            num_scalar_prefetch=1,
            grid=(count, pairs),
            in_specs=[block(0), block(1), block(2)],
            out_specs=[
                pl.BlockSpec((rows, LANES), lambda b, p, _: (b, p)),
                pl.BlockSpec((1, LANES // head_dim, rows), lambda b, p, _: (b * pairs + p, 0, 0)),
            ],
        ),
        out_shape=[
            jax.ShapeDtypeStruct((count * rows, width), BF16),
            jax.ShapeDtypeStruct((count * pairs, LANES // head_dim, rows), F32),
        ],
        compiler_params=pltpu.CompilerParams(vmem_limit_bytes=48 * MIB),
        name="attend",
    )(lengths, qkv, qkv, qkv)


def attend_back_kernel(lengths, q_ref, k_ref, v_ref, grad_ref, log_ref, out_ref, *, head_dim):
    length = lengths[pl.program_id(0)]
    rows, lanes = q_ref.shape
    scale = head_dim**-0.5
    q = q_ref[...] * scale
    k = k_ref[...]
    v = v_ref[...]
    grad = grad_ref[...]
    head_of = lax.broadcasted_iota(jnp.int32, (rows, lanes), 1) // head_dim
    visible = lax.broadcasted_iota(jnp.int32, (rows, rows), 0) < length
    totals = [jnp.zeros((rows, lanes), F32)] * 3
    for head in range(lanes // head_dim):
        mine = head_of == head
        scores = back_mul(k, jnp.where(mine, q, jnp.zeros_like(q)))
        share = jnp.where(visible, jnp.exp(scores - log_ref[0, head : head + 1, :]), 0.0)
        share_grad = back_mul(jnp.where(mine, v, jnp.zeros_like(v)), grad)
        inner = jnp.sum(share * share_grad, axis=0, keepdims=True)
        score_grad = (share * (share_grad - inner)).astype(BF16)
        parts = (
            outer_sum(score_grad, k) * scale,
            matmul(score_grad, q),
            matmul(share.astype(BF16), grad),
        )
        totals = [jnp.where(mine, part, total) for part, total in zip(parts, totals)]
    for i, total in enumerate(totals):
        out_ref[i] = total.astype(BF16)


def attend_back(qkv, grad, logs, lengths):
    count = lengths.shape[0]
    rows = qkv.shape[0] // count
    width = qkv.shape[1] // 3
    pairs = width // LANES
    head_dim = width // HEADS
    block = lambda part: pl.BlockSpec((rows, LANES), lambda b, p, _: (b, part * pairs + p))
    return pl.pallas_call(
        functools.partial(attend_back_kernel, head_dim=head_dim),
        grid_spec=pltpu.PrefetchScalarGridSpec(
            num_scalar_prefetch=1,
            grid=(count, pairs),
            in_specs=[
                block(0),
                block(1),
                block(2),
                block(0),
                pl.BlockSpec((1, LANES // head_dim, rows), lambda b, p, _: (b * pairs + p, 0, 0)),
            ],
            out_specs=pl.BlockSpec((3, rows, LANES), lambda b, p, _: (0, b, p)),
        ),
        out_shape=jax.ShapeDtypeStruct((3, count * rows, width), BF16),
        compiler_params=pltpu.CompilerParams(vmem_limit_bytes=48 * MIB),
        name="attend_back",
    )(lengths, qkv, qkv, qkv, grad, logs)


def tail_kernel(
    ctx_ref, x_ref, mixer_ref, expand_ref, contract_ref, gain_ref, bias_ref, shift_ref,
    y_ref, normed_one_ref, scale_one_ref, first_ref, active_ref, slope_ref, normed_two_ref, scale_two_ref,
    *, chunk,
):
    mixed = matmul(ctx_ref[...], mixer_ref[...]) + bias_ref[2:3]
    normed, scale = normalise(x_ref[...].astype(F32) + mixed)
    first = normed * gain_ref[0:1] + bias_ref[3:4]
    first_low = first.astype(BF16)
    normed_one_ref[...] = normed.astype(BF16)
    scale_one_ref[...] = jnp.broadcast_to(scale, scale_one_ref.shape)
    first_ref[...] = first_low
    total = first + bias_ref[4:5]
    for start in range(0, expand_ref.shape[1], chunk):
        part = slice(start, start + chunk)
        hidden = matmul(first_low, expand_ref[:, part]) + shift_ref[0:1, part]
        active, slope = gelu_and_slope(hidden)
        active = active.astype(BF16)
        active_ref[:, part] = active
        slope_ref[:, part] = slope.astype(BF16)
        total = total + matmul(active, contract_ref[part, :])
    normed, scale = normalise(total)
    normed_two_ref[...] = normed.astype(BF16)
    scale_two_ref[...] = jnp.broadcast_to(scale, scale_two_ref.shape)
    y_ref[...] = (normed * gain_ref[1:2] + bias_ref[5:6]).astype(BF16)


def whole(array):
    return pl.BlockSpec(array.shape, lambda *_: (0,) * array.ndim, pipeline_mode=pl.Buffered(1))


def layer_tail(ctx, x, mats, gain, bias, shift, step=256, chunk=3072):
    rows, width = x.shape
    hidden = shift.shape[1]
    step = min(step, rows)
    by_row = lambda n: pl.BlockSpec((step, n), lambda i: (i, 0))
    shape = lambda n, kind: jax.ShapeDtypeStruct((rows, n), kind)
    widths = [(width, BF16), (width, BF16), (LANES, F32), (width, BF16), (hidden, BF16), (hidden, BF16), (width, BF16), (LANES, F32)]
    return pl.pallas_call(
        functools.partial(tail_kernel, chunk=min(chunk, hidden)),
        grid=(rows // step,),
        in_specs=[by_row(width), by_row(width)] + [whole(m) for m in mats + (gain, bias, shift)],
        out_specs=[by_row(n) for n, _ in widths],
        out_shape=[shape(n, kind) for n, kind in widths],
        compiler_params=pltpu.CompilerParams(vmem_limit_bytes=48 * MIB),
        name="layer_tail",
    )(ctx, x, *mats, gain, bias, shift)


def tail_back_kernel(
    grad_ref, normed_two_ref, scale_two_ref, slope_ref, normed_one_ref, scale_one_ref,
    mixer_ref, expand_ref, contract_ref, gain_ref,
    branch_ref, hidden_ref, one_ref, mixed_ref, ctx_ref, sums_ref, shift_sum_ref,
    *, chunk,
):
    @pl.when(pl.program_id(0) == 0)
    def _():
        sums_ref[...] = jnp.zeros_like(sums_ref)
        shift_sum_ref[...] = jnp.zeros_like(shift_sum_ref)

    def add_sum(row, value):
        sums_ref[row : row + 1] += jnp.sum(value, axis=0, keepdims=True)

    grad = grad_ref[...]
    normed = normed_two_ref[...].astype(F32)
    add_sum(0, grad * normed)
    add_sum(1, grad)
    total = norm_back(grad * gain_ref[1:2], normed, scale_two_ref[:, 0:1])
    branch = total.astype(BF16)
    branch_ref[...] = branch
    add_sum(2, branch.astype(F32))
    for start in range(0, expand_ref.shape[1], chunk):
        part = slice(start, start + chunk)
        hidden = back_mul(branch, contract_ref[part, :]) * slope_ref[:, part].astype(F32)
        hidden = hidden.astype(BF16)
        hidden_ref[:, part] = hidden
        shift_sum_ref[0:1, part] += jnp.sum(hidden.astype(F32), axis=0, keepdims=True)
        total = total + back_mul(hidden, expand_ref[:, part])
    normed = normed_one_ref[...].astype(F32)
    add_sum(3, total * normed)
    add_sum(4, total)
    total = norm_back(total * gain_ref[0:1], normed, scale_one_ref[:, 0:1])
    one_ref[...] = total
    mixed = total.astype(BF16)
    mixed_ref[...] = mixed
    add_sum(5, mixed.astype(F32))
    ctx_ref[...] = back_mul(mixed, mixer_ref[...]).astype(BF16)


def tail_back(grad, kept, mats, gain, step=256, chunk=3072):
    rows, width = grad.shape
    hidden = mats[1].shape[1]
    step = min(step, rows)
    by_row = lambda n: pl.BlockSpec((step, n), lambda i: (i, 0))
    shape = lambda n, kind: jax.ShapeDtypeStruct((rows, n), kind)
    widths = [(width, BF16), (hidden, BF16), (width, F32), (width, BF16), (width, BF16)]
    return pl.pallas_call(
        functools.partial(tail_back_kernel, chunk=min(chunk, hidden)),
        grid=(rows // step,),
        in_specs=[by_row(array.shape[1]) for array in (grad,) + kept] + [whole(m) for m in mats + (gain,)],
        out_specs=[by_row(n) for n, _ in widths]
        + [pl.BlockSpec((8, width), lambda i: (0, 0)), pl.BlockSpec((1, hidden), lambda i: (0, 0))],
        out_shape=[shape(n, kind) for n, kind in widths]
        + [jax.ShapeDtypeStruct((8, width), F32), jax.ShapeDtypeStruct((1, hidden), F32)],
        compiler_params=pltpu.CompilerParams(vmem_limit_bytes=48 * MIB),
        name="tail_back",
    )(grad, *kept, *mats, gain)


PACK = 16


def first_block(rows, width, passage):
    return pl.BlockSpec((PACK, width), lambda *_: (passage * rows // PACK, 0))


def packed(refs):
    rows = [ref[...].astype(F32)[0:1] for ref in refs]
    place = lax.broadcasted_iota(jnp.int32, (PACK, rows[0].shape[1]), 0)
    total = jnp.zeros((PACK, rows[0].shape[1]), F32)
    for i, row in enumerate(rows):
        total = jnp.where(place == i, row, total)
    return total


def per_head(row, head_dim):
    shape = (PACK, row.shape[1])
    mine = lax.broadcasted_iota(jnp.int32, shape, 1) // head_dim == lax.broadcasted_iota(jnp.int32, shape, 0)
    return jnp.where(mine, row, 0.0)


def heads_joined(block, head_dim):
    mine = lax.broadcasted_iota(jnp.int32, block.shape, 1) // head_dim == lax.broadcasted_iota(jnp.int32, block.shape, 0)
    return jnp.sum(jnp.where(mine, block, 0.0), axis=0, keepdims=True)


def first_share(query, keys, length):
    scores = back_mul(query, keys)
    visible = lax.broadcasted_iota(jnp.int32, scores.shape, 1) < length
    scores = jnp.where(visible, scores, HIDDEN)
    powers = jnp.exp(scores - jnp.max(scores, axis=1, keepdims=True))
    return powers / jnp.sum(powers, axis=1, keepdims=True)


def cls_kernel(lengths, *refs, count, rows, head_dim, chunk):
    x_refs, (qkv_ref, mixer_ref, expand_ref, contract_ref, gain_ref, bias_ref, shift_ref, out_ref) = (
        refs[:count],
        refs[count:],
    )
    width = out_ref.shape[1]
    x = packed(x_refs)
    place = lax.broadcasted_iota(jnp.int32, (PACK, width), 0)
    ctx = jnp.zeros((PACK, width), F32)
    for b in range(count):
        base = b * rows
        query = qkv_ref[base : base + PACK, 0:width].astype(F32)[0:1] * head_dim**-0.5
        query = per_head(query, head_dim).astype(BF16)
        share = first_share(query, qkv_ref[base : base + rows, width : 2 * width], lengths[b])
        mixed = matmul(share.astype(BF16), qkv_ref[base : base + rows, 2 * width : 3 * width])
        ctx = jnp.where(place == b, heads_joined(mixed, head_dim), ctx)
    mixed = matmul(ctx.astype(BF16), mixer_ref[...]) + bias_ref[2:3]
    first = normalise(x + mixed)[0] * gain_ref[0:1] + bias_ref[3:4]
    first_low = first.astype(BF16)
    total = first + bias_ref[4:5]
    for start in range(0, expand_ref.shape[1], chunk):
        part = slice(start, start + chunk)
        active, _ = gelu_and_slope(matmul(first_low, expand_ref[:, part]) + shift_ref[0:1, part])
        total = total + matmul(active.astype(BF16), contract_ref[part, :])
    out_ref[...] = (normalise(total)[0] * gain_ref[1:2] + bias_ref[5:6]).astype(BF16)


def cls_forward(x, qkv, lengths, mats, gain, bias, shift):
    count = lengths.shape[0]
    rows, width = x.shape[0] // count, x.shape[1]
    rest = (qkv,) + mats + (gain, bias, shift)
    return pl.pallas_call(
        functools.partial(cls_kernel, count=count, rows=rows, head_dim=width // HEADS, chunk=768),
        grid_spec=pltpu.PrefetchScalarGridSpec(
            num_scalar_prefetch=1,
            grid=(1,),
            in_specs=[first_block(rows, width, b) for b in range(count)] + [whole(r) for r in rest],
            out_specs=pl.BlockSpec((PACK, width), lambda *_: (0, 0)),
        ),
        out_shape=jax.ShapeDtypeStruct((PACK, width), BF16),
        compiler_params=pltpu.CompilerParams(vmem_limit_bytes=26 * MIB),
        name="cls_forward",
    )(lengths, *[x] * count, *rest)


def place_kernel(decoder, cls_ref, x_ref, qkv_ref, joint_ref, shift_ref, x_out, qkv_out, new_ref):
    step = pl.program_id(0)

    @pl.when(step == 0)
    def _():
        new_ref[...] = (matmul(cls_ref[...], joint_ref[...]) + shift_ref[...]).astype(BF16).astype(F32)

    def put(old, new, out):
        spot = lax.broadcasted_iota(jnp.int32, new.shape, 0)
        row = jnp.sum(jnp.where(spot == step, new, 0.0), axis=0, keepdims=True)
        here = (spot == 0) & (decoder[0] == 1)
        out[...] = jnp.where(here, row, old.astype(F32)).astype(BF16)

    put(x_ref[...], cls_ref[...].astype(F32), x_out)
    put(qkv_ref[...], new_ref[...], qkv_out)


def place_first(decoder, cls, x, qkv, joint, shift, count):
    rows, width = x.shape[0] // count, x.shape[1]
    block = lambda n: pl.BlockSpec((PACK, n), lambda b, _: (b * rows // PACK, 0))
    return pl.pallas_call(
        place_kernel,
        grid_spec=pltpu.PrefetchScalarGridSpec(
            num_scalar_prefetch=1,
            grid=(count,),
            in_specs=[whole(cls), block(width), block(3 * width), whole(joint), whole(shift)],
            out_specs=[block(width), block(3 * width)],
            scratch_shapes=[pltpu.VMEM((PACK, 3 * width), F32)],
        ),
        out_shape=[jax.ShapeDtypeStruct(x.shape, BF16), jax.ShapeDtypeStruct(qkv.shape, BF16)],
        input_output_aliases={2: 0, 3: 1},
        compiler_params=pltpu.CompilerParams(vmem_limit_bytes=8 * MIB),
        name="place_first",
    )(decoder, cls, x, qkv, joint, shift)


def cls_grad_kernel(*refs, count):
    part_refs, one_refs, (joint_ref, out_ref) = refs[:count], refs[count : 2 * count], refs[2 * count :]
    width = out_ref.shape[1]
    total = packed(one_refs)
    for i in range(3):
        grad = packed([ref.at[i] for ref in part_refs]).astype(BF16)
        total = total + back_mul(grad, joint_ref[:, i * width : (i + 1) * width])
    out_ref[...] = total.astype(BF16)


def cls_back(parts, one, joint, count):
    rows, width = one.shape[0] // count, one.shape[1]
    part = lambda b: pl.BlockSpec((3, PACK, width), lambda *_: (0, b * rows // PACK, 0))
    return pl.pallas_call(
        functools.partial(cls_grad_kernel, count=count),
        grid=(1,),
        in_specs=[part(b) for b in range(count)]
        + [first_block(rows, width, b) for b in range(count)]
        + [whole(joint)],
        out_specs=pl.BlockSpec((PACK, width), lambda *_: (0, 0)),
        out_shape=jax.ShapeDtypeStruct((PACK, width), BF16),
        compiler_params=pltpu.CompilerParams(vmem_limit_bytes=48 * MIB),
        name="cls_back",
    )(*[parts] * count, *[one] * count, joint)


def first_back_kernel(lengths, grad_ref, *refs, count, rows, head_dim, chunk):
    kept = [packed(refs[i * count : (i + 1) * count]) for i in range(5)]
    normed_two, scale_two, slope, normed_one, scale_one = kept
    scale_two, scale_one = scale_two[:, 0:1], scale_one[:, 0:1]
    mixer_ref, expand_ref, contract_ref, gain_ref, qkv_ref, parts_ref = refs[5 * count : 5 * count + 6]
    branch_ref, hidden_ref, mixed_ref, one_ref, sums_ref, shift_sum_ref, out_ref, part_sums_ref = refs[5 * count + 6 :]
    width = grad_ref.shape[1]
    grad = grad_ref[...].astype(F32)
    sums_ref[...] = jnp.zeros_like(sums_ref)

    def add_sum(row, value):
        sums_ref[row : row + 1] = jnp.sum(value, axis=0, keepdims=True)

    add_sum(0, grad * normed_two)
    add_sum(1, grad)
    total = norm_back(grad * gain_ref[1:2], normed_two, scale_two)
    branch = total.astype(BF16)
    branch_ref[...] = branch
    add_sum(2, branch.astype(F32))
    for start in range(0, expand_ref.shape[1], chunk):
        part = slice(start, start + chunk)
        hidden = (back_mul(branch, contract_ref[part, :]) * slope[:, part]).astype(BF16)
        hidden_ref[:, part] = hidden
        shift_sum_ref[0:1, part] = jnp.sum(hidden.astype(F32), axis=0, keepdims=True)
        total = total + back_mul(hidden, expand_ref[:, part])
    add_sum(3, total * normed_one)
    add_sum(4, total)
    total = norm_back(total * gain_ref[0:1], normed_one, scale_one)
    one_ref[...] = total
    mixed = total.astype(BF16)
    mixed_ref[...] = mixed
    add_sum(5, mixed.astype(F32))
    ctx = back_mul(mixed, mixer_ref[...]).astype(BF16).astype(F32)
    for b in range(count):
        span = slice(b * rows, (b + 1) * rows)
        keys, values = qkv_ref[span, width : 2 * width], qkv_ref[span, 2 * width : 3 * width]
        query = qkv_ref[b * rows : b * rows + PACK, 0:width].astype(F32)[0:1] * head_dim**-0.5
        query = per_head(query, head_dim).astype(BF16)
        share = first_share(query, keys, lengths[b])
        ctx_heads = per_head(ctx[b : b + 1], head_dim).astype(BF16)
        share_grad = back_mul(ctx_heads, values)
        inner = jnp.sum(share * share_grad, axis=1, keepdims=True)
        score = (share * (share_grad - inner)).astype(BF16)
        query_grad = heads_joined(matmul(score, keys), head_dim) * head_dim**-0.5
        head_rows = parts_ref[0, b * rows : b * rows + PACK].astype(F32)
        top = lax.broadcasted_iota(jnp.int32, head_rows.shape, 0) == 0
        out_ref[0, span] = parts_ref[0, span]
        out_ref[0, b * rows : b * rows + PACK] = jnp.where(top, head_rows + query_grad, head_rows).astype(BF16)
        out_ref[1, span] = (parts_ref[1, span].astype(F32) + outer_sum(score, query)).astype(BF16)
        out_ref[2, span] = (parts_ref[2, span].astype(F32) + outer_sum(share.astype(BF16), ctx_heads)).astype(BF16)
    part_sums_ref[...] = jnp.zeros_like(part_sums_ref)
    for i in (0, 2):
        part_sums_ref[i : i + 1] = jnp.sum(out_ref[i].astype(F32), axis=0, keepdims=True)


def first_back(grad, kept, mats, gain, qkv, parts, lengths):
    count = lengths.shape[0]
    rows, width = qkv.shape[0] // count, grad.shape[1]
    hidden = mats[1].shape[1]
    blocks = [first_block(rows, array.shape[1], b) for array in kept for b in range(count)]
    rest = mats + (gain, qkv, parts)
    small = lambda n, kind, r=PACK: (pl.BlockSpec((r, n), lambda *_: (0, 0)), jax.ShapeDtypeStruct((r, n), kind))
    outs = [small(width, BF16), small(hidden, BF16), small(width, BF16), small(width, F32), small(width, F32, 8), small(hidden, F32, 1)]
    outs.append((whole(parts), jax.ShapeDtypeStruct(parts.shape, BF16)))
    outs.append(small(width, F32, 8))
    return pl.pallas_call(
        functools.partial(first_back_kernel, count=count, rows=rows, head_dim=width // HEADS, chunk=768),
        grid_spec=pltpu.PrefetchScalarGridSpec(
            num_scalar_prefetch=1,
            grid=(1,),
            in_specs=[whole(grad)] + blocks + [whole(r) for r in rest],
            out_specs=[spec for spec, _ in outs],
        ),
        out_shape=[shape for _, shape in outs],
        compiler_params=pltpu.CompilerParams(vmem_limit_bytes=32 * MIB),
        name="first_back",
    )(lengths, grad, *[array for array in kept for _ in range(count)], *rest)


def project_kernel(x_ref, joint_ref, shift_ref, out_ref):
    out_ref[...] = (matmul(x_ref[...], joint_ref[...]) + shift_ref[...]).astype(BF16)


def project(x, joint, shift):
    rows, width = x.shape
    step = min(256, rows)
    return pl.pallas_call(
        project_kernel,
        grid=(rows // step,),
        in_specs=[pl.BlockSpec((step, width), lambda i: (i, 0)), whole(joint), whole(shift)],
        out_specs=pl.BlockSpec((step, joint.shape[1]), lambda i: (i, 0)),
        out_shape=jax.ShapeDtypeStruct((rows, joint.shape[1]), BF16),
        compiler_params=pltpu.CompilerParams(vmem_limit_bytes=16 * MIB),
        name="project",
    )(x, joint, shift)


def input_grad_kernel(decoder, parts_ref, one_ref, first_ref, joint_ref, out_ref, *, step, rows):
    i = pl.program_id(0)
    width = out_ref.shape[1]

    total = one_ref[...]
    for j in range(3):
        total = total + back_mul(parts_ref[j], joint_ref[:, j * width : (j + 1) * width])
    out_ref[...] = total

    @pl.when(lax.rem(i * step, rows) == 0)
    def _():
        spot = lax.broadcasted_iota(jnp.int32, first_ref.shape, 0)
        row = jnp.sum(jnp.where(spot == i * step // rows, first_ref[...], 0.0), axis=0, keepdims=True)
        head = total[0:8]
        keep = jnp.where(decoder[0] == 1, 0.0, 1.0)
        top = lax.broadcasted_iota(jnp.int32, head.shape, 0) == 0
        out_ref[0:8] = jnp.where(top, (head + row) * keep, head)


def input_gradient(decoder, parts, one, one_first, joint, count):
    total_rows, width = one.shape
    rows = total_rows // count
    step = min(256, rows)
    return pl.pallas_call(
        functools.partial(input_grad_kernel, step=step, rows=rows),
        grid_spec=pltpu.PrefetchScalarGridSpec(
            num_scalar_prefetch=1,
            grid=(total_rows // step,),
            in_specs=[
                pl.BlockSpec((3, step, width), lambda i, _: (0, i, 0)),
                pl.BlockSpec((step, width), lambda i, _: (i, 0)),
                whole(one_first),
                whole(joint),
            ],
            out_specs=pl.BlockSpec((step, width), lambda i, _: (i, 0)),
        ),
        out_shape=jax.ShapeDtypeStruct(one.shape, F32),
        compiler_params=pltpu.CompilerParams(vmem_limit_bytes=48 * MIB),
        name="input_gradient",
    )(decoder, parts, one, one_first, joint)


def weight_grad_kernel(place, left_ref, right_ref, *refs):
    keep_ref, send_ref = refs[-2:]
    own, rows, _ = keep_ref.shape
    total = outer_sum(left_ref[...], right_ref[0]).astype(BF16)
    odd = lax.rem(place[0], 2) == 1
    for i in range(own):
        pair = [total[(2 * i + j) * rows : (2 * i + j + 1) * rows] for j in range(2)]
        keep_ref[i] = jnp.where(odd, pair[1], pair[0])
        send_ref[i] = jnp.where(odd, pair[0], pair[1])


def weight_grads(place, *pairs, tile=768):
    groups = lax.axis_size("dp")
    pairs = [(left, right if right.ndim == 3 else right[None]) for left, right in pairs]
    width = min(right.shape[2] for _, right in pairs)
    sizes = [left.shape[1] // groups for left, _ in pairs]
    heights = [size * right.shape[0] * right.shape[2] // width for size, (_, right) in zip(sizes, pairs)]
    if any(size % 16 for size in sizes):
        blocks = []
        for size, (left, right) in zip(sizes, pairs):
            total = jnp.concatenate([outer_sum(left, r) for r in right], axis=1).astype(BF16)
            total = total.reshape(groups, size, -1, width).transpose(0, 2, 1, 3)
            blocks.append(total.reshape(groups // 2, 2, -1, width))
        blocks = jnp.concatenate(blocks, axis=2)
        odd = lax.rem(place, 2)
        return tuple(lax.dynamic_index_in_dim(blocks, i, 1, False) for i in (odd, 1 - odd))
    shape = jax.ShapeDtypeStruct((groups // 2, sum(heights), width), BF16)
    done = []
    for i, (size, (left, right)) in enumerate(zip(sizes, pairs)):
        rows, height = left.shape
        cuts = right.shape[2] // width
        first = sum(heights[:i]) // size
        spec = pl.BlockSpec((tile // size // 2, size, width), lambda j, i, _, first=first: (i, first + j, 0))
        done = pl.pallas_call(
            weight_grad_kernel,
            grid_spec=pltpu.PrefetchScalarGridSpec(
                num_scalar_prefetch=1,
                grid=(right.shape[0] * cuts, height // tile),
                in_specs=[
                    pl.BlockSpec((rows, tile), lambda j, i, _: (0, i)),
                    pl.BlockSpec((1, rows, width), lambda j, i, _, cuts=cuts: (j // cuts, 0, j % cuts)),
                ]
                + [pl.BlockSpec(memory_space=pl.ANY)] * len(done),
                out_specs=[spec, spec],
            ),
            out_shape=[shape, shape],
            input_output_aliases={3: 0, 4: 1} if done else {},
            compiler_params=pltpu.CompilerParams(vmem_limit_bytes=48 * MIB),
            name="weight_grad",
        )(place.reshape(1), left, right, *done)
    return tuple(done)


def unstacked(total, shapes):
    parts = []
    start = 0
    for rows, columns in shapes:
        height = rows * columns // total.shape[1]
        part = total[start : start + height].reshape(-1, rows, total.shape[1])
        parts.append(part.transpose(1, 0, 2).reshape(rows, columns))
        start += height
    return parts


def add_split_kernel(mine, keep_a, got_a, keep_b, got_b, keep_ref, send_ref):
    keep_ref[...] = (keep_a[...].astype(F32) + got_a[...].astype(F32)).astype(BF16)
    send_ref[...] = (keep_b[...].astype(F32) + got_b[...].astype(F32)).astype(BF16)


def add_split(keep, got, axis, mine):
    rows, width = keep.shape[-2:]
    if rows % 16:
        total = (keep.astype(F32) + got.astype(F32)).astype(BF16)
        return tuple(lax.dynamic_index_in_dim(total, i, axis, False) for i in (mine, 1 - mine))
    rest = keep.shape[:axis] + keep.shape[axis + 1 : -2]
    before = 2**axis
    after = 2 ** (len(rest) - axis)
    shaped = [array.reshape(before, 2, after, rows, width) for array in (keep, got)]
    block = lambda other: pl.BlockSpec(
        (before, None, after, rows, min(width, 768)), lambda j, m: (0, (1 - m[0]) if other else m[0], 0, 0, j)
    )
    out = pl.BlockSpec((before, after, rows, min(width, 768)), lambda j, m: (0, 0, 0, j))
    shape = jax.ShapeDtypeStruct((before, after, rows, width), BF16)
    keep, send = pl.pallas_call(
        add_split_kernel,
        grid_spec=pltpu.PrefetchScalarGridSpec(
            num_scalar_prefetch=1,
            grid=(width // min(width, 768),),
            in_specs=[block(False), block(False), block(True), block(True)],
            out_specs=[out, out],
        ),
        out_shape=[shape, shape],
        compiler_params=pltpu.CompilerParams(vmem_limit_bytes=48 * MIB),
        name="add_split",
    )(mine.reshape(1), *shaped, *shaped)
    return keep.reshape(rest + (rows, width)), send.reshape(rest + (rows, width))


def first_hop(pair):
    keep, send = pair
    axes = tuple(reversed(bits_of(lax.axis_size("dp"))))[:-1]
    shape = (2,) * len(axes) + keep.shape[1:]
    return keep.reshape(shape), swapped(send, 1).reshape(shape), axes


def added(state, bit):
    keep, got, axes = state
    axis = axes.index(bit)
    mine = jnp.where((lax.axis_index("dp") & bit) == 0, 0, 1)
    return (*add_split(keep, got, axis, mine), axes[:axis] + axes[axis + 1 :])


def sent(halves, bit):
    keep, send, axes = halves
    return keep, swapped(send, bit), axes


def rest_of(state, order):
    for bit in order:
        state = sent(added(state, bit), bit)
    return state[0].astype(F32) + state[1].astype(F32)


def as_row(column):
    return jnp.broadcast_to(column, (column.shape[0], LANES)).T[0:1]


def as_column(row):
    return jnp.broadcast_to(row, (LANES, row.shape[1])).T[:, 0:1]


def word_cuts(slice_rows):
    size = 768
    return [
        (i, slice(start, min(start + size, slice_rows)), slice(i * slice_rows + start, i * slice_rows + min(start + size, slice_rows)))
        for i in range(2)
        for start in range(0, slice_rows, size)
    ]


def join(section, mine_ref, other_ref, out_ref):
    @pl.when(pl.program_id(0) == 0)
    def _():
        half = mine_ref.shape[0]
        out_ref[pl.ds(pl.multiple_of(section * half, 16), half)] = mine_ref[...]
        out_ref[pl.ds(pl.multiple_of((1 - section) * half, 16), half)] = other_ref[...]


def word_kernel(section, head_ref, own_ref, mine_ref, other_ref, shift_ref, peak_ref, total_ref, scores_ref, far_ref):
    join(section[0], mine_ref, other_ref, far_ref)
    group, picks, _ = head_ref.shape
    width = own_ref.shape[1]
    rows = group * picks
    head = head_ref[:, :, 0:width].reshape(rows, width)
    peak = jnp.full((rows, 1), -jnp.inf, F32)
    cuts = word_cuts(own_ref.shape[0])
    for table, part, columns in cuts:
        scores = back_mul(head, (own_ref, far_ref)[table][part]) + shift_ref[0:1, columns]
        scores_ref[:, columns] = scores
        peak = jnp.maximum(peak, jnp.max(scores, axis=1, keepdims=True))
    total = jnp.zeros_like(peak)
    for _, _, columns in cuts:
        total = total + jnp.sum(jnp.exp(scores_ref[:, columns] - peak), axis=1, keepdims=True)
    for g in range(group):
        part = slice(g * picks, (g + 1) * picks)
        peak_ref[g] = as_row(peak[part])
        total_ref[g] = as_row(total[part])


def word_scores(section, head, own, mine, other, shift, group=4):
    near, picks, padded = head.shape
    vocab = shift.shape[1]
    row = pl.BlockSpec((group, 1, picks), lambda k, _: (k, 0, 0))
    row_shape = jax.ShapeDtypeStruct((near, 1, picks), F32)
    return pl.pallas_call(
        word_kernel,
        grid_spec=pltpu.PrefetchScalarGridSpec(
            num_scalar_prefetch=1,
            grid=(near // group,),
            in_specs=[pl.BlockSpec((group, picks, padded), lambda k, _: (k, 0, 0))]
            + [whole(array) for array in (own, mine, other, shift)],
            out_specs=[row, row],
            scratch_shapes=[pltpu.VMEM((group * picks, vocab), F32), pltpu.VMEM(own.shape, BF16)],
        ),
        out_shape=[row_shape] * 2,
        compiler_params=pltpu.CompilerParams(vmem_limit_bytes=48 * MIB),
        name="word_scores",
    )(section, head, own, mine, other, shift)


def logit_kernel(place, head_ref, *refs, wholes):
    pairs = len(wholes)
    tables = refs[: sum(1 if w else 2 for w in wholes)]
    shift_ref, logit_ref, *joined = refs[len(tables) :]
    group, picks, _ = head_ref.shape
    width = tables[0].shape[1]
    head = head_ref[:, :, 0:width].reshape(group * picks, width)
    slice_rows = shift_ref.shape[1] // pairs
    for i, is_whole in enumerate(wholes):
        table_ref, *tables = tables
        if not is_whole:
            mine_ref, (other_ref, *tables) = table_ref, tables
            table_ref, *joined = joined
            join(place[1], mine_ref, other_ref, table_ref)
        columns = slice(i * slice_rows, (i + 1) * slice_rows)
        scores = (back_mul(head, table_ref[...]) + shift_ref[0:1, columns]).astype(BF16)
        for g in range(group):
            spot = jnp.bitwise_xor(lax.rem(place[0], group), g)
            logit_ref[spot, :, columns] = scores[g * picks : (g + 1) * picks]


def word_logits(place, head, tables, shift, group=4):
    near, picks, padded = head.shape
    vocab = shift.shape[1]
    slice_rows = vocab // len(tables)
    quarter = near // 2
    wholes = tuple(len(table) == 1 for table in tables)
    arrays = [array for table in tables for array in table]
    spot = lambda k, p: (jnp.bitwise_xor(lax.rem(p[0], quarter) // group, k), 0, 0)
    return pl.pallas_call(
        functools.partial(logit_kernel, wholes=wholes),
        grid_spec=pltpu.PrefetchScalarGridSpec(
            num_scalar_prefetch=1,
            grid=(quarter // group,),
            in_specs=[pl.BlockSpec((group, picks, padded), lambda k, _: (k, 0, 0))]
            + [whole(array) for array in arrays + [shift]],
            out_specs=pl.BlockSpec((group, picks, vocab), spot),
            scratch_shapes=[pltpu.VMEM((slice_rows, arrays[0].shape[1]), BF16)] * (len(tables) - sum(wholes)),
        ),
        out_shape=jax.ShapeDtypeStruct((quarter, picks, vocab), BF16),
        compiler_params=pltpu.CompilerParams(vmem_limit_bytes=48 * MIB),
        name="word_logits",
    )(place, head, *arrays, shift)


def labels_of(head_ref, width):
    label = head_ref[:, :, width:].astype(F32)
    label = label.reshape(-1, label.shape[2])
    return (label[:, 0:1] * 256.0 + label[:, 1:2]).astype(jnp.int32)


def word_back_kernel(first, head_ref, log_ref, own_ref, mine_ref, other_ref, shift_ref, grad_ref, out_ref, hit_ref, far_ref, *, masked):
    join(first[2], mine_ref, other_ref, far_ref)
    group, picks, width = out_ref.shape
    rows = group * picks
    label = labels_of(head_ref, width)
    logs = jnp.concatenate([as_column(log_ref[g]) for g in range(group)])
    head = head_ref[:, :, 0:width].reshape(rows, width)
    total = jnp.zeros((rows, width), F32)
    hit = jnp.zeros((rows, 1), F32)
    for table, part, columns in word_cuts(own_ref.shape[0]):
        words = (own_ref, far_ref)[table][part]
        scores = back_mul(head, words) + shift_ref[0:1, columns]
        share = jnp.exp(scores - logs)
        mine = lax.broadcasted_iota(jnp.int32, share.shape, 1) == label - (first[table] + part.start)
        hit = hit + jnp.sum(jnp.where(mine, scores, 0.0), axis=1, keepdims=True)
        grad = (jnp.where(mine, share - 1.0, share) * (1.0 / masked)).astype(BF16)
        if table == 0:
            grad_ref[:, :, columns] = grad.reshape(group, picks, -1)
        total = total + matmul(grad, words)
    out_ref[...] = total.astype(BF16).reshape(group, picks, width)
    for g in range(group):
        hit_ref[g] = as_row(hit[g * picks : (g + 1) * picks])


def word_back(first, head, logs, own, mine, other, shift, masked, group=4):
    near, picks, padded = head.shape
    width = own.shape[1]
    vocab = shift.shape[1]
    block = lambda n: pl.BlockSpec((group, picks, n), lambda k, _: (k, 0, 0))
    row = pl.BlockSpec((group, 1, picks), lambda k, _: (k, 0, 0))
    return pl.pallas_call(
        functools.partial(word_back_kernel, masked=masked),
        grid_spec=pltpu.PrefetchScalarGridSpec(
            num_scalar_prefetch=1,
            grid=(near // group,),
            in_specs=[block(padded), row] + [whole(array) for array in (own, mine, other, shift)],
            out_specs=[block(vocab // 2), block(width), row],
            scratch_shapes=[pltpu.VMEM(own.shape, BF16)],
        ),
        out_shape=[
            jax.ShapeDtypeStruct((near, picks, vocab // 2), BF16),
            jax.ShapeDtypeStruct((near, picks, width), BF16),
            jax.ShapeDtypeStruct((near, 1, picks), F32),
        ],
        compiler_params=pltpu.CompilerParams(vmem_limit_bytes=48 * MIB),
        name="word_back",
    )(first, head, logs, own, mine, other, shift)


def table_kernel(first, grad_ref, head_ref, other_ref, log_ref, own_ref, shift_ref, out_ref, sums_ref, total_ref, *, masked):
    @pl.when(pl.program_id(0) == 0)
    def _():
        total_ref[...] = jnp.zeros_like(total_ref)
        sums_ref[...] = jnp.zeros_like(sums_ref)

    group, picks, slice_rows = grad_ref.shape
    rows = group * picks
    width = own_ref.shape[1]
    label = labels_of(other_ref, width)
    logs = jnp.concatenate([as_column(log_ref[g]) for g in range(group)])
    head = head_ref[:, :, 0:width].reshape(rows, width)
    other = other_ref[:, :, 0:width].reshape(rows, width)
    for table, part, columns in word_cuts(slice_rows):
        if table == 0:
            share = jnp.exp(back_mul(other, own_ref[part]) + shift_ref[0:1, columns] - logs)
            mine = lax.broadcasted_iota(jnp.int32, share.shape, 1) == label - (first[0] + part.start)
            other_grad = (jnp.where(mine, share - 1.0, share) * (1.0 / masked)).astype(BF16)
            grad = grad_ref[:, :, part].reshape(rows, -1)
            sums_ref[0:1, part] += jnp.sum(grad.astype(F32) + other_grad.astype(F32), axis=0, keepdims=True)
            total_ref[part] += outer_sum(grad, head) + outer_sum(other_grad, other)

    @pl.when(pl.program_id(0) == pl.num_programs(0) - 1)
    def _():
        out_ref[...] = total_ref[...].astype(BF16)


def table_gradient(first, grad, head, other, logs, own, shift, masked, group=4):
    near, picks, slice_rows = grad.shape
    padded, width = head.shape[2], own.shape[1]
    block = lambda n: pl.BlockSpec((group, picks, n), lambda k, _: (k, 0, 0))
    row = pl.BlockSpec((group, 1, picks), lambda k, _: (k, 0, 0))
    return pl.pallas_call(
        functools.partial(table_kernel, masked=masked),
        grid_spec=pltpu.PrefetchScalarGridSpec(
            num_scalar_prefetch=1,
            grid=(near // group,),
            in_specs=[block(slice_rows), block(padded), block(padded), row, whole(own), whole(shift)],
            out_specs=[pl.BlockSpec(own.shape, lambda k, _: (0, 0)), pl.BlockSpec((1, slice_rows), lambda k, _: (0, 0))],
            scratch_shapes=[pltpu.VMEM(own.shape, F32)],
        ),
        out_shape=[jax.ShapeDtypeStruct(own.shape, BF16), jax.ShapeDtypeStruct((1, slice_rows), F32)],
        compiler_params=pltpu.CompilerParams(vmem_limit_bytes=48 * MIB),
        name="table_gradient",
    )(first, grad, head, other, logs, own, shift)


def assemble_kernel(place, near_ref, side_ref, out_ref, *, quarter):
    turn = jnp.bitwise_xor(place[0] // quarter, pl.program_id(0))
    for side, ref in enumerate((near_ref, side_ref)):

        @pl.when(turn % 2 == side)
        def _():
            for i in range(ref.shape[0]):
                out_ref[:, i * ref.shape[2] : (i + 1) * ref.shape[2]] = ref[i]


def assembled(place, nears, sides):
    quarter, picks, vocab = nears.shape
    slice_rows = vocab // 2
    if slice_rows % LANES:
        parts = jnp.stack([array.reshape(quarter, picks, 2, slice_rows) for array in (nears, sides)], axis=3)
        parts = parts.reshape(quarter, picks, 4, slice_rows)
        parts = jnp.take(parts, jnp.bitwise_xor(jnp.arange(4), place // quarter), axis=2)
        return parts.transpose(1, 2, 0, 3).reshape(picks, 2 * quarter * vocab)

    together = 2
    steps = quarter // together

    def spec(side):
        def index(b, j, p):
            turn = jnp.bitwise_xor(p[0] // quarter, b)
            last = jnp.bitwise_xor(p[0] // quarter, jnp.bitwise_xor(b, 1)) // 2
            first_of_pair = lax.rem(b, 2) == 0
            return (
                jnp.where(lax.rem(turn, 2) == side, j, jnp.where(first_of_pair, 0, steps - 1)),
                0,
                jnp.where(lax.rem(turn, 2) == side, turn // 2, last),
            )

        return pl.BlockSpec((together, picks, slice_rows), index)

    return pl.pallas_call(
        functools.partial(assemble_kernel, quarter=quarter),
        grid_spec=pltpu.PrefetchScalarGridSpec(
            num_scalar_prefetch=1,
            grid=(4, steps),
            in_specs=[spec(0), spec(1)],
            out_specs=pl.BlockSpec((picks, together * slice_rows), lambda b, j, _: (0, b * steps + j)),
        ),
        out_shape=jax.ShapeDtypeStruct((picks, 2 * quarter * vocab), BF16),
        compiler_params=pltpu.CompilerParams(vmem_limit_bytes=48 * MIB),
        name="assemble",
    )(place.reshape(1), nears, sides)


def on_device(
    embedded,
    lengths,
    positions,
    labels,
    joint_weight,
    mixer_weight,
    expand_weight,
    contract_weight,
    head_weight,
    gains,
    biases,
    expand_bias,
    word_table,
    word_bias,
):
    section = lax.axis_index("section")
    place = lax.axis_index("dp")
    groups = lax.axis_size("dp")
    decoder = section == 1
    count, rows, width = embedded.shape[1:]
    total_rows = count * rows
    head_dim = width // HEADS
    masked = positions.shape[-1]
    picks = count * masked
    joint = joint_weight[0]
    mats = (mixer_weight[0], expand_weight[0], contract_weight[0])
    head_matrix = head_weight[0]
    gain = gains[0]
    bias = biases[0]
    shift = expand_bias
    slice_rows = word_table.shape[0]

    flag = section.astype(jnp.int32).reshape(1)
    place32 = place.astype(jnp.int32)
    units = shift.shape[1]
    own = width // groups
    near, quarter = groups // 2, groups // 4
    half = slice_rows // 2
    bits = bits_of(groups)
    order = bits[-2:-1] + bits[1:-2] + bits[-1:]
    turned = bits[1:]
    across = lambda array: lax.ppermute(array, "section", [(0, 1), (1, 0)])

    my_half = lax.dynamic_slice_in_dim(word_table, section * half, half)
    far_one, far_two = (swapped(piece, near) for piece in (my_half[: half // 2], my_half[half // 2 :]))
    side_half = swapped(my_half, quarter)

    x = embedded[0].reshape(total_rows, width)
    joint_shift = jnp.concatenate([bias[0], jnp.zeros((width,), F32), bias[1]])[None]
    qkv = project(x, joint, joint_shift)
    cls_out = cls_forward(x, qkv, lengths, mats, gain, bias, shift)
    cls_in = passed_along(cls_out, "section", 1)
    x, qkv = place_first(flag, cls_in, x, qkv, joint, joint_shift, count)
    ctx, logs = attend(qkv, lengths, count)
    ctx, far_one = tied(ctx, far_one)
    far_one_other = across(far_one)
    far_shift = swapped(word_bias, near)
    side_shift = swapped(word_bias, quarter)
    y, normed_one, scale_one, first_low, active, slope, normed_two, scale_two = layer_tail(
        ctx, x, mats, gain, bias, shift
    )
    y, far_one_other, far_two, far_shift, side_shift, side_half = tied(
        y, far_one_other, far_two, far_shift, side_shift, side_half
    )
    far_two_other = across(far_two)
    far_mine = jnp.concatenate([far_one, far_two])
    side_far_shift = swapped(far_shift, quarter)

    chosen = positions[0][:, :, None] == jnp.arange(rows)[None, None, :]
    picked = jnp.einsum(
        "bml,blw->bmw", chosen.astype(BF16), y.reshape(count, rows, width), preferred_element_type=F32
    )
    picked_low = picked.astype(BF16).reshape(picks, width)
    dense = matmul(picked_low, head_matrix) + bias[6]
    dense_active, dense_slope = gelu_and_slope(dense)
    normed_head, scale_head = normalise(dense_active)
    head_low = (normed_head * gain[2] + bias[7]).astype(BF16)
    answers = labels[0].reshape(-1, 1)
    answers = jnp.concatenate([answers // 256, answers % 256, jnp.zeros((picks, LANES - 2), jnp.int32)], axis=1)
    head_low = jnp.concatenate([head_low, answers.astype(BF16)], axis=1)
    head_all, head_low, far_two_other, side_far_shift = tied(
        gather_chips(head_low), head_low, far_two_other, side_far_shift
    )
    head_all = gather_cores(head_all)
    head_other = swapped(head_low, near)
    far_other = jnp.concatenate([far_one_other, far_two_other])
    word_shift = jnp.concatenate([word_bias, far_shift]).astype(F32)[None]
    side_word_shift = jnp.concatenate([side_shift, side_far_shift]).astype(F32)[None]
    where_to = jnp.stack([place32, section.astype(jnp.int32)])
    head_all, side_half = tied(head_all, side_half)
    side_half_other = across(side_half)
    peak, total = word_scores(flag, head_all, word_table, far_mine, far_other, word_shift)
    peak, head_other = tied(peak, head_other)
    grid = (2,) * (len(bits) - 1)
    peak, total = (array.reshape(grid + (picks,)) for array in (peak, total))
    for axis, bit in enumerate(reversed(bits[:-1])):
        other_peak, other_total = jnp.flip(swapped(jnp.stack([peak, total]), bit), axis + 1)
        top = jnp.maximum(peak, other_peak)
        total = total * jnp.exp(peak - top) + other_total * jnp.exp(other_peak - top)
        peak = top
    log_total = (peak + jnp.log(total)).reshape(near, 1, picks)
    log_other = swapped(log_total, near)
    head_other = gather_chips(head_other)
    first = (jnp.stack([place, jnp.bitwise_xor(place, near)]) * slice_rows).astype(jnp.int32)
    first = jnp.concatenate([first, flag])
    score_grad, head_back, hits = word_back(
        first, head_all, log_total, word_table, far_mine, far_other, word_shift, masked
    )
    head_back, side_half_other, head_other, log_other = tied(head_back, side_half_other, head_other, log_other)
    head_other = gather_cores(head_other)
    loss_part = jnp.sum(log_total[0]) - jnp.sum(hits)
    head_grad = scatter_near(head_back)
    table_grad, word_sums = table_gradient(
        first, score_grad, head_all, head_other, log_other, word_table, word_shift, masked
    )
    head_grad, table_grad, word_sums, far_mine = tied(head_grad, table_grad, word_sums, far_mine)
    word_other = across(word_sums)
    side_far_half = swapped(far_mine, quarter)
    exchanged = lambda part: lax.all_to_all(
        part, "dp", 0, 0, axis_index_groups=[list(range(i, i + quarter)) for i in range(0, groups, quarter)]
    )
    logits_near = word_logits(where_to, head_all, ((word_table,), (far_mine, far_other)), word_shift)
    head_grad, logits_near = tied(head_grad, logits_near)
    logits_near = exchanged(logits_near)

    gain_head = jnp.sum(head_grad * normed_head, 0)
    shift_head = jnp.sum(head_grad, 0)
    dense_grad = (norm_back(head_grad * gain[2], normed_head, scale_head) * dense_slope).astype(BF16)
    dense_shift = jnp.sum(dense_grad, axis=0, dtype=F32)
    picked_grad = back_mul(dense_grad, head_matrix).reshape(count, masked, width)
    grad = jnp.einsum(
        "bml,bmw->blw", chosen.astype(F32), picked_grad, precision=lax.Precision.HIGHEST
    ).reshape(total_rows, width)

    kept = (normed_two, scale_two, slope, normed_one, scale_one)
    branch, hidden, one, mixed, ctx_grad, sums, shift_sum = tail_back(grad, kept, mats, gain)
    hidden, branch, side_far_half, word_other = tied(hidden, branch, side_far_half, word_other)
    side_far_other = across(side_far_half)
    one_pair = weight_grads(place32, (active, branch), (ctx, mixed))
    hidden, one_pair = tied(hidden, one_pair)
    one_state = first_hop(one_pair)
    two_pair = weight_grads(place32, (first_low, hidden), (picked_low, dense_grad))
    ctx_grad, two_pair, logits_near = tied(ctx_grad, two_pair, logits_near)
    two_state = first_hop(two_pair)
    one_halves, two_halves = added(one_state, order[0]), added(two_state, turned[0])
    ctx_grad, one_now, two_now = tied(ctx_grad, one_halves[:2], two_halves[:2])
    one_state, two_state = sent((*one_now, one_halves[2]), order[0]), sent((*two_now, two_halves[2]), turned[0])
    parts = attend_back(qkv, ctx_grad, logs, lengths)
    one_halves, two_halves = added(one_state, order[1]), added(two_state, turned[1])
    parts, one_now, two_now, side_far_other = tied(parts, one_halves[:2], two_halves[:2], side_far_other)
    logits_side = word_logits(
        where_to, head_all, ((side_half, side_half_other), (side_far_half, side_far_other)), side_word_shift
    )
    one_state, two_state = sent((*one_now, one_halves[2]), order[1]), sent((*two_now, two_halves[2]), turned[1])
    logits_side = exchanged(logits_side)
    cls_grad = passed_along(cls_back(parts, one, joint, count), "section", -1)
    cls_grad, table_grad = tied(cls_grad, table_grad)
    table_top = across(table_grad[:half])

    branch_f, hidden_f, mixed_f, one_f, sums_f, shift_f, parts, part_sums = first_back(
        cls_grad, kept, mats, gain, qkv, parts, lengths
    )
    two_halves = added(two_state, turned[2])
    parts, two_now = tied(parts, two_halves[:2])
    two_state = sent((*two_now, two_halves[2]), turned[2])

    def firsts(array):
        return jnp.concatenate([array[b * rows : b * rows + 1] for b in range(count)])

    mine = jnp.concatenate(
        [firsts(active), firsts(first_low), firsts(ctx), branch_f[:count], hidden_f[:count], mixed_f[:count]],
        axis=1,
    )
    sums = sums + sums_f
    small = jnp.concatenate(
        [
            jnp.stack([sums[3], sums[0], gain_head]),
            jnp.stack(
                [part_sums[0], part_sums[2], sums[5], sums[4], sums[2], sums[1], dense_shift, shift_head]
            ),
            (shift_sum + shift_f).reshape(-1, width),
            jnp.broadcast_to(loss_part, (1, width)),
        ]
    )
    small_high = lax.reduce_precision(small, 8, 7)
    small_low = (small - small_high).astype(BF16)
    small_high = small_high.astype(BF16)
    mine = mine.reshape(-1, width)
    counts = [mine.shape[0], small.shape[0], small.shape[0]]
    gathered = jnp.concatenate([mine, small_high, small_low])[None]
    arriving = swapped(gathered, near)
    joint_pair = weight_grads(place32, (x, parts))
    parts, joint_pair, arriving, logits_side = tied(parts, joint_pair, arriving, logits_side)
    joint_state = first_hop(joint_pair)
    gathered = side_by_side(gathered, arriving, near)
    arriving = swapped(gathered, quarter)
    joint_halves = added(joint_state, order[0])
    parts, joint_now, arriving = tied(parts, joint_halves[:2], arriving)
    joint_state = sent((*joint_now, joint_halves[2]), order[0])
    bit = quarter
    for below in reversed(bits[:-2]):
        gathered = side_by_side(gathered, arriving, bit)
        arriving = swapped(gathered, below)
        bit = below
        if bit == 2:
            input_grad = input_gradient(flag, parts, one, one_f, joint, count)
            input_grad, logits_near, logits_side = tied(input_grad, logits_near, logits_side)
            logits_out = assembled(place32, logits_near, logits_side)
            logits_out, arriving = tied(logits_out, arriving)
    logits_out, one_got, table_top = tied(logits_out, one_state[1], table_top)
    table_rest = across(table_grad[half:])
    one_halves = added((one_state[0], one_got, one_state[2]), order[2])
    logits_out, one_now = tied(logits_out, one_halves[:2])
    one_state = sent((*one_now, one_halves[2]), order[2])
    joint_keep, joint_got, logits_out, input_grad, two_got = tied(
        *joint_state[:2], logits_out, input_grad, two_state[1]
    )
    two_state = two_state[0], two_got, two_state[2]
    joint_state = sent(added((joint_keep, joint_got, joint_state[2]), order[1]), order[1])
    expand_sum, head_sum = unstacked(rest_of(two_state, turned[3:]), [(own, units), (own, width)])
    joint_keep, joint_got, expand_sum, head_sum = tied(*joint_state[:2], expand_sum, head_sum)
    joint_keep, joint_send, axes = added((joint_keep, joint_got, joint_state[2]), order[2])
    joint_got = swapped(joint_send, order[2])
    joint_keep, arriving, one_got = tied(joint_keep, arriving, one_state[1])
    one_state = one_state[0], one_got, one_state[2]
    contract_sum, mixer_sum = unstacked(rest_of(one_state, order[3:]), [(units // groups, width), (own, width)])
    joint_got, table_rest = tied(joint_got, table_rest)
    joint_sum = unstacked(rest_of((joint_keep, joint_got, axes), order[3:]), [(own, 3 * width)])[0]
    table_total = table_grad.astype(F32) + jnp.concatenate([table_top, table_rest]).astype(F32)
    rows_all = side_by_side(gathered, arriving, 1)
    small = jnp.sum(rows_all[:, counts[0] :].astype(F32), axis=0)
    small = small[: counts[1]] + small[counts[1] :]
    rows_all = rows_all[:, : counts[0]].reshape(groups * count, -1)
    word_total = word_sums[0] + word_other[0]
    cuts = [units, width, width, width, units, width]
    starts = [sum(cuts[:i]) for i in range(len(cuts))]
    active_a, first_a, ctx_a, branch_a, hidden_a, mixed_a = (
        rows_all[:, s : s + n] for s, n in zip(starts, cuts)
    )

    def own_columns(array):
        size = array.shape[1] // groups
        return lax.dynamic_slice_in_dim(array, place * size, size, 1)

    contract_sum = contract_sum + outer_sum(own_columns(active_a), branch_a)
    expand_sum = expand_sum + outer_sum(own_columns(first_a), hidden_a)
    mixer_sum = mixer_sum + outer_sum(own_columns(ctx_a), mixed_a)

    loss = (small[-1, 0] / (picks * groups)).reshape(1)
    return (
        loss,
        logits_out.reshape(1, count, masked, -1),
        input_grad.reshape(1, count, rows, width),
        joint_sum[None],
        mixer_sum[None],
        expand_sum[None],
        contract_sum[None],
        head_sum[None],
        small[None, :3],
        small[None, 3:11],
        small[11:-1].reshape(1, -1),
        table_total,
        word_total,
    )


def solution(mesh):
    in_specs = (
        P("section", "dp", None, None),
        P("dp"),
        P("section", "dp", None),
        P("section", "dp", None),
        P("section", None, None),
        P("section", None, None),
        P("section", None, None),
        P("section", None, None),
        P("section", None, None),
        P("section", None, None),
        P("section", None, None),
        P("section", None),
        P("dp", None),
        P("dp"),
    )
    out_specs = (
        P("section"),
        P("section", "dp", None, None),
        P("section", "dp", None, None),
        P("section", "dp", None),
        P("section", "dp", None),
        P("section", "dp", None),
        P("section", "dp", None),
        P("section", "dp", None),
        P("section", None, None),
        P("section", None, None),
        P("section", None),
        P("dp", None),
        P("dp"),
    )
    return jax.shard_map(
        on_device, mesh=mesh, in_specs=in_specs, out_specs=out_specs, check_vma=False
    )
```

```python
import functools

import jax
import jax.numpy as jnp
from jax import lax
from jax.experimental import pallas as pl
from jax.experimental.pallas import tpu as pltpu
from jax.sharding import PartitionSpec as P

HEADS = 12
EPS = 1e-12
ROOT_HALF = 0.7071067811865476
INV_ROOT_TAU = 0.3989422804014327
HIDDEN = -1000000000.0
LANES = 128
MIB = 1024 * 1024
F32 = jnp.float32
BF16 = jnp.bfloat16


def product(left, right, left_dim, right_dim):
    return lax.dot_general(
        left, right, (((left_dim,), (right_dim,)), ((), ())), preferred_element_type=F32
    )


def matmul(left, right):
    return product(left, right, 1, 0)


def outer_sum(left, right):
    return product(left, right, 0, 0)


def back_mul(left, right):
    return product(left, right, 1, 1)


def passed_along(block, axis, distance):
    devices = range(lax.axis_size(axis))
    route = [(i - distance, i) for i in devices if i - distance in devices]
    return lax.ppermute(block, axis, route)


def swapped(block, bit):
    devices = range(lax.axis_size("dp"))
    return lax.ppermute(block, "dp", [(i, i ^ bit) for i in devices])


def bits_of(order):
    return [1 << i for i in range(order.bit_length() - 1)]


def tied(*values):
    return lax.optimization_barrier(values)


def side_by_side(blocks, other, bit):
    low = (lax.axis_index("dp") & bit) == 0
    pair = [jnp.where(low, blocks, other), jnp.where(low, other, blocks)]
    return jnp.stack(pair, axis=1).reshape((-1,) + blocks.shape[1:])


def gather_chips(block):
    return [block] + [swapped(block, mask) for mask in range(2, lax.axis_size("dp") // 2, 2)]


def gather_cores(blocks):
    blocks = jnp.stack(blocks)
    return jnp.stack([blocks, swapped(blocks, 1)], axis=1).reshape((-1,) + blocks.shape[1:])


def scatter_near(blocks):
    blocks = blocks.reshape((-1, 2) + blocks.shape[1:])
    got = swapped(blocks[:, 1], 1)
    blocks = (blocks[:, 0].astype(F32) + got.astype(F32)).astype(BF16)
    total = blocks[0].astype(F32)
    for i in range(1, blocks.shape[0]):
        total = total + swapped(blocks[i], 2 * i).astype(F32)
    return total


def normalise(resid):
    centre = resid - jnp.mean(resid, axis=-1, keepdims=True)
    scale_inv = lax.rsqrt(jnp.mean(centre * centre, axis=-1, keepdims=True) + EPS)
    return centre * scale_inv, scale_inv


def norm_back(scaled, normed, scale_inv):
    first_mean = jnp.mean(scaled, axis=-1, keepdims=True)
    second_mean = jnp.mean(scaled * normed, axis=-1, keepdims=True)
    return scale_inv * (scaled - first_mean - normed * second_mean)


def gelu_and_slope(value):
    gate = 0.5 * (1.0 + lax.erf(value * ROOT_HALF))
    return value * gate, gate + value * jnp.exp(-0.5 * value * value) * INV_ROOT_TAU


def attend_kernel(lengths, q_ref, k_ref, v_ref, out_ref, log_ref, *, head_dim):
    length = lengths[pl.program_id(0)]
    rows, lanes = q_ref.shape
    q = q_ref[...] * (head_dim**-0.5)
    k = k_ref[...]
    v_t = v_ref[...].T
    head_of = lax.broadcasted_iota(jnp.int32, (rows, lanes), 1) // head_dim
    half = rows // 2
    visible = lax.broadcasted_iota(jnp.int32, (rows - half, rows), 0) < length - half
    parts = []
    for head in range(lanes // head_dim):
        scores = back_mul(k, jnp.where(head_of == head, q, jnp.zeros_like(q)))
        scores = jnp.concatenate([scores[:half], jnp.where(visible, scores[half:], HIDDEN)])
        peak = jnp.max(scores, axis=0, keepdims=True)
        powers = jnp.exp(scores - peak)
        total = jnp.sum(powers, axis=0, keepdims=True)
        piece = matmul(v_t[head * head_dim : (head + 1) * head_dim], powers.astype(BF16))
        parts.append(piece / total)
        log_ref[0, head : head + 1, :] = peak + jnp.log(total)
    out_ref[...] = jnp.concatenate(parts, axis=0).T.astype(BF16)


def attend(qkv, lengths, count):
    rows = qkv.shape[0] // count
    width = qkv.shape[1] // 3
    pairs = width // LANES
    head_dim = width // HEADS
    block = lambda part: pl.BlockSpec((rows, LANES), lambda b, p, _: (b, part * pairs + p))
    return pl.pallas_call(
        functools.partial(attend_kernel, head_dim=head_dim),
        grid_spec=pltpu.PrefetchScalarGridSpec(
            num_scalar_prefetch=1,
            grid=(count, pairs),
            in_specs=[block(0), block(1), block(2)],
            out_specs=[
                pl.BlockSpec((rows, LANES), lambda b, p, _: (b, p)),
                pl.BlockSpec((1, LANES // head_dim, rows), lambda b, p, _: (b * pairs + p, 0, 0)),
            ],
        ),
        out_shape=[
            jax.ShapeDtypeStruct((count * rows, width), BF16),
            jax.ShapeDtypeStruct((count * pairs, LANES // head_dim, rows), F32),
        ],
        compiler_params=pltpu.CompilerParams(vmem_limit_bytes=48 * MIB),
        name="attend",
    )(lengths, qkv, qkv, qkv)


def attend_back_kernel(lengths, q_ref, k_ref, v_ref, grad_ref, log_ref, out_ref, *, head_dim):
    length = lengths[pl.program_id(0)]
    rows, lanes = q_ref.shape
    scale = head_dim**-0.5
    q = q_ref[...] * scale
    k = k_ref[...]
    v = v_ref[...]
    grad = grad_ref[...]
    head_of = lax.broadcasted_iota(jnp.int32, (rows, lanes), 1) // head_dim
    half = rows // 2
    visible = lax.broadcasted_iota(jnp.int32, (rows - half, rows), 0) < length - half
    totals = [jnp.zeros((rows, lanes), F32)] * 3
    for head in range(lanes // head_dim):
        mine = head_of == head
        scores = back_mul(k, jnp.where(mine, q, jnp.zeros_like(q)))
        share = jnp.exp(scores - log_ref[0, head : head + 1, :])
        share = jnp.concatenate([share[:half], jnp.where(visible, share[half:], 0.0)])
        share_grad = back_mul(jnp.where(mine, v, jnp.zeros_like(v)), grad)
        inner = jnp.sum(share * share_grad, axis=0, keepdims=True)
        score_grad = (share * (share_grad - inner)).astype(BF16)
        parts = (
            outer_sum(score_grad, k) * scale,
            matmul(score_grad, q),
            matmul(share.astype(BF16), grad),
        )
        totals = [jnp.where(mine, part, total) for part, total in zip(parts, totals)]
    for i, total in enumerate(totals):
        out_ref[i] = total.astype(BF16)


def attend_back(qkv, grad, logs, lengths):
    count = lengths.shape[0]
    rows = qkv.shape[0] // count
    width = qkv.shape[1] // 3
    pairs = width // LANES
    head_dim = width // HEADS
    block = lambda part: pl.BlockSpec((rows, LANES), lambda b, p, _: (b, part * pairs + p))
    return pl.pallas_call(
        functools.partial(attend_back_kernel, head_dim=head_dim),
        grid_spec=pltpu.PrefetchScalarGridSpec(
            num_scalar_prefetch=1,
            grid=(count, pairs),
            in_specs=[
                block(0),
                block(1),
                block(2),
                block(0),
                pl.BlockSpec((1, LANES // head_dim, rows), lambda b, p, _: (b * pairs + p, 0, 0)),
            ],
            out_specs=pl.BlockSpec((3, rows, LANES), lambda b, p, _: (0, b, p)),
        ),
        out_shape=jax.ShapeDtypeStruct((3, count * rows, width), BF16),
        compiler_params=pltpu.CompilerParams(vmem_limit_bytes=48 * MIB),
        name="attend_back",
    )(lengths, qkv, qkv, qkv, grad, logs)


def tail_kernel(
    ctx_ref, x_ref, mixer_ref, expand_ref, contract_ref, gain_ref, bias_ref, shift_ref,
    y_ref, normed_one_ref, scale_one_ref, first_ref, active_ref, slope_ref, normed_two_ref, scale_two_ref,
    *, chunk,
):
    mixed = matmul(ctx_ref[...], mixer_ref[...]) + bias_ref[2:3]
    normed, scale = normalise(x_ref[...].astype(F32) + mixed)
    first = normed * gain_ref[0:1] + bias_ref[3:4]
    first_low = first.astype(BF16)
    normed_one_ref[...] = normed.astype(BF16)
    scale_one_ref[...] = jnp.broadcast_to(scale, scale_one_ref.shape)
    first_ref[...] = first_low
    total = first + bias_ref[4:5]
    for start in range(0, expand_ref.shape[1], chunk):
        part = slice(start, start + chunk)
        hidden = matmul(first_low, expand_ref[:, part]) + shift_ref[0:1, part]
        active, slope = gelu_and_slope(hidden)
        active = active.astype(BF16)
        active_ref[:, part] = active
        slope_ref[:, part] = slope.astype(BF16)
        total = total + matmul(active, contract_ref[part, :])
    normed, scale = normalise(total)
    normed_two_ref[...] = normed.astype(BF16)
    scale_two_ref[...] = jnp.broadcast_to(scale, scale_two_ref.shape)
    y_ref[...] = (normed * gain_ref[1:2] + bias_ref[5:6]).astype(BF16)


def whole(array):
    return pl.BlockSpec(array.shape, lambda *_: (0,) * array.ndim, pipeline_mode=pl.Buffered(1))


def layer_tail(ctx, x, mats, gain, bias, shift, step=256, chunk=3072):
    rows, width = x.shape
    hidden = shift.shape[1]
    step = min(step, rows)
    by_row = lambda n: pl.BlockSpec((step, n), lambda i: (i, 0))
    shape = lambda n, kind: jax.ShapeDtypeStruct((rows, n), kind)
    widths = [(width, BF16), (width, BF16), (LANES, F32), (width, BF16), (hidden, BF16), (hidden, BF16), (width, BF16), (LANES, F32)]
    return pl.pallas_call(
        functools.partial(tail_kernel, chunk=min(chunk, hidden)),
        grid=(rows // step,),
        in_specs=[by_row(width), by_row(width)] + [whole(m) for m in mats + (gain, bias, shift)],
        out_specs=[by_row(n) for n, _ in widths],
        out_shape=[shape(n, kind) for n, kind in widths],
        compiler_params=pltpu.CompilerParams(vmem_limit_bytes=48 * MIB),
        name="layer_tail",
    )(ctx, x, *mats, gain, bias, shift)


def tail_back_kernel(
    grad_ref, normed_two_ref, scale_two_ref, slope_ref, normed_one_ref, scale_one_ref,
    mixer_ref, expand_ref, contract_ref, gain_ref,
    branch_ref, hidden_ref, one_ref, mixed_ref, ctx_ref, sums_ref, shift_sum_ref,
    *, chunk,
):
    @pl.when(pl.program_id(0) == 0)
    def _():
        sums_ref[...] = jnp.zeros_like(sums_ref)
        shift_sum_ref[...] = jnp.zeros_like(shift_sum_ref)

    def add_sum(row, value):
        sums_ref[row : row + 1] += jnp.sum(value, axis=0, keepdims=True)

    grad = grad_ref[...]
    normed = normed_two_ref[...].astype(F32)
    add_sum(0, grad * normed)
    add_sum(1, grad)
    total = norm_back(grad * gain_ref[1:2], normed, scale_two_ref[:, 0:1])
    branch = total.astype(BF16)
    branch_ref[...] = branch
    add_sum(2, branch.astype(F32))
    for start in range(0, expand_ref.shape[1], chunk):
        part = slice(start, start + chunk)
        hidden = back_mul(branch, contract_ref[part, :]) * slope_ref[:, part].astype(F32)
        hidden = hidden.astype(BF16)
        hidden_ref[:, part] = hidden
        shift_sum_ref[0:1, part] += jnp.sum(hidden.astype(F32), axis=0, keepdims=True)
        total = total + back_mul(hidden, expand_ref[:, part])
    normed = normed_one_ref[...].astype(F32)
    add_sum(3, total * normed)
    add_sum(4, total)
    total = norm_back(total * gain_ref[0:1], normed, scale_one_ref[:, 0:1])
    one_ref[...] = total
    mixed = total.astype(BF16)
    mixed_ref[...] = mixed
    add_sum(5, mixed.astype(F32))
    ctx_ref[...] = back_mul(mixed, mixer_ref[...]).astype(BF16)


def tail_back(grad, kept, mats, gain, step=256, chunk=3072):
    rows, width = grad.shape
    hidden = mats[1].shape[1]
    step = min(step, rows)
    by_row = lambda n: pl.BlockSpec((step, n), lambda i: (i, 0))
    shape = lambda n, kind: jax.ShapeDtypeStruct((rows, n), kind)
    widths = [(width, BF16), (hidden, BF16), (width, F32), (width, BF16), (width, BF16)]
    return pl.pallas_call(
        functools.partial(tail_back_kernel, chunk=min(chunk, hidden)),
        grid=(rows // step,),
        in_specs=[by_row(array.shape[1]) for array in (grad,) + kept] + [whole(m) for m in mats + (gain,)],
        out_specs=[by_row(n) for n, _ in widths]
        + [pl.BlockSpec((8, width), lambda i: (0, 0)), pl.BlockSpec((1, hidden), lambda i: (0, 0))],
        out_shape=[shape(n, kind) for n, kind in widths]
        + [jax.ShapeDtypeStruct((8, width), F32), jax.ShapeDtypeStruct((1, hidden), F32)],
        compiler_params=pltpu.CompilerParams(vmem_limit_bytes=48 * MIB),
        name="tail_back",
    )(grad, *kept, *mats, gain)


PACK = 16


def first_block(rows, width, passage):
    return pl.BlockSpec((PACK, width), lambda *_: (passage * rows // PACK, 0))


def packed(refs):
    rows = [ref[...].astype(F32)[0:1] for ref in refs]
    place = lax.broadcasted_iota(jnp.int32, (PACK, rows[0].shape[1]), 0)
    total = jnp.zeros((PACK, rows[0].shape[1]), F32)
    for i, row in enumerate(rows):
        total = jnp.where(place == i, row, total)
    return total


def per_head(row, head_dim):
    shape = (PACK, row.shape[1])
    mine = lax.broadcasted_iota(jnp.int32, shape, 1) // head_dim == lax.broadcasted_iota(jnp.int32, shape, 0)
    return jnp.where(mine, row, 0.0)


def heads_joined(block, head_dim):
    mine = lax.broadcasted_iota(jnp.int32, block.shape, 1) // head_dim == lax.broadcasted_iota(jnp.int32, block.shape, 0)
    return jnp.sum(jnp.where(mine, block, 0.0), axis=0, keepdims=True)


def first_share(query, keys, length):
    scores = back_mul(query, keys)
    visible = lax.broadcasted_iota(jnp.int32, scores.shape, 1) < length
    scores = jnp.where(visible, scores, HIDDEN)
    powers = jnp.exp(scores - jnp.max(scores, axis=1, keepdims=True))
    return powers / jnp.sum(powers, axis=1, keepdims=True)


def cls_kernel(lengths, *refs, count, rows, head_dim, chunk):
    x_refs, (qkv_ref, mixer_ref, expand_ref, contract_ref, gain_ref, bias_ref, shift_ref, out_ref) = (
        refs[:count],
        refs[count:],
    )
    width = out_ref.shape[1]
    x = packed(x_refs)
    place = lax.broadcasted_iota(jnp.int32, (PACK, width), 0)
    ctx = jnp.zeros((PACK, width), F32)
    for b in range(count):
        base = b * rows
        query = qkv_ref[base : base + PACK, 0:width].astype(F32)[0:1] * head_dim**-0.5
        query = per_head(query, head_dim).astype(BF16)
        share = first_share(query, qkv_ref[base : base + rows, width : 2 * width], lengths[b])
        mixed = matmul(share.astype(BF16), qkv_ref[base : base + rows, 2 * width : 3 * width])
        ctx = jnp.where(place == b, heads_joined(mixed, head_dim), ctx)
    mixed = matmul(ctx.astype(BF16), mixer_ref[...]) + bias_ref[2:3]
    first = normalise(x + mixed)[0] * gain_ref[0:1] + bias_ref[3:4]
    first_low = first.astype(BF16)
    total = first + bias_ref[4:5]
    for start in range(0, expand_ref.shape[1], chunk):
        part = slice(start, start + chunk)
        active, _ = gelu_and_slope(matmul(first_low, expand_ref[:, part]) + shift_ref[0:1, part])
        total = total + matmul(active.astype(BF16), contract_ref[part, :])
    out_ref[...] = (normalise(total)[0] * gain_ref[1:2] + bias_ref[5:6]).astype(BF16)


def cls_forward(x, qkv, lengths, mats, gain, bias, shift):
    count = lengths.shape[0]
    rows, width = x.shape[0] // count, x.shape[1]
    rest = (qkv,) + mats + (gain, bias, shift)
    return pl.pallas_call(
        functools.partial(cls_kernel, count=count, rows=rows, head_dim=width // HEADS, chunk=768),
        grid_spec=pltpu.PrefetchScalarGridSpec(
            num_scalar_prefetch=1,
            grid=(1,),
            in_specs=[first_block(rows, width, b) for b in range(count)] + [whole(r) for r in rest],
            out_specs=pl.BlockSpec((PACK, width), lambda *_: (0, 0)),
        ),
        out_shape=jax.ShapeDtypeStruct((PACK, width), BF16),
        compiler_params=pltpu.CompilerParams(vmem_limit_bytes=26 * MIB),
        name="cls_forward",
    )(lengths, *[x] * count, *rest)


def place_kernel(decoder, cls_ref, x_ref, qkv_ref, joint_ref, shift_ref, x_out, qkv_out, new_ref):
    step = pl.program_id(0)

    @pl.when(step == 0)
    def _():
        new_ref[...] = (matmul(cls_ref[...], joint_ref[...]) + shift_ref[...]).astype(BF16).astype(F32)

    def put(old, new, out):
        spot = lax.broadcasted_iota(jnp.int32, new.shape, 0)
        row = jnp.sum(jnp.where(spot == step, new, 0.0), axis=0, keepdims=True)
        here = (spot == 0) & (decoder[0] == 1)
        out[...] = jnp.where(here, row, old.astype(F32)).astype(BF16)

    put(x_ref[...], cls_ref[...].astype(F32), x_out)
    put(qkv_ref[...], new_ref[...], qkv_out)


def place_first(decoder, cls, x, qkv, joint, shift, count):
    rows, width = x.shape[0] // count, x.shape[1]
    block = lambda n: pl.BlockSpec((PACK, n), lambda b, _: (b * rows // PACK, 0))
    return pl.pallas_call(
        place_kernel,
        grid_spec=pltpu.PrefetchScalarGridSpec(
            num_scalar_prefetch=1,
            grid=(count,),
            in_specs=[whole(cls), block(width), block(3 * width), whole(joint), whole(shift)],
            out_specs=[block(width), block(3 * width)],
            scratch_shapes=[pltpu.VMEM((PACK, 3 * width), F32)],
        ),
        out_shape=[jax.ShapeDtypeStruct(x.shape, BF16), jax.ShapeDtypeStruct(qkv.shape, BF16)],
        input_output_aliases={2: 0, 3: 1},
        compiler_params=pltpu.CompilerParams(vmem_limit_bytes=8 * MIB),
        name="place_first",
    )(decoder, cls, x, qkv, joint, shift)


def cls_grad_kernel(*refs, count):
    part_refs, one_refs, (joint_ref, out_ref) = refs[:count], refs[count : 2 * count], refs[2 * count :]
    width = out_ref.shape[1]
    total = packed(one_refs)
    for i in range(3):
        grad = packed([ref.at[i] for ref in part_refs]).astype(BF16)
        total = total + back_mul(grad, joint_ref[:, i * width : (i + 1) * width])
    out_ref[...] = total.astype(BF16)


def cls_back(parts, one, joint, count):
    rows, width = one.shape[0] // count, one.shape[1]
    part = lambda b: pl.BlockSpec((3, PACK, width), lambda *_: (0, b * rows // PACK, 0))
    return pl.pallas_call(
        functools.partial(cls_grad_kernel, count=count),
        grid=(1,),
        in_specs=[part(b) for b in range(count)]
        + [first_block(rows, width, b) for b in range(count)]
        + [whole(joint)],
        out_specs=pl.BlockSpec((PACK, width), lambda *_: (0, 0)),
        out_shape=jax.ShapeDtypeStruct((PACK, width), BF16),
        compiler_params=pltpu.CompilerParams(vmem_limit_bytes=48 * MIB),
        name="cls_back",
    )(*[parts] * count, *[one] * count, joint)


def first_back_kernel(lengths, grad_ref, *refs, count, rows, head_dim, chunk):
    kept = [packed(refs[i * count : (i + 1) * count]) for i in range(5)]
    normed_two, scale_two, slope, normed_one, scale_one = kept
    scale_two, scale_one = scale_two[:, 0:1], scale_one[:, 0:1]
    mixer_ref, expand_ref, contract_ref, gain_ref, qkv_ref, parts_ref = refs[5 * count : 5 * count + 6]
    branch_ref, hidden_ref, mixed_ref, one_ref, sums_ref, shift_sum_ref, out_ref, part_sums_ref = refs[5 * count + 6 :]
    width = grad_ref.shape[1]
    grad = grad_ref[...].astype(F32)
    sums_ref[...] = jnp.zeros_like(sums_ref)

    def add_sum(row, value):
        sums_ref[row : row + 1] = jnp.sum(value, axis=0, keepdims=True)

    add_sum(0, grad * normed_two)
    add_sum(1, grad)
    total = norm_back(grad * gain_ref[1:2], normed_two, scale_two)
    branch = total.astype(BF16)
    branch_ref[...] = branch
    add_sum(2, branch.astype(F32))
    for start in range(0, expand_ref.shape[1], chunk):
        part = slice(start, start + chunk)
        hidden = (back_mul(branch, contract_ref[part, :]) * slope[:, part]).astype(BF16)
        hidden_ref[:, part] = hidden
        shift_sum_ref[0:1, part] = jnp.sum(hidden.astype(F32), axis=0, keepdims=True)
        total = total + back_mul(hidden, expand_ref[:, part])
    add_sum(3, total * normed_one)
    add_sum(4, total)
    total = norm_back(total * gain_ref[0:1], normed_one, scale_one)
    one_ref[...] = total
    mixed = total.astype(BF16)
    mixed_ref[...] = mixed
    add_sum(5, mixed.astype(F32))
    ctx = back_mul(mixed, mixer_ref[...]).astype(BF16).astype(F32)
    for b in range(count):
        span = slice(b * rows, (b + 1) * rows)
        keys, values = qkv_ref[span, width : 2 * width], qkv_ref[span, 2 * width : 3 * width]
        query = qkv_ref[b * rows : b * rows + PACK, 0:width].astype(F32)[0:1] * head_dim**-0.5
        query = per_head(query, head_dim).astype(BF16)
        share = first_share(query, keys, lengths[b])
        ctx_heads = per_head(ctx[b : b + 1], head_dim).astype(BF16)
        share_grad = back_mul(ctx_heads, values)
        inner = jnp.sum(share * share_grad, axis=1, keepdims=True)
        score = (share * (share_grad - inner)).astype(BF16)
        query_grad = heads_joined(matmul(score, keys), head_dim) * head_dim**-0.5
        head_rows = parts_ref[0, b * rows : b * rows + PACK].astype(F32)
        top = lax.broadcasted_iota(jnp.int32, head_rows.shape, 0) == 0
        out_ref[0, span] = parts_ref[0, span]
        out_ref[0, b * rows : b * rows + PACK] = jnp.where(top, head_rows + query_grad, head_rows).astype(BF16)
        out_ref[1, span] = (parts_ref[1, span].astype(F32) + outer_sum(score, query)).astype(BF16)
        out_ref[2, span] = (parts_ref[2, span].astype(F32) + outer_sum(share.astype(BF16), ctx_heads)).astype(BF16)
    part_sums_ref[...] = jnp.zeros_like(part_sums_ref)
    for i in (0, 2):
        part_sums_ref[i : i + 1] = jnp.sum(out_ref[i].astype(F32), axis=0, keepdims=True)


def first_back(grad, kept, mats, gain, qkv, parts, lengths):
    count = lengths.shape[0]
    rows, width = qkv.shape[0] // count, grad.shape[1]
    hidden = mats[1].shape[1]
    blocks = [first_block(rows, array.shape[1], b) for array in kept for b in range(count)]
    rest = mats + (gain, qkv, parts)
    small = lambda n, kind, r=PACK: (pl.BlockSpec((r, n), lambda *_: (0, 0)), jax.ShapeDtypeStruct((r, n), kind))
    outs = [small(width, BF16), small(hidden, BF16), small(width, BF16), small(width, F32), small(width, F32, 8), small(hidden, F32, 1)]
    outs.append((whole(parts), jax.ShapeDtypeStruct(parts.shape, BF16)))
    outs.append(small(width, F32, 8))
    return pl.pallas_call(
        functools.partial(first_back_kernel, count=count, rows=rows, head_dim=width // HEADS, chunk=768),
        grid_spec=pltpu.PrefetchScalarGridSpec(
            num_scalar_prefetch=1,
            grid=(1,),
            in_specs=[whole(grad)] + blocks + [whole(r) for r in rest],
            out_specs=[spec for spec, _ in outs],
        ),
        out_shape=[shape for _, shape in outs],
        compiler_params=pltpu.CompilerParams(vmem_limit_bytes=32 * MIB),
        name="first_back",
    )(lengths, grad, *[array for array in kept for _ in range(count)], *rest)


def project_kernel(x_ref, joint_ref, shift_ref, out_ref):
    out_ref[...] = (matmul(x_ref[...], joint_ref[...]) + shift_ref[...]).astype(BF16)


def project(x, joint, shift):
    rows, width = x.shape
    step = min(256, rows)
    return pl.pallas_call(
        project_kernel,
        grid=(rows // step,),
        in_specs=[pl.BlockSpec((step, width), lambda i: (i, 0)), whole(joint), whole(shift)],
        out_specs=pl.BlockSpec((step, joint.shape[1]), lambda i: (i, 0)),
        out_shape=jax.ShapeDtypeStruct((rows, joint.shape[1]), BF16),
        compiler_params=pltpu.CompilerParams(vmem_limit_bytes=16 * MIB),
        name="project",
    )(x, joint, shift)


def input_grad_kernel(decoder, parts_ref, one_ref, first_ref, joint_ref, out_ref, *, step, rows):
    i = pl.program_id(0)
    width = out_ref.shape[1]

    total = one_ref[...]
    for j in range(3):
        total = total + back_mul(parts_ref[j], joint_ref[:, j * width : (j + 1) * width])
    out_ref[...] = total

    @pl.when(lax.rem(i * step, rows) == 0)
    def _():
        spot = lax.broadcasted_iota(jnp.int32, first_ref.shape, 0)
        row = jnp.sum(jnp.where(spot == i * step // rows, first_ref[...], 0.0), axis=0, keepdims=True)
        head = total[0:8]
        keep = jnp.where(decoder[0] == 1, 0.0, 1.0)
        top = lax.broadcasted_iota(jnp.int32, head.shape, 0) == 0
        out_ref[0:8] = jnp.where(top, (head + row) * keep, head)


def input_gradient(decoder, parts, one, one_first, joint, count):
    total_rows, width = one.shape
    rows = total_rows // count
    step = min(256, rows)
    return pl.pallas_call(
        functools.partial(input_grad_kernel, step=step, rows=rows),
        grid_spec=pltpu.PrefetchScalarGridSpec(
            num_scalar_prefetch=1,
            grid=(total_rows // step,),
            in_specs=[
                pl.BlockSpec((3, step, width), lambda i, _: (0, i, 0)),
                pl.BlockSpec((step, width), lambda i, _: (i, 0)),
                whole(one_first),
                whole(joint),
            ],
            out_specs=pl.BlockSpec((step, width), lambda i, _: (i, 0)),
        ),
        out_shape=jax.ShapeDtypeStruct(one.shape, F32),
        compiler_params=pltpu.CompilerParams(vmem_limit_bytes=48 * MIB),
        name="input_gradient",
    )(decoder, parts, one, one_first, joint)


def weight_grad_kernel(place, left_ref, right_ref, *refs):
    keep_ref, send_ref = refs[-2:]
    own, rows, _ = keep_ref.shape
    total = outer_sum(left_ref[...], right_ref[0]).astype(BF16)
    odd = lax.rem(place[0], 2) == 1
    for i in range(own):
        pair = [total[(2 * i + j) * rows : (2 * i + j + 1) * rows] for j in range(2)]
        keep_ref[i] = jnp.where(odd, pair[1], pair[0])
        send_ref[i] = jnp.where(odd, pair[0], pair[1])


def weight_grads(place, *pairs, tile=768):
    groups = lax.axis_size("dp")
    pairs = [(left, right if right.ndim == 3 else right[None]) for left, right in pairs]
    width = min(right.shape[2] for _, right in pairs)
    sizes = [left.shape[1] // groups for left, _ in pairs]
    heights = [size * right.shape[0] * right.shape[2] // width for size, (_, right) in zip(sizes, pairs)]
    if any(size % 16 for size in sizes):
        blocks = []
        for size, (left, right) in zip(sizes, pairs):
            total = jnp.concatenate([outer_sum(left, r) for r in right], axis=1).astype(BF16)
            total = total.reshape(groups, size, -1, width).transpose(0, 2, 1, 3)
            blocks.append(total.reshape(groups // 2, 2, -1, width))
        blocks = jnp.concatenate(blocks, axis=2)
        odd = lax.rem(place, 2)
        return tuple(lax.dynamic_index_in_dim(blocks, i, 1, False) for i in (odd, 1 - odd))
    shape = jax.ShapeDtypeStruct((groups // 2, sum(heights), width), BF16)
    done = []
    for i, (size, (left, right)) in enumerate(zip(sizes, pairs)):
        rows, height = left.shape
        cuts = right.shape[2] // width
        first = sum(heights[:i]) // size
        spec = pl.BlockSpec((tile // size // 2, size, width), lambda j, i, _, first=first: (i, first + j, 0))
        done = pl.pallas_call(
            weight_grad_kernel,
            grid_spec=pltpu.PrefetchScalarGridSpec(
                num_scalar_prefetch=1,
                grid=(right.shape[0] * cuts, height // tile),
                in_specs=[
                    pl.BlockSpec((rows, tile), lambda j, i, _: (0, i)),
                    pl.BlockSpec((1, rows, width), lambda j, i, _, cuts=cuts: (j // cuts, 0, j % cuts)),
                ]
                + [pl.BlockSpec(memory_space=pl.ANY)] * len(done),
                out_specs=[spec, spec],
            ),
            out_shape=[shape, shape],
            input_output_aliases={3: 0, 4: 1} if done else {},
            compiler_params=pltpu.CompilerParams(vmem_limit_bytes=48 * MIB),
            name="weight_grad",
        )(place.reshape(1), left, right, *done)
    return tuple(done)


def unstacked(total, shapes):
    parts = []
    start = 0
    for rows, columns in shapes:
        height = rows * columns // total.shape[1]
        part = total[start : start + height].reshape(-1, rows, total.shape[1])
        parts.append(part.transpose(1, 0, 2).reshape(rows, columns))
        start += height
    return parts


def add_split_kernel(mine, keep_a, got_a, keep_b, got_b, keep_ref, send_ref):
    keep_ref[...] = (keep_a[...].astype(F32) + got_a[...].astype(F32)).astype(BF16)
    send_ref[...] = (keep_b[...].astype(F32) + got_b[...].astype(F32)).astype(BF16)


def add_split(keep, got, axis, mine):
    rows, width = keep.shape[-2:]
    if rows % 16:
        total = (keep.astype(F32) + got.astype(F32)).astype(BF16)
        return tuple(lax.dynamic_index_in_dim(total, i, axis, False) for i in (mine, 1 - mine))
    rest = keep.shape[:axis] + keep.shape[axis + 1 : -2]
    before = 2**axis
    after = 2 ** (len(rest) - axis)
    shaped = [array.reshape(before, 2, after, rows, width) for array in (keep, got)]
    block = lambda other: pl.BlockSpec(
        (before, None, after, rows, min(width, 768)), lambda j, m: (0, (1 - m[0]) if other else m[0], 0, 0, j)
    )
    out = pl.BlockSpec((before, after, rows, min(width, 768)), lambda j, m: (0, 0, 0, j))
    shape = jax.ShapeDtypeStruct((before, after, rows, width), BF16)
    keep, send = pl.pallas_call(
        add_split_kernel,
        grid_spec=pltpu.PrefetchScalarGridSpec(
            num_scalar_prefetch=1,
            grid=(width // min(width, 768),),
            in_specs=[block(False), block(False), block(True), block(True)],
            out_specs=[out, out],
        ),
        out_shape=[shape, shape],
        compiler_params=pltpu.CompilerParams(vmem_limit_bytes=48 * MIB),
        name="add_split",
    )(mine.reshape(1), *shaped, *shaped)
    return keep.reshape(rest + (rows, width)), send.reshape(rest + (rows, width))


def first_hop(pair):
    keep, send = pair
    axes = tuple(reversed(bits_of(lax.axis_size("dp"))))[:-1]
    shape = (2,) * len(axes) + keep.shape[1:]
    return keep.reshape(shape), swapped(send, 1).reshape(shape), axes


def added(state, bit):
    keep, got, axes = state
    axis = axes.index(bit)
    mine = jnp.where((lax.axis_index("dp") & bit) == 0, 0, 1)
    return (*add_split(keep, got, axis, mine), axes[:axis] + axes[axis + 1 :])


def sent(halves, bit):
    keep, send, axes = halves
    return keep, swapped(send, bit), axes


def rest_of(state, order):
    for bit in order:
        state = sent(added(state, bit), bit)
    return state[0].astype(F32) + state[1].astype(F32)


def as_row(column):
    return jnp.broadcast_to(column, (column.shape[0], LANES)).T[0:1]


def as_column(row):
    return jnp.broadcast_to(row, (LANES, row.shape[1])).T[:, 0:1]


def word_cuts(slice_rows):
    size = 768
    return [
        (i, slice(start, min(start + size, slice_rows)), slice(i * slice_rows + start, i * slice_rows + min(start + size, slice_rows)))
        for i in range(2)
        for start in range(0, slice_rows, size)
    ]


def join(section, mine_ref, other_ref, out_ref):
    @pl.when(pl.program_id(0) == 0)
    def _():
        half = mine_ref.shape[0]
        out_ref[pl.ds(pl.multiple_of(section * half, 16), half)] = mine_ref[...]
        out_ref[pl.ds(pl.multiple_of((1 - section) * half, 16), half)] = other_ref[...]


def word_kernel(section, head_ref, own_ref, mine_ref, other_ref, shift_ref, peak_ref, total_ref, scores_ref, far_ref):
    join(section[0], mine_ref, other_ref, far_ref)
    group, picks, _ = head_ref.shape
    width = own_ref.shape[1]
    rows = group * picks
    head = head_ref[:, :, 0:width].reshape(rows, width)
    peak = jnp.full((rows, 1), -jnp.inf, F32)
    cuts = word_cuts(own_ref.shape[0])
    for table, part, columns in cuts:
        scores = back_mul(head, (own_ref, far_ref)[table][part]) + shift_ref[0:1, columns]
        scores_ref[:, columns] = scores
        peak = jnp.maximum(peak, jnp.max(scores, axis=1, keepdims=True))
    total = jnp.zeros_like(peak)
    for _, _, columns in cuts:
        total = total + jnp.sum(jnp.exp(scores_ref[:, columns] - peak), axis=1, keepdims=True)
    for g in range(group):
        part = slice(g * picks, (g + 1) * picks)
        peak_ref[g] = as_row(peak[part])
        total_ref[g] = as_row(total[part])


def word_scores(section, head, own, mine, other, shift, group=4):
    near, picks, padded = head.shape
    vocab = shift.shape[1]
    row = pl.BlockSpec((group, 1, picks), lambda k, _: (k, 0, 0))
    row_shape = jax.ShapeDtypeStruct((near, 1, picks), F32)
    return pl.pallas_call(
        word_kernel,
        grid_spec=pltpu.PrefetchScalarGridSpec(
            num_scalar_prefetch=1,
            grid=(near // group,),
            in_specs=[pl.BlockSpec((group, picks, padded), lambda k, _: (k, 0, 0))]
            + [whole(array) for array in (own, mine, other, shift)],
            out_specs=[row, row],
            scratch_shapes=[pltpu.VMEM((group * picks, vocab), F32), pltpu.VMEM(own.shape, BF16)],
        ),
        out_shape=[row_shape] * 2,
        compiler_params=pltpu.CompilerParams(vmem_limit_bytes=48 * MIB),
        name="word_scores",
    )(section, head, own, mine, other, shift)


def logit_kernel(place, head_ref, *refs, wholes):
    pairs = len(wholes)
    tables = refs[: sum(1 if w else 2 for w in wholes)]
    shift_ref, logit_ref, *joined = refs[len(tables) :]
    group, picks, _ = head_ref.shape
    width = tables[0].shape[1]
    head = head_ref[:, :, 0:width].reshape(group * picks, width)
    slice_rows = shift_ref.shape[1] // pairs
    for i, is_whole in enumerate(wholes):
        table_ref, *tables = tables
        if not is_whole:
            mine_ref, (other_ref, *tables) = table_ref, tables
            table_ref, *joined = joined
            join(place[1], mine_ref, other_ref, table_ref)
        columns = slice(i * slice_rows, (i + 1) * slice_rows)
        scores = (back_mul(head, table_ref[...]) + shift_ref[0:1, columns]).astype(BF16)
        for g in range(group):
            spot = jnp.bitwise_xor(lax.rem(place[0], group), g)
            logit_ref[spot, :, columns] = scores[g * picks : (g + 1) * picks]


def word_logits(place, head, tables, shift, group=4):
    near, picks, padded = head.shape
    vocab = shift.shape[1]
    slice_rows = vocab // len(tables)
    quarter = near // 2
    wholes = tuple(len(table) == 1 for table in tables)
    arrays = [array for table in tables for array in table]
    spot = lambda k, p: (jnp.bitwise_xor(lax.rem(p[0], quarter) // group, k), 0, 0)
    return pl.pallas_call(
        functools.partial(logit_kernel, wholes=wholes),
        grid_spec=pltpu.PrefetchScalarGridSpec(
            num_scalar_prefetch=1,
            grid=(quarter // group,),
            in_specs=[pl.BlockSpec((group, picks, padded), lambda k, _: (k, 0, 0))]
            + [whole(array) for array in arrays + [shift]],
            out_specs=pl.BlockSpec((group, picks, vocab), spot),
            scratch_shapes=[pltpu.VMEM((slice_rows, arrays[0].shape[1]), BF16)] * (len(tables) - sum(wholes)),
        ),
        out_shape=jax.ShapeDtypeStruct((quarter, picks, vocab), BF16),
        compiler_params=pltpu.CompilerParams(vmem_limit_bytes=48 * MIB),
        name="word_logits",
    )(place, head, *arrays, shift)


def labels_of(head_ref, width):
    label = head_ref[:, :, width:].astype(F32)
    label = label.reshape(-1, label.shape[2])
    return (label[:, 0:1] * 256.0 + label[:, 1:2]).astype(jnp.int32)


def word_back_kernel(first, head_ref, log_ref, own_ref, mine_ref, other_ref, shift_ref, grad_ref, out_ref, hit_ref, far_ref, *, masked):
    join(first[2], mine_ref, other_ref, far_ref)
    group, picks, width = out_ref.shape
    rows = group * picks
    label = labels_of(head_ref, width)
    logs = jnp.concatenate([as_column(log_ref[g]) for g in range(group)])
    head = head_ref[:, :, 0:width].reshape(rows, width)
    total = jnp.zeros((rows, width), F32)
    hit = jnp.zeros((rows, 1), F32)
    for table, part, columns in word_cuts(own_ref.shape[0]):
        words = (own_ref, far_ref)[table][part]
        scores = back_mul(head, words) + shift_ref[0:1, columns]
        share = jnp.exp(scores - logs)
        mine = lax.broadcasted_iota(jnp.int32, share.shape, 1) == label - (first[table] + part.start)
        hit = hit + jnp.sum(jnp.where(mine, scores, 0.0), axis=1, keepdims=True)
        grad = (jnp.where(mine, share - 1.0, share) * (1.0 / masked)).astype(BF16)
        if table == 0:
            grad_ref[:, :, columns] = grad.reshape(group, picks, -1)
        total = total + matmul(grad, words)
    out_ref[...] = total.astype(BF16).reshape(group, picks, width)
    for g in range(group):
        hit_ref[g] = as_row(hit[g * picks : (g + 1) * picks])


def word_back(first, head, logs, own, mine, other, shift, masked, group=4):
    near, picks, padded = head.shape
    width = own.shape[1]
    vocab = shift.shape[1]
    block = lambda n: pl.BlockSpec((group, picks, n), lambda k, _: (k, 0, 0))
    row = pl.BlockSpec((group, 1, picks), lambda k, _: (k, 0, 0))
    return pl.pallas_call(
        functools.partial(word_back_kernel, masked=masked),
        grid_spec=pltpu.PrefetchScalarGridSpec(
            num_scalar_prefetch=1,
            grid=(near // group,),
            in_specs=[block(padded), row] + [whole(array) for array in (own, mine, other, shift)],
            out_specs=[block(vocab // 2), block(width), row],
            scratch_shapes=[pltpu.VMEM(own.shape, BF16)],
        ),
        out_shape=[
            jax.ShapeDtypeStruct((near, picks, vocab // 2), BF16),
            jax.ShapeDtypeStruct((near, picks, width), BF16),
            jax.ShapeDtypeStruct((near, 1, picks), F32),
        ],
        compiler_params=pltpu.CompilerParams(vmem_limit_bytes=48 * MIB),
        name="word_back",
    )(first, head, logs, own, mine, other, shift)


def table_kernel(first, grad_ref, head_ref, other_ref, log_ref, own_ref, shift_ref, out_ref, sums_ref, total_ref, *, masked):
    @pl.when(pl.program_id(0) == 0)
    def _():
        total_ref[...] = jnp.zeros_like(total_ref)
        sums_ref[...] = jnp.zeros_like(sums_ref)

    group, picks, slice_rows = grad_ref.shape
    rows = group * picks
    width = own_ref.shape[1]
    label = labels_of(other_ref, width)
    logs = jnp.concatenate([as_column(log_ref[g]) for g in range(group)])
    head = head_ref[:, :, 0:width].reshape(rows, width)
    other = other_ref[:, :, 0:width].reshape(rows, width)
    for table, part, columns in word_cuts(slice_rows):
        if table == 0:
            share = jnp.exp(back_mul(other, own_ref[part]) + shift_ref[0:1, columns] - logs)
            mine = lax.broadcasted_iota(jnp.int32, share.shape, 1) == label - (first[0] + part.start)
            other_grad = (jnp.where(mine, share - 1.0, share) * (1.0 / masked)).astype(BF16)
            grad = grad_ref[:, :, part].reshape(rows, -1)
            sums_ref[0:1, part] += jnp.sum(grad.astype(F32) + other_grad.astype(F32), axis=0, keepdims=True)
            total_ref[part] += outer_sum(grad, head) + outer_sum(other_grad, other)

    @pl.when(pl.program_id(0) == pl.num_programs(0) - 1)
    def _():
        out_ref[...] = total_ref[...].astype(BF16)


def table_gradient(first, grad, head, other, logs, own, shift, masked, group=4):
    near, picks, slice_rows = grad.shape
    padded, width = head.shape[2], own.shape[1]
    block = lambda n: pl.BlockSpec((group, picks, n), lambda k, _: (k, 0, 0))
    row = pl.BlockSpec((group, 1, picks), lambda k, _: (k, 0, 0))
    return pl.pallas_call(
        functools.partial(table_kernel, masked=masked),
        grid_spec=pltpu.PrefetchScalarGridSpec(
            num_scalar_prefetch=1,
            grid=(near // group,),
            in_specs=[block(slice_rows), block(padded), block(padded), row, whole(own), whole(shift)],
            out_specs=[pl.BlockSpec(own.shape, lambda k, _: (0, 0)), pl.BlockSpec((1, slice_rows), lambda k, _: (0, 0))],
            scratch_shapes=[pltpu.VMEM(own.shape, F32)],
        ),
        out_shape=[jax.ShapeDtypeStruct(own.shape, BF16), jax.ShapeDtypeStruct((1, slice_rows), F32)],
        compiler_params=pltpu.CompilerParams(vmem_limit_bytes=48 * MIB),
        name="table_gradient",
    )(first, grad, head, other, logs, own, shift)


def assemble_kernel(place, near_ref, side_ref, out_ref, *, quarter):
    turn = jnp.bitwise_xor(place[0] // quarter, pl.program_id(0))
    for side, ref in enumerate((near_ref, side_ref)):

        @pl.when(turn % 2 == side)
        def _():
            for i in range(ref.shape[0]):
                out_ref[:, i * ref.shape[2] : (i + 1) * ref.shape[2]] = ref[i]


def assembled(place, nears, sides):
    quarter, picks, vocab = nears.shape
    slice_rows = vocab // 2
    if slice_rows % LANES:
        parts = jnp.stack([array.reshape(quarter, picks, 2, slice_rows) for array in (nears, sides)], axis=3)
        parts = parts.reshape(quarter, picks, 4, slice_rows)
        parts = jnp.take(parts, jnp.bitwise_xor(jnp.arange(4), place // quarter), axis=2)
        return parts.transpose(1, 2, 0, 3).reshape(picks, 2 * quarter * vocab)

    together = 2
    steps = quarter // together

    def spec(side):
        def index(b, j, p):
            turn = jnp.bitwise_xor(p[0] // quarter, b)
            last = jnp.bitwise_xor(p[0] // quarter, jnp.bitwise_xor(b, 1)) // 2
            first_of_pair = lax.rem(b, 2) == 0
            return (
                jnp.where(lax.rem(turn, 2) == side, j, jnp.where(first_of_pair, 0, steps - 1)),
                0,
                jnp.where(lax.rem(turn, 2) == side, turn // 2, last),
            )

        return pl.BlockSpec((together, picks, slice_rows), index)

    return pl.pallas_call(
        functools.partial(assemble_kernel, quarter=quarter),
        grid_spec=pltpu.PrefetchScalarGridSpec(
            num_scalar_prefetch=1,
            grid=(4, steps),
            in_specs=[spec(0), spec(1)],
            out_specs=pl.BlockSpec((picks, together * slice_rows), lambda b, j, _: (0, b * steps + j)),
        ),
        out_shape=jax.ShapeDtypeStruct((picks, 2 * quarter * vocab), BF16),
        compiler_params=pltpu.CompilerParams(vmem_limit_bytes=48 * MIB),
        name="assemble",
    )(place.reshape(1), nears, sides)


def on_device(
    embedded,
    lengths,
    positions,
    labels,
    joint_weight,
    mixer_weight,
    expand_weight,
    contract_weight,
    head_weight,
    gains,
    biases,
    expand_bias,
    word_table,
    word_bias,
):
    section = lax.axis_index("section")
    place = lax.axis_index("dp")
    groups = lax.axis_size("dp")
    decoder = section == 1
    count, rows, width = embedded.shape[1:]
    total_rows = count * rows
    head_dim = width // HEADS
    masked = positions.shape[-1]
    picks = count * masked
    joint = joint_weight[0]
    mats = (mixer_weight[0], expand_weight[0], contract_weight[0])
    head_matrix = head_weight[0]
    gain = gains[0]
    bias = biases[0]
    shift = expand_bias
    slice_rows = word_table.shape[0]

    flag = section.astype(jnp.int32).reshape(1)
    place32 = place.astype(jnp.int32)
    units = shift.shape[1]
    own = width // groups
    near, quarter = groups // 2, groups // 4
    half = slice_rows // 2
    bits = bits_of(groups)
    order = bits[-2:-1] + bits[1:-2] + bits[-1:]
    turned = bits[1:]
    across = lambda array: lax.ppermute(array, "section", [(0, 1), (1, 0)])

    my_half = lax.dynamic_slice_in_dim(word_table, section * half, half)
    far_one, far_two = (swapped(piece, near) for piece in (my_half[: half // 2], my_half[half // 2 :]))
    side_half = swapped(my_half, quarter)

    x = embedded[0].reshape(total_rows, width)
    joint_shift = jnp.concatenate([bias[0], jnp.zeros((width,), F32), bias[1]])[None]
    qkv = project(x, joint, joint_shift)
    cls_out = cls_forward(x, qkv, lengths, mats, gain, bias, shift)
    cls_in = passed_along(cls_out, "section", 1)
    x, qkv = place_first(flag, cls_in, x, qkv, joint, joint_shift, count)
    ctx, logs = attend(qkv, lengths, count)
    ctx, far_one = tied(ctx, far_one)
    far_one_other = across(far_one)
    far_shift = swapped(word_bias, near)
    side_shift = swapped(word_bias, quarter)
    y, normed_one, scale_one, first_low, active, slope, normed_two, scale_two = layer_tail(
        ctx, x, mats, gain, bias, shift
    )
    y, far_one_other, far_two, far_shift, side_shift, side_half = tied(
        y, far_one_other, far_two, far_shift, side_shift, side_half
    )
    far_two_other = across(far_two)
    far_mine = jnp.concatenate([far_one, far_two])
    side_far_shift = swapped(far_shift, quarter)

    chosen = positions[0][:, :, None] == jnp.arange(rows)[None, None, :]
    picked = jnp.einsum(
        "bml,blw->bmw", chosen.astype(BF16), y.reshape(count, rows, width), preferred_element_type=F32
    )
    picked_low = picked.astype(BF16).reshape(picks, width)
    dense = matmul(picked_low, head_matrix) + bias[6]
    dense_active, dense_slope = gelu_and_slope(dense)
    normed_head, scale_head = normalise(dense_active)
    head_low = (normed_head * gain[2] + bias[7]).astype(BF16)
    answers = labels[0].reshape(-1, 1)
    answers = jnp.concatenate([answers // 256, answers % 256, jnp.zeros((picks, LANES - 2), jnp.int32)], axis=1)
    head_low = jnp.concatenate([head_low, answers.astype(BF16)], axis=1)
    head_all, head_low, far_two_other, side_far_shift = tied(
        gather_chips(head_low), head_low, far_two_other, side_far_shift
    )
    head_all = gather_cores(head_all)
    head_other = swapped(head_low, near)
    far_other = jnp.concatenate([far_one_other, far_two_other])
    word_shift = jnp.concatenate([word_bias, far_shift]).astype(F32)[None]
    side_word_shift = jnp.concatenate([side_shift, side_far_shift]).astype(F32)[None]
    where_to = jnp.stack([place32, section.astype(jnp.int32)])
    head_all, side_half = tied(head_all, side_half)
    side_half_other = across(side_half)
    peak, total = word_scores(flag, head_all, word_table, far_mine, far_other, word_shift)
    peak, head_other = tied(peak, head_other)
    grid = (2,) * (len(bits) - 1)
    peak, total = (array.reshape(grid + (picks,)) for array in (peak, total))
    for axis, bit in enumerate(reversed(bits[:-1])):
        other_peak, other_total = jnp.flip(swapped(jnp.stack([peak, total]), bit), axis + 1)
        top = jnp.maximum(peak, other_peak)
        total = total * jnp.exp(peak - top) + other_total * jnp.exp(other_peak - top)
        peak = top
    log_total = (peak + jnp.log(total)).reshape(near, 1, picks)
    log_other = swapped(log_total, near)
    head_other = gather_chips(head_other)
    first = (jnp.stack([place, jnp.bitwise_xor(place, near)]) * slice_rows).astype(jnp.int32)
    first = jnp.concatenate([first, flag])
    score_grad, head_back, hits = word_back(
        first, head_all, log_total, word_table, far_mine, far_other, word_shift, masked
    )
    head_back, side_half_other, head_other, log_other = tied(head_back, side_half_other, head_other, log_other)
    head_other = gather_cores(head_other)
    loss_part = jnp.sum(log_total[0]) - jnp.sum(hits)
    head_grad = scatter_near(head_back)
    table_grad, word_sums = table_gradient(
        first, score_grad, head_all, head_other, log_other, word_table, word_shift, masked
    )
    head_grad, table_grad, word_sums, far_mine = tied(head_grad, table_grad, word_sums, far_mine)
    word_other = across(word_sums)
    side_far_half = swapped(far_mine, quarter)
    exchanged = lambda part: lax.all_to_all(
        part, "dp", 0, 0, axis_index_groups=[list(range(i, i + quarter)) for i in range(0, groups, quarter)]
    )
    logits_near = word_logits(where_to, head_all, ((word_table,), (far_mine, far_other)), word_shift)
    head_grad, logits_near = tied(head_grad, logits_near)
    logits_near = exchanged(logits_near)

    gain_head = jnp.sum(head_grad * normed_head, 0)
    shift_head = jnp.sum(head_grad, 0)
    dense_grad = (norm_back(head_grad * gain[2], normed_head, scale_head) * dense_slope).astype(BF16)
    dense_shift = jnp.sum(dense_grad, axis=0, dtype=F32)
    picked_grad = back_mul(dense_grad, head_matrix).reshape(count, masked, width)
    grad = jnp.einsum(
        "bml,bmw->blw", chosen.astype(F32), picked_grad, precision=lax.Precision.HIGHEST
    ).reshape(total_rows, width)

    kept = (normed_two, scale_two, slope, normed_one, scale_one)
    branch, hidden, one, mixed, ctx_grad, sums, shift_sum = tail_back(grad, kept, mats, gain)
    hidden, branch, side_far_half, word_other = tied(hidden, branch, side_far_half, word_other)
    side_far_other = across(side_far_half)
    one_pair = weight_grads(place32, (active, branch), (ctx, mixed))
    hidden, one_pair = tied(hidden, one_pair)
    one_state = first_hop(one_pair)
    two_pair = weight_grads(place32, (first_low, hidden), (picked_low, dense_grad))
    ctx_grad, two_pair, logits_near = tied(ctx_grad, two_pair, logits_near)
    two_state = first_hop(two_pair)
    one_halves, two_halves = added(one_state, order[0]), added(two_state, turned[0])
    ctx_grad, one_now, two_now = tied(ctx_grad, one_halves[:2], two_halves[:2])
    one_state, two_state = sent((*one_now, one_halves[2]), order[0]), sent((*two_now, two_halves[2]), turned[0])
    parts = attend_back(qkv, ctx_grad, logs, lengths)
    one_halves, two_halves = added(one_state, order[1]), added(two_state, turned[1])
    parts, one_now, two_now, side_far_other = tied(parts, one_halves[:2], two_halves[:2], side_far_other)
    logits_side = word_logits(
        where_to, head_all, ((side_half, side_half_other), (side_far_half, side_far_other)), side_word_shift
    )
    one_state, two_state = sent((*one_now, one_halves[2]), order[1]), sent((*two_now, two_halves[2]), turned[1])
    logits_side = exchanged(logits_side)
    cls_grad = passed_along(cls_back(parts, one, joint, count), "section", -1)
    cls_grad, table_grad = tied(cls_grad, table_grad)
    table_other = across(table_grad)

    branch_f, hidden_f, mixed_f, one_f, sums_f, shift_f, parts, part_sums = first_back(
        cls_grad, kept, mats, gain, qkv, parts, lengths
    )
    two_halves = added(two_state, turned[2])
    parts, two_now = tied(parts, two_halves[:2])
    two_state = sent((*two_now, two_halves[2]), turned[2])

    def firsts(array):
        return jnp.concatenate([array[b * rows : b * rows + 1] for b in range(count)])

    mine = jnp.concatenate(
        [firsts(active), firsts(first_low), firsts(ctx), branch_f[:count], hidden_f[:count], mixed_f[:count]],
        axis=1,
    )
    sums = sums + sums_f
    small = jnp.concatenate(
        [
            jnp.stack([sums[3], sums[0], gain_head]),
            jnp.stack(
                [part_sums[0], part_sums[2], sums[5], sums[4], sums[2], sums[1], dense_shift, shift_head]
            ),
            (shift_sum + shift_f).reshape(-1, width),
            jnp.broadcast_to(loss_part, (1, width)),
        ]
    )
    small_high = lax.reduce_precision(small, 8, 7)
    small_low = (small - small_high).astype(BF16)
    small_high = small_high.astype(BF16)
    mine = mine.reshape(-1, width)
    counts = [mine.shape[0], small.shape[0], small.shape[0]]
    gathered = jnp.concatenate([mine, small_high, small_low])[None]
    arriving = swapped(gathered, near)
    joint_pair = weight_grads(place32, (x, parts))
    parts, joint_pair, arriving, logits_side = tied(parts, joint_pair, arriving, logits_side)
    joint_state = first_hop(joint_pair)
    gathered = side_by_side(gathered, arriving, near)
    arriving = swapped(gathered, quarter)
    joint_halves = added(joint_state, order[0])
    parts, joint_now, arriving = tied(parts, joint_halves[:2], arriving)
    joint_state = sent((*joint_now, joint_halves[2]), order[0])
    bit = quarter
    for below in reversed(bits[:-2]):
        gathered = side_by_side(gathered, arriving, bit)
        arriving = swapped(gathered, below)
        bit = below
        if bit == 2:
            input_grad = input_gradient(flag, parts, one, one_f, joint, count)
            input_grad, logits_near, logits_side = tied(input_grad, logits_near, logits_side)
            logits_out = assembled(place32, logits_near, logits_side)
            logits_out, arriving = tied(logits_out, arriving)
    logits_out, one_got = tied(logits_out, one_state[1])
    one_halves = added((one_state[0], one_got, one_state[2]), order[2])
    logits_out, one_now = tied(logits_out, one_halves[:2])
    one_state = sent((*one_now, one_halves[2]), order[2])
    joint_keep, joint_got, logits_out, input_grad, two_got = tied(
        *joint_state[:2], logits_out, input_grad, two_state[1]
    )
    two_state = two_state[0], two_got, two_state[2]
    joint_state = sent(added((joint_keep, joint_got, joint_state[2]), order[1]), order[1])
    expand_sum, head_sum = unstacked(rest_of(two_state, turned[3:]), [(own, units), (own, width)])
    joint_keep, joint_got, expand_sum, head_sum = tied(*joint_state[:2], expand_sum, head_sum)
    joint_keep, joint_send, axes = added((joint_keep, joint_got, joint_state[2]), order[2])
    joint_got = swapped(joint_send, order[2])
    joint_keep, arriving, one_got = tied(joint_keep, arriving, one_state[1])
    one_state = one_state[0], one_got, one_state[2]
    contract_sum, mixer_sum = unstacked(rest_of(one_state, order[3:]), [(units // groups, width), (own, width)])
    joint_got, table_other = tied(joint_got, table_other)
    joint_sum = unstacked(rest_of((joint_keep, joint_got, axes), order[3:]), [(own, 3 * width)])[0]
    table_total = table_grad.astype(F32) + table_other.astype(F32)
    rows_all = side_by_side(gathered, arriving, 1)
    small = jnp.sum(rows_all[:, counts[0] :].astype(F32), axis=0)
    small = small[: counts[1]] + small[counts[1] :]
    rows_all = rows_all[:, : counts[0]].reshape(groups * count, -1)
    word_total = word_sums[0] + word_other[0]
    cuts = [units, width, width, width, units, width]
    starts = [sum(cuts[:i]) for i in range(len(cuts))]
    active_a, first_a, ctx_a, branch_a, hidden_a, mixed_a = (
        rows_all[:, s : s + n] for s, n in zip(starts, cuts)
    )

    def own_columns(array):
        size = array.shape[1] // groups
        return lax.dynamic_slice_in_dim(array, place * size, size, 1)

    contract_sum = contract_sum + outer_sum(own_columns(active_a), branch_a)
    expand_sum = expand_sum + outer_sum(own_columns(first_a), hidden_a)
    mixer_sum = mixer_sum + outer_sum(own_columns(ctx_a), mixed_a)

    loss = (small[-1, 0] / (picks * groups)).reshape(1)
    return (
        loss,
        logits_out.reshape(1, count, masked, -1),
        input_grad.reshape(1, count, rows, width),
        joint_sum[None],
        mixer_sum[None],
        expand_sum[None],
        contract_sum[None],
        head_sum[None],
        small[None, :3],
        small[None, 3:11],
        small[11:-1].reshape(1, -1),
        table_total,
        word_total,
    )


def solution(mesh):
    in_specs = (
        P("section", "dp", None, None),
        P("dp"),
        P("section", "dp", None),
        P("section", "dp", None),
        P("section", None, None),
        P("section", None, None),
        P("section", None, None),
        P("section", None, None),
        P("section", None, None),
        P("section", None, None),
        P("section", None, None),
        P("section", None),
        P("dp", None),
        P("dp"),
    )
    out_specs = (
        P("section"),
        P("section", "dp", None, None),
        P("section", "dp", None, None),
        P("section", "dp", None),
        P("section", "dp", None),
        P("section", "dp", None),
        P("section", "dp", None),
        P("section", "dp", None),
        P("section", None, None),
        P("section", None, None),
        P("section", None),
        P("dp", None),
        P("dp"),
    )
    return jax.shard_map(
        on_device, mesh=mesh, in_specs=in_specs, out_specs=out_specs, check_vma=False
    )
```
